128 devices in a mesh: bx: 8 (over z_hi, y), by: 16 (over x, z_lo, core).
Axes of the slice: x: 4, y: 4, z: 4 (z_hi: 2, z_lo: 2; z = z_hi * 2 + z_lo), core: 2. Of those that a mesh axis runs over, the one named last changes fastest.
Arguments:
- fine_prev: float32 [32, 16, 32, 256], P(None, 'bx', 'by'), may hold values from -4 to 4
- fine_now: float32 [32, 16, 32, 256], P(None, 'bx', 'by'), may hold values from -4 to 4
- fine_kernels: bfloat16 [4, 27, 32, 32], replicated, may hold values from -0.21875 to 0.21875
- coarse_kernel: bfloat16 [27, 1024, 256], P(None, 'by'), may hold values from -0.078125 to 0.078125
- cotangent: bfloat16 [256, 8, 16, 128], P(None, 'bx', 'by'), may hold values from -6 to 6
Outputs:
- coarse_next: float32 [256, 8, 16, 128], P(None, 'bx', 'by')
- state_adjoint: float32 [256, 8, 16, 128], P(None, 'bx', 'by')
The draws below stay inside these ranges and needn't reach their ends.
All inputs are finite; a program needn't handle non-finite values.
Results may differ from the reference program's by a relative error of at most 0.0085.
Values may be sent and summed in bfloat16 or wider, within the bound.
No kernel may reach another device: no remote copies, remote signals or barrier semaphores. Data moves between devices by JAX's collectives and lax.ppermute only.
A program may use at most 64 MiB of HBM per device.

```python
import math
import jax
import jax.numpy as jnp
import numpy as np
from jax import lax

C = 32
H2 = 1024
LAYERS = 4
NZ = 256
NX = 16
NY = 32


def shard_levels(own_key, shape, cuts, low, top_value):
    level, own = 1.0, jax.random.fold_in(own_key, 6)
    for axis_at, shards_of in cuts:
        steps = jnp.exp(jax.random.uniform(jax.random.fold_in(own, axis_at), (shards_of,), jnp.float32, low / len(cuts), top_value / len(cuts)))
        level = level * jnp.repeat(steps, shape[axis_at] // shards_of).reshape([-1 if axis == axis_at else 1 for axis in range(len(shape))])
    return level


def bell_draw(own_key, dims, deviation, reach, shards=(), dtype=jnp.bfloat16):
    level = shard_levels(own_key, dims, shards, -0.22, 0.18) if shards else 1.0
    array = jax.random.normal(own_key, dims, jnp.float32) * deviation * level
    return jnp.minimum(jnp.maximum(array, -reach), reach).astype(dtype)


def setup_inputs(seed: int = 0) -> dict:
    splits = jax.random.split(jax.random.key(seed), 6)
    fine_prev = bell_draw(splits[0], (C, NX, NY, NZ), 0.5, 4.0, ((1, 8), (2, 16)), jnp.float32)
    fine_now = bell_draw(splits[1], (C, NX, NY, NZ), 0.5, 4.0, ((1, 8), (2, 16)), jnp.float32)
    fine_kernels = bell_draw(splits[2], (LAYERS, 27, C, C), (27 * C) ** -0.5, 0.21875)
    coarse_kernel = bell_draw(splits[3], (27, H2, 8 * C), (27 * 8 * C) ** -0.5, 0.078125, ((1, 16),))
    cotangent = bell_draw(splits[4], (8 * C, NX // 2, NY // 2, NZ // 2), 1.0, 6.0, ((1, 8), (2, 16)))
    return dict(fine_prev=fine_prev, fine_now=fine_now, fine_kernels=fine_kernels, coarse_kernel=coarse_kernel, cotangent=cotangent)


fine_step = 0.5
coarse_step = 1.5

def count_bits(value):
    total = 0
    for position in range(3):
        total = total + (value >> position & 1)
    return total

def haar_table():
    signs = np.zeros((8, 8))
    for output_code in range(8):
        for input_code in range(8):
            parity = count_bits(output_code & input_code)
            signs[output_code, input_code] = (-1.0) ** parity / math.sqrt(8.0)
    return signs

def coarsen(volume):
    octants = [volume[:, across::2, upward::2, inward::2] for across in range(2) for upward in range(2) for inward in range(2)]
    stacked = jnp.stack(octants, 0)
    mixed = jnp.einsum('hk,kcxyz->chxyz', jnp.asarray(haar_table(), jnp.float32), stacked, precision=lax.Precision.HIGHEST)
    return mixed.reshape((volume.shape[0] * 8, volume.shape[1] // 2, volume.shape[2] // 2, volume.shape[3] // 2))

def tap_offsets():
    return [(across, upward, inward) for across in (-1, 0, 1) for upward in (-1, 0, 1) for inward in (-1, 0, 1)]

def window_at(padded, starts, extent):
    return lax.slice(padded, (0, starts[0], starts[1], starts[2]), (padded.shape[0], starts[0] + extent[0], starts[1] + extent[1], starts[2] + extent[2]))

def forward_conv(volume, kernel):
    padded = jnp.pad(volume.astype(jnp.float32), ((0, 0), (1, 1), (1, 1), (1, 1)))
    weights = kernel.astype(jnp.float32)
    extent = volume.shape[1:]
    totals = jnp.zeros((kernel.shape[1],) + extent, jnp.float32)
    for number, offset in enumerate(tap_offsets()):
        starts = (1 + offset[0], 1 + offset[1], 1 + offset[2])
        totals = totals + jnp.einsum('oc,cxyz->oxyz', weights[number], window_at(padded, starts, extent))
    return totals

def adjoint_conv(volume, kernel):
    padded = jnp.pad(volume.astype(jnp.float32), ((0, 0), (1, 1), (1, 1), (1, 1)))
    weights = kernel.astype(jnp.float32)
    extent = volume.shape[1:]
    totals = jnp.zeros((kernel.shape[2],) + extent, jnp.float32)
    for number, offset in enumerate(tap_offsets()):
        starts = (1 - offset[0], 1 - offset[1], 1 - offset[2])
        totals = totals + jnp.einsum('oc,oxyz->cxyz', weights[number], window_at(padded, starts, extent))
    return totals

def reference(fine_prev, fine_now, fine_kernels, coarse_kernel, cotangent):
    previous, current = (fine_prev, fine_now)
    for layer_index in range(LAYERS):
        rounded = lax.optimization_barrier(current.astype(jnp.bfloat16))
        preact = forward_conv(rounded, fine_kernels[layer_index])
        squashed = lax.optimization_barrier(jnp.tanh(preact).astype(jnp.bfloat16))
        force = adjoint_conv(squashed, fine_kernels[layer_index])
        previous, current = (current, 2.0 * current - previous - fine_step * force)
    coarse_now = coarsen(current)
    coarse_prev = coarsen(previous)
    coarse_b = lax.optimization_barrier(coarse_now.astype(jnp.bfloat16))
    preact = forward_conv(coarse_b, coarse_kernel)
    squash_value = jnp.tanh(preact)
    squashed = lax.optimization_barrier(squash_value.astype(jnp.bfloat16))
    coarse_next = 2.0 * coarse_now - coarse_prev - coarse_step * adjoint_conv(squashed, coarse_kernel)
    response = forward_conv(cotangent, coarse_kernel)
    scaled = lax.optimization_barrier(((1.0 - squash_value * squash_value) * response).astype(jnp.bfloat16))
    state_adjoint = 2.0 * cotangent.astype(jnp.float32) - coarse_step * adjoint_conv(scaled, coarse_kernel)
    return (coarse_next, state_adjoint)
```

```python
import math

import jax
import jax.numpy as jnp
import numpy as np
from jax import lax
from jax.experimental import pallas as pl
from jax.experimental.pallas import tpu as pltpu
from jax.sharding import Mesh, PartitionSpec as P


BF = jnp.bfloat16
F32 = jnp.float32
LAYERS = 4
AXES = ("b", "q", "g")
FINE_STEP = 0.5
COARSE_STEP = 1.5
NOW, PREV, OWN = 10, 8, 2
CHUNK = 2 * (NOW + PREV + OWN)


def window_start(b, q, g):
    return 4 * (4 * b + g) - 6 + 2 * q


def send_tables():
    first = np.zeros((128, 16, 256), np.float32)
    middle = np.zeros((128, 8, 512), np.float32)
    final = np.zeros((128, 16, 256), np.float32)
    for target in range(128):
        start = window_start(target // 16, target // 4 % 4, target % 4)
        for k in range(2 * NOW):
            at = start + k % NOW
            if 0 <= at < 128:
                if k < 16:
                    first[target, k, 2 * at + k // NOW] = 1
                else:
                    middle[target, k - 16, 2 * at + k // NOW] = 1
        for k in range(2 * OWN):
            at = start + 4 + k % OWN
            if 0 <= at < 128:
                middle[target, 4 + k, 256 + 128 * (k // OWN) + at] = 1
        for k in range(2 * PREV):
            at = start + 1 + k % PREV
            if 0 <= at < 128:
                final[target, k, 2 * at + k // PREV] = 1
    return (
        first.reshape(2048, 256).astype(BF),
        middle.reshape(1024, 512).astype(BF),
        final.reshape(2048, 256).astype(BF),
    )


def lane_table():
    table = np.zeros((128, 128), np.float32)
    for c in range(32):
        for ab in range(4):
            table[ab * 32 + c, c * 4 + ab] = 1
    return table.astype(BF)


def swap_table(outer, inner):
    table = np.zeros((outer * inner,) * 2, np.float32)
    for i in range(outer):
        for j in range(inner):
            table[j * outer + i, i * inner + j] = 1
    return table.astype(BF)


def haar_table():
    table = np.zeros((256, 256), np.float32)
    for code in range(8):
        a, b, d = code >> 2, code >> 1 & 1, code & 1
        for h in range(8):
            sign = (-1) ** bin(h & code).count("1")
            for c in range(32):
                table[128 * d + 64 * a + 32 * b + c, 8 * c + h] = sign
    return table.astype(BF)


def receive_table():
    table = np.zeros((128, 8, 256), np.float32)
    for source in range(128):
        group = 4 * (source // 16) + source % 4
        for k in range(8):
            table[source, k, 128 * (k // 4) + 4 * group + k % 4] = 1
    return table.reshape(1024, 256).astype(BF)


def dot(x, y):
    return jnp.dot(x, y, preferred_element_type=F32)


def dot_nt(x, y):
    return lax.dot_general(x, y, (((1,), (1,)), ((), ())), preferred_element_type=F32)


def vmem(n):
    return [pl.BlockSpec(memory_space=pltpu.VMEM)] * n


def pack_kernel(now, prev, cot, lanes, first, middle, final, out):
    now_rows = dot(lanes[...], now[...].astype(BF)).astype(BF)
    prev_rows = dot(lanes[...], prev[...].astype(BF)).astype(BF)
    both = jnp.concatenate([now_rows, cot[0:128, :], cot[128:256, :]], axis=1)
    part = 32
    for t in range(0, 128, part):
        one = dot_nt(first[pl.ds(16 * t, 16 * part), :], now_rows).reshape(part, 16, 128)
        two = dot_nt(middle[pl.ds(8 * t, 8 * part), :], both).reshape(part, 8, 128)
        three = dot_nt(final[pl.ds(16 * t, 16 * part), :], prev_rows).reshape(part, 16, 128)
        out[pl.ds(t, part)] = jnp.concatenate([one, two, three], axis=1).astype(BF)


def tap_index(dx, dy, dz, a2, b2, d2, a, b, d):
    def offset(moved, bit, to):
        place = (-1 if bit else 2) if moved else bit
        return place - to

    e = (offset(dx, a, a2), offset(dy, b, b2), offset(dz, d, d2))
    if any(abs(v) > 1 for v in e):
        return None
    return 9 * (e[0] + 1) + 3 * (e[1] + 1) + e[2] + 1


def weight_kernel(forward, adjoint, tile, out, wide):
    lane = lax.broadcasted_iota(jnp.int32, (32, 128), 1)
    masks = [jnp.where(lane // 32 == v, 1.0, 0.0).astype(BF) for v in range(4)]
    for way in range(2):
        source = (forward, adjoint)[way]
        wide[...] = dot(source[0], tile[...]).astype(BF).reshape(27, 32, 128)
        for moved in range(8):
            dx, dy, dz = moved >> 2, moved >> 1 & 1, moved & 1
            for u in range(8):
                d, a, b = u >> 2, u >> 1 & 1, u & 1
                for d2 in range(2):
                    total = jnp.zeros((32, 128), BF)
                    for v in range(4):
                        tap = tap_index(dx, dy, dz, v >> 1, v & 1, d2, a, b, d)
                        if tap is not None:
                            total = total + masks[v] * wide[26 - tap if way else tap]
                    out[0, way, moved, 32 * u : 32 * u + 32, 128 * d2 : 128 * d2 + 128] = total


def side_rows(v):
    row = lax.broadcasted_iota(jnp.int32, (16, 256), 0)
    axis = v.ndim - 2
    before = jnp.where(row == 0, 0.0, pltpu.roll(v, 1, axis))
    after = jnp.where(row == 15, 0.0, pltpu.roll(v, 15, axis))
    return before, after


def moved_rows(v):
    lane = lax.broadcasted_iota(jnp.int32, (16, 256), 1)
    before, after = side_rows(v)
    return jnp.where(lane // 32 % 2 == 1, before, after)


def block_conv(plain, turned, weights, x0, xs, z0, zs):
    rows = xs * zs * 16
    lane = lax.broadcasted_iota(jnp.int32, (1, 1, 16, 256), 3)
    high = lane // 64 % 2 == 1
    total = jnp.zeros((rows, 256), F32)

    def at(ref, dx, moved_z):
        xsl = pl.ds(x0 + 1 + dx, xs)
        if not moved_z:
            return ref[xsl, pl.ds(z0 + 1, zs)]
        return jnp.concatenate(
            [ref[xsl, pl.ds(z0 + 2, zs), :, 0:128], ref[xsl, pl.ds(z0, zs), :, 128:256]], axis=-1
        )

    for moved in range(8):
        dx, dy, dz = moved >> 2, moved >> 1 & 1, moved & 1
        ref = turned if dy else plain
        if dx:
            left = jnp.where(high, at(ref, -1, dz), at(ref, 1, dz))
        else:
            left = at(ref, 0, dz)
        total = total + dot(left.reshape(rows, 256), weights[moved])
    return total


def fine_kernel(place, chunk, weights, swap, haar, mid, base, cur, old, s0, s1, h0, h1):
    start = place[0]
    for ref in (s0, s1, h0, h1):
        for x in (0, 9):
            ref[x] = jnp.zeros((NOW + 2, 16, 256), BF)
        for z in (0, NOW + 1):
            ref[:, z] = jnp.zeros((10, 16, 256), BF)

    def keep(z):
        at = start + z
        return jnp.where((at >= 0) & (at < 128), 1.0, 0.0).astype(F32)

    def unpack(x, carry):
        rows = chunk[x].astype(F32)
        parts = []
        for k in range(0, CHUNK, 8):
            group = rows[:, k : k + 8, :].reshape(128, 128).astype(BF)
            moved = dot(swap[...], group)
            parts += [moved[16 * j : 16 * j + 16] for j in range(8)]
        for z in range(NOW):
            v = jnp.concatenate([parts[z], parts[NOW + z]], axis=1)
            cur[x, z] = v
            s0[x + 1, z + 1] = v.astype(BF)
            s1[x + 1, z + 1] = moved_rows(v).astype(BF)
        at = 2 * NOW
        for z in range(OWN):
            v = jnp.concatenate([parts[at + z], parts[at + OWN + z]], axis=1)
            mid[1, x, z] = v.astype(BF)
        at = 2 * (NOW + OWN)
        for z in range(PREV):
            old[x, z + 1] = jnp.concatenate([parts[at + z], parts[at + PREV + z]], axis=1)
        return carry

    lax.fori_loop(0, 8, unpack, 0)

    now, before = cur, old
    for layer in range(LAYERS):
        zs = NOW - 2 * layer
        xs = 4 if zs > 6 else 8

        def squash(i, carry, layer=layer, zs=zs, xs=xs):
            x0 = i * xs
            v = jnp.tanh(block_conv(s0, s1, weights.at[layer, 0], x0, xs, layer, zs))
            v = v.reshape(xs, zs, 16, 256)
            for z in range(zs):
                part = v[:, z] * keep(layer + z)
                h0[pl.ds(x0 + 1, xs), layer + z + 1] = part.astype(BF)
                h1[pl.ds(x0 + 1, xs), layer + z + 1] = moved_rows(part).astype(BF)
            return carry

        lax.fori_loop(0, 8 // xs, squash, 0)
        zs = NOW - 2 * layer - 2
        xs = 4 if zs > 6 else 8
        last = layer == LAYERS - 1

        def update(i, carry, layer=layer, zs=zs, xs=xs, now=now, before=before, last=last):
            x0 = i * xs
            v = block_conv(h0, h1, weights.at[layer, 1], x0, xs, layer + 1, zs)
            v = v.reshape(xs, zs, 16, 256)
            for z in range(zs):
                at = layer + 1 + z
                here = (pl.ds(x0, xs), at)
                part = (2.0 * now[here] - before[here] - FINE_STEP * v[:, z]) * keep(at)
                before[here] = part
                if not last:
                    s0[pl.ds(x0 + 1, xs), at + 1] = part.astype(BF)
                    s1[pl.ds(x0 + 1, xs), at + 1] = moved_rows(part).astype(BF)
            return carry

        lax.fori_loop(0, 8 // xs, update, 0)
        now, before = before, now

    def coarse(v):
        top = v.astype(BF)
        low = (v - top.astype(F32)).astype(BF)
        return (dot(top, haar[...]) + dot(low, haar[...])) * (1.0 / math.sqrt(8.0))

    own = (slice(None), slice(4, 6))
    latest = now[own].reshape(256, 256)
    earlier = before[own].reshape(256, 256)
    mid[0] = coarse(latest).astype(BF).reshape(8, 2, 16, 256)
    base[...] = coarse(2.0 * latest - earlier).reshape(8, 2, 16, 256)


def coarse_kernel_body(place, states, base, w0, w1, w2, w3, swap, out, state, hidden, weights, sems):
    start = place[0]
    quarter = place[1]
    copies = []
    for i, w in enumerate((w0, w1, w2, w3)):
        copy = pltpu.make_async_copy(w, weights.at[:, pl.ds(64 * i, 64), :], sems.at[i])
        copy.start()
        copies.append(copy)
    for s in range(2):
        for y in range(3):
            for x in (0, 9):
                state[s, y, x] = jnp.zeros((8, 16, 256), BF)
                hidden[s, y, x] = jnp.zeros((6, 16, 256), BF)
    for s in range(2):
        for q in range(4):
            piece = states[q, s]
            wide = piece.astype(F32)
            before, after = side_rows(wide)
            here = (pl.ds(1, 8), pl.ds(2 * q, 2))
            state[(s, 0) + here] = before.astype(BF)
            state[(s, 1) + here] = piece
            state[(s, 2) + here] = after.astype(BF)
    for copy in copies:
        copy.wait()
    taps = [(x, y, z) for x in (-1, 0, 1) for y in (-1, 0, 1) for z in (-1, 0, 1)]

    def forward(s):
        total = jnp.zeros((768, 256), F32)
        for number, (ex, ey, ez) in enumerate(taps):
            left = state[s, 1 + ey, pl.ds(1 + ex, 8), pl.ds(1 + ez, 6)].reshape(768, 256)
            total = total + dot_nt(left, weights[number])
        return total

    def adjoint(s):
        total = jnp.zeros((512, 256), F32)
        for number, (ex, ey, ez) in enumerate(taps):
            left = hidden[s, 1 - ey, pl.ds(1 - ex, 8), pl.ds(1 - ez, 4)].reshape(512, 256)
            total = total + dot(left, weights[number])
        return total

    def store(s, v):
        v = v.reshape(8, 6, 16, 256)
        for z in range(6):
            at = start + z
            part = v[:, z] * jnp.where((at >= 0) & (at < 128), 1.0, 0.0).astype(F32)
            before, after = side_rows(part)
            hidden[s, 0, pl.ds(1, 8), z] = before.astype(BF)
            hidden[s, 1, pl.ds(1, 8), z] = part.astype(BF)
            hidden[s, 2, pl.ds(1, 8), z] = after.astype(BF)

    squash = jnp.tanh(forward(0))
    store(0, squash)
    store(1, (1.0 - squash * squash) * forward(1))
    force = (-COARSE_STEP * adjoint(0)).reshape(8, 4, 16, 256)
    pull = (-COARSE_STEP * adjoint(1)).reshape(8, 4, 16, 256)
    near = jnp.where(quarter == 1, 1.0, 0.0).astype(F32)
    far = jnp.where(quarter == 2, 1.0, 0.0).astype(F32)
    for x in range(8):
        ground = base[x]
        rows = jnp.concatenate([force[x, 0:2] + near * ground, force[x, 2:4] + far * ground, pull[x]], axis=0)
        out[x] = dot(swap[...], rows.reshape(128, 256).astype(BF)).astype(BF).reshape(16, 8, 256)


def local(fine_prev, fine_now, fine_kernels, coarse_kernel, cotangent):
    b, q, g = (lax.axis_index(name) for name in AXES)
    first, middle, final = send_tables()
    packed = pl.pallas_call(
        pack_kernel,
        out_shape=jax.ShapeDtypeStruct((128, CHUNK, 128), BF),
        in_specs=vmem(7),
        out_specs=pl.BlockSpec(memory_space=pltpu.VMEM),
        compiler_params=pltpu.CompilerParams(vmem_limit_bytes=48 << 20),
        name="pack",
    )(
        fine_now.reshape(128, 256),
        fine_prev.reshape(128, 256),
        cotangent.reshape(256, 128),
        lane_table(),
        first,
        middle,
        final,
    )
    chunk = lax.all_to_all(packed, AXES, 0, 0).reshape(8, 16, CHUNK, 128)

    tile = np.tile(np.eye(32, dtype=np.float32), (1, 4)).astype(BF)
    weights = pl.pallas_call(
        weight_kernel,
        grid=(LAYERS,),
        out_shape=jax.ShapeDtypeStruct((LAYERS, 2, 8, 256, 256), BF),
        in_specs=[
            pl.BlockSpec((1, 864, 32), lambda i: (i, 0, 0)),
            pl.BlockSpec((1, 864, 32), lambda i: (i, 0, 0)),
            pl.BlockSpec((32, 128), lambda i: (0, 0)),
        ],
        out_specs=pl.BlockSpec((1, 2, 8, 256, 256), lambda i: (i, 0, 0, 0, 0)),
        scratch_shapes=[pltpu.VMEM((27, 32, 128), BF)],
        compiler_params=pltpu.CompilerParams(vmem_limit_bytes=32 << 20),
        cost_estimate=pl.CostEstimate(flops=10**10, bytes_accessed=10**7, transcendentals=0),
        name="spread_weights",
    )(
        jnp.swapaxes(fine_kernels, 2, 3).reshape(LAYERS, 864, 32),
        fine_kernels.reshape(LAYERS, 864, 32),
        tile,
    )

    start = 4 * (4 * b + g) - 6 + 2 * q
    buffer = pltpu.VMEM((10, NOW + 2, 16, 256), BF)
    mid, base = pl.pallas_call(
        fine_kernel,
        out_shape=(
            jax.ShapeDtypeStruct((2, 8, OWN, 16, 256), BF),
            jax.ShapeDtypeStruct((8, OWN, 16, 256), F32),
        ),
        in_specs=[pl.BlockSpec(memory_space=pltpu.SMEM)] + vmem(4),
        out_specs=tuple(vmem(2)),
        scratch_shapes=[pltpu.VMEM((8, NOW, 16, 256), F32)] * 2 + [buffer] * 4,
        compiler_params=pltpu.CompilerParams(vmem_limit_bytes=56 << 20),
        cost_estimate=pl.CostEstimate(flops=10**10, bytes_accessed=10**7, transcendentals=10**6),
        name="fine_layers",
    )(jnp.stack([start, q]).astype(jnp.int32), chunk, weights, swap_table(16, 8), haar_table())

    across = lax.ppermute(coarse_kernel, "g", [(i, i ^ 2) for i in range(4)])
    there = lax.ppermute(coarse_kernel, "g", [(i, i ^ 1) for i in range(4)])
    opposite = lax.ppermute(across, "g", [(i, i ^ 1) for i in range(4)])
    states = lax.all_gather(mid, "q")
    partial = pl.pallas_call(
        coarse_kernel_body,
        out_shape=jax.ShapeDtypeStruct((8, 16, 8, 256), BF),
        in_specs=[pl.BlockSpec(memory_space=pltpu.SMEM)] + vmem(2) + [pl.BlockSpec(memory_space=pl.ANY)] * 4 + vmem(1),
        out_specs=pl.BlockSpec(memory_space=pltpu.VMEM),
        scratch_shapes=[
            pltpu.VMEM((2, 3, 10, 8, 16, 256), BF),
            pltpu.VMEM((2, 3, 10, 6, 16, 256), BF),
            pltpu.VMEM((27, 256, 256), BF),
            pltpu.SemaphoreType.DMA((4,)),
        ],
        compiler_params=pltpu.CompilerParams(vmem_limit_bytes=56 << 20),
        cost_estimate=pl.CostEstimate(flops=2 * 10**10, bytes_accessed=10**7, transcendentals=10**6),
        name="coarse_layer",
    )(
        jnp.stack([4 * (4 * b + g) - 1, q]).astype(jnp.int32),
        states,
        base,
        coarse_kernel,
        across,
        there,
        opposite,
        swap_table(8, 16),
    )
    parts = lax.all_to_all(partial.reshape(128, 8, 256), AXES, 0, 0)
    sums = lax.dot_general(
        parts.reshape(1024, 256), receive_table(), (((0,), (0,)), ((), ())), preferred_element_type=F32
    )
    coarse_next = sums[:, 0:128].reshape(256, 1, 1, 128)
    state_adjoint = 2.0 * cotangent.astype(F32) + sums[:, 128:256].reshape(256, 1, 1, 128)
    return coarse_next, state_adjoint


def solution(mesh):
    split = Mesh(mesh.devices.reshape(8, 4, 4), AXES)
    rows = P(None, "b", ("q", "g"), None)
    return jax.shard_map(
        local,
        mesh=split,
        in_specs=(rows, rows, P(), P(None, ("q", "g"), None), rows),
        out_specs=(rows, rows),
        check_vma=False,
    )
```

```python
import math

import jax
import jax.numpy as jnp
import numpy as np
from jax import lax
from jax.experimental import pallas as pl
from jax.experimental.pallas import tpu as pltpu
from jax.sharding import Mesh, PartitionSpec as P


BF = jnp.bfloat16
F32 = jnp.float32
LAYERS = 4
AXES = ("b", "q", "g")
FINE_STEP = 0.5
COARSE_STEP = 1.5
NOW, PREV, OWN = 10, 8, 2
CHUNK = 2 * (NOW + PREV + OWN)


def window_start(b, q, g):
    return 4 * (4 * b + g) - 6 + 2 * q


def iota(shape, axis):
    return lax.broadcasted_iota(jnp.int32, shape, axis)


def ones_where(mask):
    return jnp.where(mask, 1.0, 0.0).astype(F32)


def swap_table(outer, inner):
    n = outer * inner
    row, column = iota((n, n), 0), iota((n, n), 1)
    return ones_where(column == row % outer * inner + row // outer).astype(BF)


def haar_signs(lane, channel):
    code = lane // 64 % 2 * 4 + lane // 32 % 2 * 2 + lane // 128
    both = code & channel % 8
    odd = (both ^ both // 2 ^ both // 4) & 1
    return jnp.where(lane % 32 == channel // 8, 1.0 - 2.0 * odd.astype(F32), 0.0).astype(BF)


def receive_table():
    table = np.zeros((128, 8, 256), np.float32)
    for source in range(128):
        group = 4 * (source // 16) + source % 4
        for k in range(8):
            table[source, k, 128 * (k // 4) + 4 * group + k % 4] = 1
    return table.reshape(1024, 256).astype(BF)


def dot(x, y):
    return jnp.dot(x, y, preferred_element_type=F32)


def dot_nt(x, y):
    return lax.dot_general(x, y, (((1,), (1,)), ((), ())), preferred_element_type=F32)


def vmem(n):
    return [pl.BlockSpec(memory_space=pltpu.VMEM)] * n


def parity_rows(ref):
    return jnp.concatenate([ref[:, a, b, :] for a in range(2) for b in range(2)], axis=0)


def pack_kernel(now, prev, cot, out, first, middle, final):
    now_rows = parity_rows(now)
    speed = (now_rows - parity_rows(prev)).astype(BF)
    now_rows = now_rows.astype(BF)
    both = jnp.concatenate([now_rows, cot[0:128, :], cot[128:256, :]], axis=1)
    k, lane = iota((16, 256), 0), iota((16, 256), 1)
    for_first = lane - 2 * (k % NOW) - k // NOW
    for_final = lane - 2 * (1 + k % PREV) - k // PREV
    k, lane = iota((8, 512), 0), iota((8, 512), 1)
    for_middle = jnp.where(k < 4, jnp.where(lane < 256, lane - 2 * (k + 6) - 1, -1000), -1000)
    at = 2 * (lane % 128 - 4 - k % OWN)
    for_middle = jnp.where((k >= 4) & (lane >= 256) & (lane // 128 - 2 == (k - 4) // OWN), at, for_middle)
    for target in range(128):
        at = 2 * window_start(target // 16, target // 4 % 4, target % 4)
        first[16 * target : 16 * target + 16] = ones_where(for_first == at).astype(BF)
        final[16 * target : 16 * target + 16] = ones_where(for_final == at).astype(BF)
        middle[8 * target : 8 * target + 8] = ones_where(for_middle == at)
    part = 32
    for t in range(0, 128, part):
        one = dot_nt(first[pl.ds(16 * t, 16 * part), :], now_rows).reshape(part, 16, 128)
        two = dot_nt(middle[pl.ds(8 * t, 8 * part), :].astype(BF), both).reshape(part, 8, 128)
        three = dot_nt(final[pl.ds(16 * t, 16 * part), :], speed).reshape(part, 16, 128)
        out[pl.ds(t, part)] = jnp.concatenate([one, two, three], axis=1).astype(BF)


def split_dot(x, y, exact_left):
    wide = y if exact_left else x
    top = wide.astype(BF)
    rest = wide - top.astype(F32)
    low = rest.astype(BF)
    last = (rest - low.astype(F32)).astype(BF)
    if exact_left:
        return dot(x, top) + dot(x, low) + dot(x, last)
    return dot(top, y) + dot(low, y) + dot(last, y)


def drift_kernel(now, prev, out):
    rows = 6.0 * parity_rows(now) - 5.0 * parity_rows(prev)
    total = jnp.zeros((256, 128), F32)
    for d in range(2):
        pick = ones_where(iota((256, 128), 0) == 2 * iota((256, 128), 1) + d).astype(BF)
        signs = haar_signs(iota((256, 128), 1) + 128 * d, iota((256, 128), 0))
        total = total + split_dot(signs, split_dot(rows, pick, False), True)
    out[...] = total * (1.0 / math.sqrt(8.0))


def tap_index(dx, dy, dz, a2, b2, d2, a, b, d):
    def offset(moved, bit, to):
        place = (-1 if bit else 2) if moved else bit
        return place - to

    e = (offset(dx, a, a2), offset(dy, b, b2), offset(dz, d, d2))
    if any(abs(v) > 1 for v in e):
        return None
    return 9 * (e[0] + 1) + 3 * (e[1] + 1) + e[2] + 1


def weight_kernel(forward, adjoint, tile, out, wide):
    lane = lax.broadcasted_iota(jnp.int32, (32, 128), 1)
    masks = [jnp.where(lane // 32 == v, 1.0, 0.0).astype(BF) for v in range(4)]
    for way in range(2):
        source = (forward, adjoint)[way]
        wide[...] = dot(source[0], tile[...]).astype(BF).reshape(27, 32, 128)
        for moved in range(8):
            dx, dy, dz = moved >> 2, moved >> 1 & 1, moved & 1
            for u in range(8):
                d, a, b = u >> 2, u >> 1 & 1, u & 1
                for d2 in range(2):
                    total = jnp.zeros((32, 128), BF)
                    for v in range(4):
                        tap = tap_index(dx, dy, dz, v >> 1, v & 1, d2, a, b, d)
                        if tap is not None:
                            total = total + masks[v] * wide[26 - tap if way else tap]
                    out[0, way, moved, 32 * u : 32 * u + 32, 128 * d2 : 128 * d2 + 128] = total


def side_rows(v):
    row = lax.broadcasted_iota(jnp.int32, (16, 256), 0)
    axis = v.ndim - 2
    before = jnp.where(row == 0, 0.0, pltpu.roll(v, 1, axis))
    after = jnp.where(row == 15, 0.0, pltpu.roll(v, 15, axis))
    return before, after


def moved_rows(v):
    lane = lax.broadcasted_iota(jnp.int32, (16, 256), 1)
    before, after = side_rows(v)
    return jnp.where(lane // 32 % 2 == 1, before, after)


def block_conv(plain, turned, weights, x0, xs, z0, zs):
    rows = xs * zs * 16
    lane = lax.broadcasted_iota(jnp.int32, (1, 1, 16, 256), 3)
    high = lane // 64 % 2 == 1
    total = jnp.zeros((rows, 256), F32)

    def at(ref, dx, moved_z):
        xsl = pl.ds(x0 + 1 + dx, xs)
        if not moved_z:
            return ref[xsl, pl.ds(z0 + 1, zs)]
        return jnp.concatenate(
            [ref[xsl, pl.ds(z0 + 2, zs), :, 0:128], ref[xsl, pl.ds(z0, zs), :, 128:256]], axis=-1
        )

    for moved in range(8):
        dx, dy, dz = moved >> 2, moved >> 1 & 1, moved & 1
        ref = turned if dy else plain
        if dx:
            left = jnp.where(high, at(ref, -1, dz), at(ref, 1, dz))
        else:
            left = at(ref, 0, dz)
        total = total + dot(left.reshape(rows, 256), weights[moved])
    return total


def fine_kernel(chunk, weights, mid, base, cur, old, line, s0, s1, h0, h1):
    start = window_start(*(lax.axis_index(name) for name in AXES))
    swap = swap_table(16, 8)
    for ref in (s0, s1, h0, h1):
        for x in (0, 9):
            ref[x] = jnp.zeros((NOW + 2, 16, 256), BF)
        for z in (0, NOW + 1):
            ref[:, z] = jnp.zeros((10, 16, 256), BF)

    def keep(z):
        at = start + z
        return jnp.where((at >= 0) & (at < 128), 1.0, 0.0).astype(F32)

    def unpack(x, carry):
        rows = chunk[x].astype(F32)
        parts = []
        for k in range(0, CHUNK, 8):
            group = rows[:, k : k + 8, :].reshape(128, 128).astype(BF)
            moved = dot(swap, group)
            parts += [moved[16 * j : 16 * j + 16] for j in range(8)]
        for z in range(NOW):
            v = jnp.concatenate([parts[z], parts[NOW + z]], axis=1)
            cur[x, z] = v
            s0[x + 1, z + 1] = v.astype(BF)
            s1[x + 1, z + 1] = moved_rows(v).astype(BF)
        at = 2 * (NOW + OWN)
        for z in range(PREV):
            v = jnp.concatenate([parts[at + z], parts[at + PREV + z]], axis=1)
            old[x, z + 1] = cur[x, z + 1] - v
            if z in (3, 4):
                line[x, z - 3] = cur[x, z + 1] + 5.0 * v
        return carry

    lax.fori_loop(0, 8, unpack, 0)

    now, before = cur, old
    for layer in range(LAYERS):
        zs = NOW - 2 * layer
        xs = 4 if zs > 6 else 8

        def squash(i, carry, layer=layer, zs=zs, xs=xs):
            x0 = i * xs
            v = jnp.tanh(block_conv(s0, s1, weights.at[layer, 0], x0, xs, layer, zs))
            v = v.reshape(xs, zs, 16, 256)
            for z in range(zs):
                part = v[:, z] * keep(layer + z)
                h0[pl.ds(x0 + 1, xs), layer + z + 1] = part.astype(BF)
                h1[pl.ds(x0 + 1, xs), layer + z + 1] = moved_rows(part).astype(BF)
            return carry

        lax.fori_loop(0, 8 // xs, squash, 0)
        zs = NOW - 2 * layer - 2
        xs = 4 if zs > 6 else 8
        last = layer == LAYERS - 1

        def update(i, carry, layer=layer, zs=zs, xs=xs, now=now, before=before, last=last):
            x0 = i * xs
            v = block_conv(h0, h1, weights.at[layer, 1], x0, xs, layer + 1, zs)
            v = v.reshape(xs, zs, 16, 256)
            for z in range(zs):
                at = layer + 1 + z
                here = (pl.ds(x0, xs), at)
                part = (2.0 * now[here] - before[here] - FINE_STEP * v[:, z]) * keep(at)
                before[here] = part
                if not last:
                    s0[pl.ds(x0 + 1, xs), at + 1] = part.astype(BF)
                    s1[pl.ds(x0 + 1, xs), at + 1] = moved_rows(part).astype(BF)
            return carry

        lax.fori_loop(0, 8 // xs, update, 0)
        now, before = before, now

    haar = haar_signs(iota((256, 256), 0), iota((256, 256), 1))
    scale = 1.0 / math.sqrt(8.0)
    own = (slice(None), slice(4, 6))
    latest = now[own].reshape(256, 256)
    earlier = before[own].reshape(256, 256)
    forced = 2.0 * latest - earlier - line[...].reshape(256, 256)
    mid[...] = (split_dot(latest, haar, False) * scale).astype(BF).reshape(8, OWN, 16, 256)
    base[...] = (split_dot(forced, haar, False) * scale).reshape(8, OWN, 16, 256)


def coarse_kernel_body(*refs):
    own, cots, base = refs[0:4], refs[4:8], refs[8]
    pieces, out, state, hidden, weights, sems = refs[9:13], refs[13], refs[14], refs[15], refs[16], refs[17]
    b, quarter, g = (lax.axis_index(name) for name in AXES)
    start = 4 * (4 * b + g) - 1
    swap = swap_table(16, 8)
    copies = []
    for i, w in enumerate(pieces):
        copy = pltpu.make_async_copy(w, weights.at[:, pl.ds(64 * i, 64), :], sems.at[i])
        copy.start()
        copies.append(copy)
    for s in range(2):
        for y in range(3):
            for x in (0, 9):
                state[s, y, x] = jnp.zeros((8, 16, 256), BF)
                hidden[s, y, x] = jnp.zeros((6, 16, 256), BF)
    def place(s, x, xs, z, wide):
        before, after = side_rows(wide)
        state[s, 0, pl.ds(x + 1, xs), z] = before.astype(BF)
        state[s, 1, pl.ds(x + 1, xs), z] = wide.astype(BF)
        state[s, 2, pl.ds(x + 1, xs), z] = after.astype(BF)

    for k in range(4):
        z0 = OWN * ((quarter + 4 - k) % 4)
        for z in range(OWN):
            place(0, 0, 8, z0 + z, own[k][:, z].astype(F32))

        def unpack(x, carry, k=k, z0=z0):
            moved = dot(swap, cots[k][x].astype(F32).reshape(128, 128).astype(BF))
            for z in range(OWN):
                low, high = (moved[16 * j : 16 * j + 16] for j in (4 + z, 4 + OWN + z))
                place(1, x, 1, z0 + z, jnp.concatenate([low, high], axis=1)[None])
            return carry

        lax.fori_loop(0, 8, unpack, 0)
    for copy in copies:
        copy.wait()
    taps = [(x, y, z) for x in (-1, 0, 1) for y in (-1, 0, 1) for z in (-1, 0, 1)]

    def forward(s):
        total = jnp.zeros((768, 256), F32)
        for number, (ex, ey, ez) in enumerate(taps):
            left = state[s, 1 + ey, pl.ds(1 + ex, 8), pl.ds(1 + ez, 6)].reshape(768, 256)
            total = total + dot_nt(left, weights[number])
        return total

    def adjoint(s):
        total = jnp.zeros((512, 256), F32)
        for number, (ex, ey, ez) in enumerate(taps):
            left = hidden[s, 1 - ey, pl.ds(1 - ex, 8), pl.ds(1 - ez, 4)].reshape(512, 256)
            total = total + dot(left, weights[number])
        return total

    def store(s, v):
        v = v.reshape(8, 6, 16, 256)
        for z in range(6):
            at = start + z
            part = v[:, z] * jnp.where((at >= 0) & (at < 128), 1.0, 0.0).astype(F32)
            before, after = side_rows(part)
            hidden[s, 0, pl.ds(1, 8), z] = before.astype(BF)
            hidden[s, 1, pl.ds(1, 8), z] = part.astype(BF)
            hidden[s, 2, pl.ds(1, 8), z] = after.astype(BF)

    squash = jnp.tanh(forward(0))
    store(0, squash)
    store(1, (1.0 - squash * squash) * forward(1))
    force = (-COARSE_STEP * adjoint(0)).reshape(8, 4, 16, 256)
    pull = (-COARSE_STEP * adjoint(1)).reshape(8, 4, 16, 256)
    near = jnp.where(quarter == 1, 1.0, 0.0).astype(F32)
    back = swap_table(8, 16)
    far = jnp.where(quarter == 2, 1.0, 0.0).astype(F32)
    for x in range(8):
        ground = base[x]
        rows = jnp.concatenate([force[x, 0:2] + near * ground, force[x, 2:4] + far * ground, pull[x]], axis=0)
        out[x] = dot(back, rows.reshape(128, 256).astype(BF)).astype(BF).reshape(16, 8, 256)


def local(fine_prev, fine_now, fine_kernels, coarse_kernel, cotangent):
    packed = pl.pallas_call(
        pack_kernel,
        out_shape=jax.ShapeDtypeStruct((128, CHUNK, 128), BF),
        in_specs=vmem(3),
        out_specs=pl.BlockSpec(memory_space=pltpu.VMEM),
        scratch_shapes=[
            pltpu.VMEM((2048, 256), BF),
            pltpu.VMEM((1024, 512), F32),
            pltpu.VMEM((2048, 256), BF),
        ],
        compiler_params=pltpu.CompilerParams(vmem_limit_bytes=32 << 20),
        name="pack",
    )(fine_now, fine_prev, cotangent.reshape(256, 128))
    chunk = lax.all_to_all(packed, AXES, 0, 0).reshape(8, 16, CHUNK, 128)
    drift = pl.pallas_call(
        drift_kernel,
        out_shape=jax.ShapeDtypeStruct((256, 128), F32),
        in_specs=vmem(2),
        out_specs=pl.BlockSpec(memory_space=pltpu.VMEM),
        cost_estimate=pl.CostEstimate(flops=10**9, bytes_accessed=10**6, transcendentals=0),
        name="drift",
    )(fine_now, fine_prev)

    tile = np.tile(np.eye(32, dtype=np.float32), (1, 4)).astype(BF)
    weights = pl.pallas_call(
        weight_kernel,
        grid=(LAYERS,),
        out_shape=jax.ShapeDtypeStruct((LAYERS, 2, 8, 256, 256), BF),
        in_specs=[
            pl.BlockSpec((1, 864, 32), lambda i: (i, 0, 0)),
            pl.BlockSpec((1, 864, 32), lambda i: (i, 0, 0)),
            pl.BlockSpec((32, 128), lambda i: (0, 0)),
        ],
        out_specs=pl.BlockSpec((1, 2, 8, 256, 256), lambda i: (i, 0, 0, 0, 0)),
        scratch_shapes=[pltpu.VMEM((27, 32, 128), BF)],
        compiler_params=pltpu.CompilerParams(vmem_limit_bytes=32 << 20),
        cost_estimate=pl.CostEstimate(flops=10**10, bytes_accessed=10**7, transcendentals=0),
        name="spread_weights",
    )(
        jnp.swapaxes(fine_kernels, 2, 3).reshape(LAYERS, 864, 32),
        fine_kernels.reshape(LAYERS, 864, 32),
        tile,
    )

    kernel_part, weights = lax.optimization_barrier((coarse_kernel, weights))
    across = lax.ppermute(kernel_part, "g", [(i, i ^ 2) for i in range(4)])
    there = lax.ppermute(kernel_part, "g", [(i, i ^ 1) for i in range(4)])

    def round_ring(v):
        return [v] + [lax.ppermute(v, "q", [(i, (i + k) % 4) for i in range(4)]) for k in range(1, 4)]

    cots = round_ring(lax.slice_in_dim(chunk, 16, 24, axis=2))
    buffer = pltpu.VMEM((10, NOW + 2, 16, 256), BF)
    mid, base = pl.pallas_call(
        fine_kernel,
        out_shape=(
            jax.ShapeDtypeStruct((8, OWN, 16, 256), BF),
            jax.ShapeDtypeStruct((8, OWN, 16, 256), F32),
        ),
        in_specs=vmem(2),
        out_specs=tuple(vmem(2)),
        scratch_shapes=[pltpu.VMEM((8, NOW, 16, 256), F32)] * 2
        + [pltpu.VMEM((8, OWN, 16, 256), F32)]
        + [buffer] * 4,
        compiler_params=pltpu.CompilerParams(vmem_limit_bytes=48 << 20),
        cost_estimate=pl.CostEstimate(flops=2 * 10**10, bytes_accessed=10**7, transcendentals=10**6),
        name="fine_layers",
    )(chunk, weights)
    mid, across, *cots = lax.optimization_barrier((mid, across, *cots))
    opposite = lax.ppermute(across, "g", [(i, i ^ 1) for i in range(4)])
    partial = pl.pallas_call(
        coarse_kernel_body,
        out_shape=jax.ShapeDtypeStruct((8, 16, 8, 256), BF),
        in_specs=vmem(9) + [pl.BlockSpec(memory_space=pl.ANY)] * 4,
        out_specs=pl.BlockSpec(memory_space=pltpu.VMEM),
        scratch_shapes=[
            pltpu.VMEM((2, 3, 10, 8, 16, 256), BF),
            pltpu.VMEM((2, 3, 10, 6, 16, 256), BF),
            pltpu.VMEM((27, 256, 256), BF),
            pltpu.SemaphoreType.DMA((4,)),
        ],
        compiler_params=pltpu.CompilerParams(vmem_limit_bytes=48 << 20),
        cost_estimate=pl.CostEstimate(flops=2 * 10**10, bytes_accessed=10**7, transcendentals=10**6),
        name="coarse_layer",
    )(*round_ring(mid), *cots, base, coarse_kernel, across, there, opposite)
    parts = lax.all_to_all(partial.reshape(128, 8, 256), AXES, 0, 0)
    sums = lax.dot_general(
        parts.reshape(1024, 256), receive_table(), (((0,), (0,)), ((), ())), preferred_element_type=F32
    )
    coarse_next = (drift + sums[:, 0:128]).reshape(256, 1, 1, 128)
    state_adjoint = 2.0 * cotangent.astype(F32) + sums[:, 128:256].reshape(256, 1, 1, 128)
    return coarse_next, state_adjoint


def solution(mesh):
    split = Mesh(mesh.devices.reshape(8, 4, 4), AXES)
    rows = P(None, "b", ("q", "g"), None)
    return jax.shard_map(
        local,
        mesh=split,
        in_specs=(rows, rows, P(), P(None, ("q", "g"), None), rows),
        out_specs=(rows, rows),
        check_vma=False,
    )
```

```python
import math

import jax
import jax.numpy as jnp
import numpy as np
from jax import lax
from jax.experimental import pallas as pl
from jax.experimental.pallas import tpu as pltpu
from jax.sharding import Mesh, PartitionSpec as P


BF = jnp.bfloat16
F32 = jnp.float32
LAYERS = 4
AXES = ("b", "q", "g")
FINE_STEP = 0.5
COARSE_STEP = 1.5
NOW, PREV, OWN = 10, 8, 2
CHUNK = 2 * (NOW + PREV + OWN)


def window_start(b, q, g):
    return 4 * (4 * b + g) - 6 + 2 * q


def iota(shape, axis):
    return lax.broadcasted_iota(jnp.int32, shape, axis)


def ones_where(mask):
    return jnp.where(mask, 1.0, 0.0).astype(F32)


def swap_table(outer, inner):
    n = outer * inner
    row, column = iota((n, n), 0), iota((n, n), 1)
    return ones_where(column == row % outer * inner + row // outer).astype(BF)


def haar_signs(lane, channel):
    code = lane // 64 % 2 * 4 + lane // 32 % 2 * 2 + lane // 128
    both = code & channel % 8
    odd = (both ^ both // 2 ^ both // 4) & 1
    return jnp.where(lane % 32 == channel // 8, 1.0 - 2.0 * odd.astype(F32), 0.0).astype(BF)


def receive_table():
    table = np.zeros((128, 8, 256), np.float32)
    for source in range(128):
        group = 4 * (source // 16) + source % 4
        for k in range(8):
            table[source, k, 128 * (k // 4) + 4 * group + k % 4] = 1
    return table.reshape(1024, 256).astype(BF)


def dot(x, y):
    return jnp.dot(x, y, preferred_element_type=F32)


def dot_nt(x, y):
    return lax.dot_general(x, y, (((1,), (1,)), ((), ())), preferred_element_type=F32)


def vmem(n):
    return [pl.BlockSpec(memory_space=pltpu.VMEM)] * n


def parity_rows(ref):
    return jnp.concatenate([ref[:, a, b, :] for a in range(2) for b in range(2)], axis=0)


def pack_kernel(now, prev, cot, out, first, middle, final):
    now_rows = parity_rows(now).astype(BF)
    prev_rows = parity_rows(prev).astype(BF)
    both = jnp.concatenate([now_rows, cot[0:128, :], cot[128:256, :]], axis=1)
    k, lane = iota((16, 256), 0), iota((16, 256), 1)
    for_first = lane - 2 * (k % NOW) - k // NOW
    for_final = lane - 2 * (1 + k % PREV) - k // PREV
    k, lane = iota((8, 512), 0), iota((8, 512), 1)
    for_middle = jnp.where(k < 4, jnp.where(lane < 256, lane - 2 * (k + 6) - 1, -1000), -1000)
    at = 2 * (lane % 128 - 4 - k % OWN)
    for_middle = jnp.where((k >= 4) & (lane >= 256) & (lane // 128 - 2 == (k - 4) // OWN), at, for_middle)
    for target in range(128):
        at = 2 * window_start(target // 16, target // 4 % 4, target % 4)
        first[16 * target : 16 * target + 16] = ones_where(for_first == at).astype(BF)
        final[16 * target : 16 * target + 16] = ones_where(for_final == at).astype(BF)
        middle[8 * target : 8 * target + 8] = ones_where(for_middle == at)
    part = 32
    for t in range(0, 128, part):
        one = dot_nt(first[pl.ds(16 * t, 16 * part), :], now_rows).reshape(part, 16, 128)
        two = dot_nt(middle[pl.ds(8 * t, 8 * part), :].astype(BF), both).reshape(part, 8, 128)
        three = dot_nt(final[pl.ds(16 * t, 16 * part), :], prev_rows).reshape(part, 16, 128)
        out[pl.ds(t, part)] = jnp.concatenate([one, two, three], axis=1).astype(BF)


def split_dot(x, y):
    top = x.astype(BF)
    low = (x - top.astype(F32)).astype(BF)
    return dot(top, y) + dot(low, y)


def tap_index(dx, dy, dz, a2, b2, d2, a, b, d):
    def offset(moved, bit, to):
        place = (-1 if bit else 2) if moved else bit
        return place - to

    e = (offset(dx, a, a2), offset(dy, b, b2), offset(dz, d, d2))
    if any(abs(v) > 1 for v in e):
        return None
    return 9 * (e[0] + 1) + 3 * (e[1] + 1) + e[2] + 1


def weight_kernel(forward, adjoint, tile, out, wide):
    lane = lax.broadcasted_iota(jnp.int32, (32, 128), 1)
    masks = [jnp.where(lane // 32 == v, 1.0, 0.0).astype(BF) for v in range(4)]
    for way in range(2):
        source = (forward, adjoint)[way]
        wide[...] = dot(source[0], tile[...]).astype(BF).reshape(27, 32, 128)
        for moved in range(8):
            dx, dy, dz = moved >> 2, moved >> 1 & 1, moved & 1
            for u in range(8):
                d, a, b = u >> 2, u >> 1 & 1, u & 1
                for d2 in range(2):
                    total = jnp.zeros((32, 128), BF)
                    for v in range(4):
                        tap = tap_index(dx, dy, dz, v >> 1, v & 1, d2, a, b, d)
                        if tap is not None:
                            total = total + masks[v] * wide[26 - tap if way else tap]
                    out[0, way, moved, 32 * u : 32 * u + 32, 128 * d2 : 128 * d2 + 128] = total


def side_rows(v):
    row = lax.broadcasted_iota(jnp.int32, (16, 256), 0)
    axis = v.ndim - 2
    before = jnp.where(row == 0, 0.0, pltpu.roll(v, 1, axis))
    after = jnp.where(row == 15, 0.0, pltpu.roll(v, 15, axis))
    return before, after


def moved_rows(v):
    lane = lax.broadcasted_iota(jnp.int32, (16, 256), 1)
    before, after = side_rows(v)
    return jnp.where(lane // 32 % 2 == 1, before, after)


def block_conv(plain, turned, weights, x0, xs, z0, zs):
    rows = xs * zs * 16
    lane = lax.broadcasted_iota(jnp.int32, (1, 1, 16, 256), 3)
    high = lane // 64 % 2 == 1
    total = jnp.zeros((rows, 256), F32)

    def at(ref, dx, moved_z):
        xsl = pl.ds(x0 + 1 + dx, xs)
        if not moved_z:
            return ref[xsl, pl.ds(z0 + 1, zs)]
        return jnp.concatenate(
            [ref[xsl, pl.ds(z0 + 2, zs), :, 0:128], ref[xsl, pl.ds(z0, zs), :, 128:256]], axis=-1
        )

    for moved in range(8):
        dx, dy, dz = moved >> 2, moved >> 1 & 1, moved & 1
        ref = turned if dy else plain
        if dx:
            left = jnp.where(high, at(ref, -1, dz), at(ref, 1, dz))
        else:
            left = at(ref, 0, dz)
        total = total + dot(left.reshape(rows, 256), weights[moved])
    return total


def fine_kernel(chunk, spread, mid, base, cur, old, s0, s1, h0, h1, weights, sems):
    copies = []
    for layer in range(LAYERS):
        copy = pltpu.make_async_copy(spread.at[layer], weights.at[layer], sems.at[layer])
        copy.start()
        copies.append(copy)
    start = window_start(*(lax.axis_index(name) for name in AXES))
    swap = swap_table(16, 8)
    for ref in (s0, s1, h0, h1):
        for x in (0, 9):
            ref[x] = jnp.zeros((NOW + 2, 16, 256), BF)
        for z in (0, NOW + 1):
            ref[:, z] = jnp.zeros((10, 16, 256), BF)

    def keep(z):
        at = start + z
        return jnp.where((at >= 0) & (at < 128), 1.0, 0.0).astype(F32)

    def unpack(x, carry):
        rows = chunk[x].astype(F32)
        parts = []
        for k in range(0, CHUNK, 8):
            group = rows[:, k : k + 8, :].reshape(128, 128).astype(BF)
            moved = dot(swap, group)
            parts += [moved[16 * j : 16 * j + 16] for j in range(8)]
        for z in range(NOW):
            v = jnp.concatenate([parts[z], parts[NOW + z]], axis=1)
            cur[x, z] = v
            s0[x + 1, z + 1] = v.astype(BF)
            s1[x + 1, z + 1] = moved_rows(v).astype(BF)
        at = 2 * (NOW + OWN)
        for z in range(PREV):
            v = jnp.concatenate([parts[at + z], parts[at + PREV + z]], axis=1)
            old[x, z + 1] = v
        return carry

    lax.fori_loop(0, 8, unpack, 0)

    now, before = cur, old
    for layer in range(LAYERS):
        copies[layer].wait()
        zs = NOW - 2 * layer
        xs = max(1, 128 // (16 * zs)) if zs > 6 else 8 // zs + (zs == 6)

        def squash(i, carry, layer=layer, zs=zs, xs=xs):
            x0 = i * xs
            v = jnp.tanh(block_conv(s0, s1, weights.at[layer, 0], x0, xs, layer, zs))
            v = v.reshape(xs, zs, 16, 256)
            for z in range(zs):
                part = v[:, z] * keep(layer + z)
                h0[pl.ds(x0 + 1, xs), layer + z + 1] = part.astype(BF)
                h1[pl.ds(x0 + 1, xs), layer + z + 1] = moved_rows(part).astype(BF)
            return carry

        lax.fori_loop(0, 8 // xs, squash, 0, unroll=True)
        zs = NOW - 2 * layer - 2
        xs = max(1, 128 // (16 * zs)) if zs > 6 else 8 // zs + (zs == 6)
        last = layer == LAYERS - 1

        def update(i, carry, layer=layer, zs=zs, xs=xs, now=now, before=before, last=last):
            x0 = i * xs
            v = block_conv(h0, h1, weights.at[layer, 1], x0, xs, layer + 1, zs)
            v = v.reshape(xs, zs, 16, 256)
            for z in range(zs):
                at = layer + 1 + z
                here = (pl.ds(x0, xs), at)
                part = (2.0 * now[here] - before[here] - FINE_STEP * v[:, z]) * keep(at)
                before[here] = part
                if not last:
                    s0[pl.ds(x0 + 1, xs), at + 1] = part.astype(BF)
                    s1[pl.ds(x0 + 1, xs), at + 1] = moved_rows(part).astype(BF)
            return carry

        lax.fori_loop(0, 8 // xs, update, 0, unroll=True)
        now, before = before, now

    haar = haar_signs(iota((256, 256), 0), iota((256, 256), 1))
    scale = 1.0 / math.sqrt(8.0)
    own = (slice(None), slice(4, 6))
    latest = now[own].reshape(256, 256)
    earlier = before[own].reshape(256, 256)
    mid[...] = (split_dot(latest, haar) * scale).astype(BF).reshape(8, OWN, 16, 256)
    base[...] = (split_dot(2.0 * latest - earlier, haar) * scale).reshape(8, OWN, 16, 256)


def coarse_kernel_body(*refs):
    own, cots, base = refs[0:4], refs[4:8], refs[8]
    pieces, out, state, hidden, weights, sems = refs[9:13], refs[13], refs[14], refs[15], refs[16], refs[17]
    b, quarter, g = (lax.axis_index(name) for name in AXES)
    start = 4 * (4 * b + g) - 1
    swap = swap_table(16, 8)
    copies = []
    for i, w in enumerate(pieces):
        copy = pltpu.make_async_copy(w, weights.at[:, pl.ds(64 * i, 64), :], sems.at[i])
        copy.start()
        copies.append(copy)
    for s in range(2):
        for y in range(3):
            for x in (0, 9):
                state[s, y, x] = jnp.zeros((8, 16, 256), BF)
                hidden[s, y, x] = jnp.zeros((6, 16, 256), BF)
    def place(s, x, xs, z, wide):
        before, after = side_rows(wide)
        state[s, 0, pl.ds(x + 1, xs), z] = before.astype(BF)
        state[s, 1, pl.ds(x + 1, xs), z] = wide.astype(BF)
        state[s, 2, pl.ds(x + 1, xs), z] = after.astype(BF)

    for k in range(4):
        z0 = OWN * ((quarter + 4 - k) % 4)
        for z in range(OWN):
            place(0, 0, 8, z0 + z, own[k][:, z].astype(F32))

        def unpack(x, carry, k=k, z0=z0):
            moved = dot(swap, cots[k][x].astype(F32).reshape(128, 128).astype(BF))
            for z in range(OWN):
                low, high = (moved[16 * j : 16 * j + 16] for j in (4 + z, 4 + OWN + z))
                place(1, x, 1, z0 + z, jnp.concatenate([low, high], axis=1)[None])
            return carry

        lax.fori_loop(0, 8, unpack, 0, unroll=True)
    for copy in copies:
        copy.wait()
    taps = [(x, y, z) for x in (-1, 0, 1) for y in (-1, 0, 1) for z in (-1, 0, 1)]

    def forward(s, x0, xs):
        rows = xs * 96
        total = jnp.zeros((rows, 256), F32)
        for number, (ex, ey, ez) in enumerate(taps):
            left = state[s, 1 + ey, pl.ds(x0 + 1 + ex, xs), pl.ds(1 + ez, 6)].reshape(rows, 256)
            total = total + dot_nt(left, weights[number])
        return total

    def adjoint(s, x0, xs):
        rows = xs * 64
        total = jnp.zeros((rows, 256), F32)
        for number, (ex, ey, ez) in enumerate(taps):
            left = hidden[s, 1 - ey, pl.ds(x0 + 1 - ex, xs), pl.ds(1 - ez, 4)].reshape(rows, 256)
            total = total + dot(left, weights[number])
        return (-COARSE_STEP * total).reshape(xs, 4, 16, 256)

    def store(s, v, x0, xs):
        v = v.reshape(xs, 6, 16, 256)
        for z in range(6):
            at = start + z
            part = v[:, z] * jnp.where((at >= 0) & (at < 128), 1.0, 0.0).astype(F32)
            before, after = side_rows(part)
            here = (pl.ds(x0 + 1, xs), z)
            hidden[(s, 0) + here] = before.astype(BF)
            hidden[(s, 1) + here] = part.astype(BF)
            hidden[(s, 2) + here] = after.astype(BF)

    xs = 4
    for x0 in range(0, 8, xs):
        squash = jnp.tanh(forward(0, x0, xs))
        store(0, squash, x0, xs)
        store(1, (1.0 - squash * squash) * forward(1, x0, xs), x0, xs)
    near = jnp.where(quarter == 1, 1.0, 0.0).astype(F32)
    back = swap_table(8, 16)
    far = jnp.where(quarter == 2, 1.0, 0.0).astype(F32)
    xs = 4
    for x in range(8):
        if x % xs == 0:
            force, pull = adjoint(0, x, xs), adjoint(1, x, xs)
        at = x % xs
        ground = base[x]
        rows = jnp.concatenate([force[at, 0:2] + near * ground, force[at, 2:4] + far * ground, pull[at]], axis=0)
        out[x] = dot(back, rows.reshape(128, 256).astype(BF)).astype(BF).reshape(16, 8, 256)


def local(fine_prev, fine_now, fine_kernels, coarse_kernel, cotangent):
    packed = pl.pallas_call(
        pack_kernel,
        out_shape=jax.ShapeDtypeStruct((128, CHUNK, 128), BF),
        in_specs=vmem(3),
        out_specs=pl.BlockSpec(memory_space=pltpu.VMEM),
        scratch_shapes=[
            pltpu.VMEM((2048, 256), BF),
            pltpu.VMEM((1024, 512), F32),
            pltpu.VMEM((2048, 256), BF),
        ],
        compiler_params=pltpu.CompilerParams(vmem_limit_bytes=32 << 20),
        name="pack",
    )(fine_now, fine_prev, cotangent.reshape(256, 128))
    chunk = lax.all_to_all(packed, AXES, 0, 0).reshape(8, 16, CHUNK, 128)
    tile = np.tile(np.eye(32, dtype=np.float32), (1, 4)).astype(BF)
    weights = pl.pallas_call(
        weight_kernel,
        grid=(LAYERS,),
        out_shape=jax.ShapeDtypeStruct((LAYERS, 2, 8, 256, 256), BF),
        in_specs=[
            pl.BlockSpec((1, 864, 32), lambda i: (i, 0, 0)),
            pl.BlockSpec((1, 864, 32), lambda i: (i, 0, 0)),
            pl.BlockSpec((32, 128), lambda i: (0, 0)),
        ],
        out_specs=pl.BlockSpec((1, 2, 8, 256, 256), lambda i: (i, 0, 0, 0, 0)),
        scratch_shapes=[pltpu.VMEM((27, 32, 128), BF)],
        compiler_params=pltpu.CompilerParams(vmem_limit_bytes=32 << 20),
        cost_estimate=pl.CostEstimate(flops=10**10, bytes_accessed=10**7, transcendentals=0),
        name="spread_weights",
    )(
        jnp.swapaxes(fine_kernels, 2, 3).reshape(LAYERS, 864, 32),
        fine_kernels.reshape(LAYERS, 864, 32),
        tile,
    )

    kernel_part, weights = lax.optimization_barrier((coarse_kernel, weights))
    across = lax.ppermute(kernel_part, "g", [(i, i ^ 2) for i in range(4)])
    there = lax.ppermute(kernel_part, "g", [(i, i ^ 1) for i in range(4)])

    def round_ring(v):
        return [v] + [lax.ppermute(v, "q", [(i, (i + k) % 4) for i in range(4)]) for k in range(1, 4)]

    cots = round_ring(lax.slice_in_dim(chunk, 16, 24, axis=2))
    buffer = pltpu.VMEM((10, NOW + 2, 16, 256), BF)
    mid, base = pl.pallas_call(
        fine_kernel,
        out_shape=(
            jax.ShapeDtypeStruct((8, OWN, 16, 256), BF),
            jax.ShapeDtypeStruct((8, OWN, 16, 256), F32),
        ),
        in_specs=vmem(1) + [pl.BlockSpec(memory_space=pl.ANY)],
        out_specs=tuple(vmem(2)),
        scratch_shapes=[pltpu.VMEM((8, NOW, 16, 256), F32)] * 2
        + [buffer] * 4
        + [pltpu.VMEM((LAYERS, 2, 8, 256, 256), BF), pltpu.SemaphoreType.DMA((LAYERS,))],
        compiler_params=pltpu.CompilerParams(vmem_limit_bytes=48 << 20),
        cost_estimate=pl.CostEstimate(flops=2 * 10**10, bytes_accessed=10**7, transcendentals=10**6),
        name="fine_layers",
    )(chunk, weights)
    mid, across, *cots = lax.optimization_barrier((mid, across, *cots))
    opposite = lax.ppermute(across, "g", [(i, i ^ 1) for i in range(4)])
    partial = pl.pallas_call(
        coarse_kernel_body,
        out_shape=jax.ShapeDtypeStruct((8, 16, 8, 256), BF),
        in_specs=vmem(9) + [pl.BlockSpec(memory_space=pl.ANY)] * 4,
        out_specs=pl.BlockSpec(memory_space=pltpu.VMEM),
        scratch_shapes=[
            pltpu.VMEM((2, 3, 10, 8, 16, 256), BF),
            pltpu.VMEM((2, 3, 10, 6, 16, 256), BF),
            pltpu.VMEM((27, 256, 256), BF),
            pltpu.SemaphoreType.DMA((4,)),
        ],
        compiler_params=pltpu.CompilerParams(vmem_limit_bytes=48 << 20),
        cost_estimate=pl.CostEstimate(flops=2 * 10**10, bytes_accessed=10**7, transcendentals=10**6),
        name="coarse_layer",
    )(*round_ring(mid), *cots, base, coarse_kernel, across, there, opposite)
    parts = lax.all_to_all(partial.reshape(128, 8, 256), AXES, 0, 0)
    sums = lax.dot_general(
        parts.reshape(1024, 256), receive_table(), (((0,), (0,)), ((), ())), preferred_element_type=F32
    )
    coarse_next = sums[:, 0:128].reshape(256, 1, 1, 128)
    state_adjoint = 2.0 * cotangent.astype(F32) + sums[:, 128:256].reshape(256, 1, 1, 128)
    return coarse_next, state_adjoint


def solution(mesh):
    split = Mesh(mesh.devices.reshape(8, 4, 4), AXES)
    rows = P(None, "b", ("q", "g"), None)
    return jax.shard_map(
        local,
        mesh=split,
        in_specs=(rows, rows, P(), P(None, ("q", "g"), None), rows),
        out_specs=(rows, rows),
        check_vma=False,
    )
```

```python
import math

import jax
import jax.numpy as jnp
import numpy as np
from jax import lax
from jax.experimental import pallas as pl
from jax.experimental.pallas import tpu as pltpu
from jax.sharding import Mesh, PartitionSpec as P


BF = jnp.bfloat16
F32 = jnp.float32
LAYERS = 4
AXES = ("b", "q", "l", "c")
CHIPS = AXES[:3]
FINE_STEP = 0.5
COARSE_STEP = 1.5
NOW, OWN = 10, 2
SHIFT = 4
NOWS, PREVS, COTS = NOW + SHIFT, NOW - 2 + SHIFT, 8 + SHIFT
ROWS = (32, 2 * PREVS, 2 * COTS)
CHUNK = sum(ROWS)
EARLY = 13


def window_start(b, q, l):
    return 16 * b + 8 * l - 6 + 2 * q


def iota(shape, axis):
    return lax.broadcasted_iota(jnp.int32, shape, axis)


def ones_where(mask):
    return jnp.where(mask, 1.0, 0.0).astype(F32)


def swap_table(outer, inner):
    n = outer * inner
    row, column = iota((n, n), 0), iota((n, n), 1)
    return ones_where(column == row % outer * inner + row // outer).astype(BF)


def haar_signs(lane, channel):
    code = lane // 64 % 2 * 4 + lane // 32 % 2 * 2 + lane // 128
    both = code & channel % 8
    odd = (both ^ both // 2 ^ both // 4) & 1
    return jnp.where(lane % 32 == channel // 8, 1.0 - 2.0 * odd.astype(F32), 0.0).astype(BF)


def dot(x, y):
    return jnp.dot(x, y, preferred_element_type=F32)


def dot_nt(x, y):
    return lax.dot_general(x, y, (((1,), (1,)), ((), ())), preferred_element_type=F32)


def vmem(n):
    return [pl.BlockSpec(memory_space=pltpu.VMEM)] * n


def parity_rows(ref):
    return jnp.concatenate([ref[:, a, b, :] for a in range(2) for b in range(2)], axis=0)


def pack_kernel(now_in, prev_in, cot_in, out, now, prev, cot, first, second, third, sems):
    copies = []
    for i, (source, target) in enumerate(((now_in, now), (prev_in, prev), (cot_in, cot))):
        copy = pltpu.make_async_copy(source, target, sems.at[i])
        copy.start()
        copies.append(copy)
    k, lane = iota((32, 256), 0), iota((32, 256), 1)
    for_first = jnp.where(k < 2 * NOWS, lane - 2 * (k % NOWS) - k // NOWS, -1000)
    k, lane = iota((24, 256), 0), iota((24, 256), 1)
    for_second = lane - 2 * (1 + k % PREVS) - k // PREVS
    for_third = jnp.where(lane // 128 == k // COTS, lane % 128 - k % COTS, -1000)
    for target in range(0, 64, 2):
        spots = [(t // 8, t // 2 % 4, t % 2) for t in (target, target + 1)]
        for t, spot in enumerate(spots):
            at = 32 * (target + t)
            first[at : at + 32] = ones_where(for_first == 2 * window_start(*spot)).astype(BF)
        pair = [ones_where(for_second == 2 * window_start(*spot)) for spot in spots]
        second[24 * target : 24 * target + 48] = jnp.concatenate(pair, axis=0).astype(BF)
        pair = [ones_where(for_third == 16 * b + 8 * l - 2) for b, _, l in spots]
        third[24 * target : 24 * target + 48] = jnp.concatenate(pair, axis=0).astype(BF)
    for copy in copies:
        copy.wait()
    now_rows = parity_rows(now).astype(BF)
    prev_rows = parity_rows(prev).astype(BF)
    cot_rows = jnp.concatenate([cot[0:128, :], cot[128:256, :]], axis=1)
    part = 16
    for t in range(0, 64, part):
        groups = []
        for table, size, rows in zip((first, second, third), ROWS, (now_rows, prev_rows, cot_rows)):
            groups.append(dot_nt(table[pl.ds(size * t, size * part), :], rows).reshape(part, size, 128))
        out[pl.ds(t, part)] = jnp.concatenate(groups, axis=1).astype(BF)


def sort_table(core):
    row, column = iota((128, 128), 0), iota((128, 128), 1)
    y = row % 16
    source = (y + core) % 2
    return ones_where(column == (source * 8 + y // 2) * 8 + row // 16).astype(BF)


def sorted_parts(table, mine, other, x, start, stop):
    rows = jnp.concatenate([mine[x].astype(F32), other[x].astype(F32)], axis=0)
    parts = []
    for k in range(start, stop, 8):
        moved = dot(table, rows[:, k : k + 8, :].reshape(128, 128).astype(BF))
        parts += [moved[16 * j : 16 * j + 16] for j in range(8)]
    return parts


def split_dot(x, y):
    top = x.astype(BF)
    low = (x - top.astype(F32)).astype(BF)
    return dot(top, y) + dot(low, y)


def tap_index(dx, dy, dz, a2, b2, d2, a, b, d):
    def offset(moved, bit, to):
        place = (-1 if bit else 2) if moved else bit
        return place - to

    e = (offset(dx, a, a2), offset(dy, b, b2), offset(dz, d, d2))
    if any(abs(v) > 1 for v in e):
        return None
    return 9 * (e[0] + 1) + 3 * (e[1] + 1) + e[2] + 1


def weight_kernel(forward, adjoint, tile, out, wide):
    lane = lax.broadcasted_iota(jnp.int32, (32, 128), 1)
    masks = [jnp.where(lane // 32 == v, 1.0, 0.0).astype(BF) for v in range(4)]
    for way in range(2):
        source = (forward, adjoint)[way]
        wide[...] = dot(source[0], tile[...]).astype(BF).reshape(27, 32, 128)
        for moved in range(8):
            dx, dy, dz = moved >> 2, moved >> 1 & 1, moved & 1
            for u in range(8):
                d, a, b = u >> 2, u >> 1 & 1, u & 1
                for d2 in range(2):
                    total = jnp.zeros((32, 128), BF)
                    for v in range(4):
                        tap = tap_index(dx, dy, dz, v >> 1, v & 1, d2, a, b, d)
                        if tap is not None:
                            total = total + masks[v] * wide[26 - tap if way else tap]
                    out[0, way, moved, 32 * u : 32 * u + 32, 128 * d2 : 128 * d2 + 128] = total


def side_rows(v):
    row = lax.broadcasted_iota(jnp.int32, (16, 256), 0)
    axis = v.ndim - 2
    before = jnp.where(row == 0, 0.0, pltpu.roll(v, 1, axis))
    after = jnp.where(row == 15, 0.0, pltpu.roll(v, 15, axis))
    return before, after


def moved_rows(v):
    lane = lax.broadcasted_iota(jnp.int32, (16, 256), 1)
    before, after = side_rows(v)
    return jnp.where(lane // 32 % 2 == 1, before, after)


def block_conv(plain, turned, weights, x0, xs, z0, zs):
    rows = xs * zs * 16
    lane = lax.broadcasted_iota(jnp.int32, (1, 1, 16, 256), 3)
    high = lane // 64 % 2 == 1
    total = jnp.zeros((rows, 256), F32)

    def at(ref, dx, moved_z):
        xsl = pl.ds(x0 + 1 + dx, xs)
        if not moved_z:
            return ref[xsl, pl.ds(z0 + 1, zs)]
        return jnp.concatenate(
            [ref[xsl, pl.ds(z0 + 2, zs), :, 0:128], ref[xsl, pl.ds(z0, zs), :, 128:256]], axis=-1
        )

    for moved in range(8):
        dx, dy, dz = moved >> 2, moved >> 1 & 1, moved & 1
        ref = turned if dy else plain
        if dx:
            left = jnp.where(high, at(ref, -1, dz), at(ref, 1, dz))
        else:
            left = at(ref, 0, dz)
        total = total + dot(left.reshape(rows, 256), weights[moved])
    return total


def fine_kernel(mine, other, spread, mid, base, cur, old, s0, s1, h0, h1, weights, sems):
    copies = []
    for layer in range(LAYERS):
        copy = pltpu.make_async_copy(spread.at[layer], weights.at[layer], sems.at[layer])
        copy.start()
        copies.append(copy)
    core = lax.axis_index("c")
    shift = SHIFT * core
    start = window_start(*(lax.axis_index(name) for name in CHIPS)) + shift
    table = sort_table(core)
    for ref in (s0, s1, h0, h1):
        for x in (0, 9):
            ref[x] = jnp.zeros((NOW + 2, 16, 256), BF)
        for z in (0, NOW + 1):
            ref[:, z] = jnp.zeros((10, 16, 256), BF)

    def keep(z):
        at = start + z
        return jnp.where((at >= 0) & (at < 128), 1.0, 0.0).astype(F32)

    def unpack(x, carry):
        parts = sorted_parts(table, mine, other, x, 0, ROWS[0] + ROWS[1])
        for z in range(NOWS):
            cur[x, z] = jnp.concatenate([parts[z], parts[NOWS + z]], axis=1)
        at = ROWS[0]
        for z in range(PREVS):
            old[x, z + 1] = jnp.concatenate([parts[at + z], parts[at + PREVS + z]], axis=1)
        for z in range(NOW):
            v = cur[x, shift + z]
            s0[x + 1, z + 1] = v.astype(BF)
            s1[x + 1, z + 1] = moved_rows(v).astype(BF)
        return carry

    lax.fori_loop(0, 8, unpack, 0)

    now, before = cur, old
    for layer in range(LAYERS):
        copies[layer].wait()
        zs = NOW - 2 * layer
        xs = max(1, 128 // (16 * zs)) if zs > 6 else 8 // zs + (zs == 6)

        def squash(i, carry, layer=layer, zs=zs, xs=xs):
            x0 = i * xs
            v = jnp.tanh(block_conv(s0, s1, weights.at[layer, 0], x0, xs, layer, zs))
            v = v.reshape(xs, zs, 16, 256)
            for z in range(zs):
                part = v[:, z] * keep(layer + z)
                h0[pl.ds(x0 + 1, xs), layer + z + 1] = part.astype(BF)
                h1[pl.ds(x0 + 1, xs), layer + z + 1] = moved_rows(part).astype(BF)
            return carry

        lax.fori_loop(0, 8 // xs, squash, 0, unroll=True)
        zs = NOW - 2 * layer - 2
        xs = max(1, 128 // (16 * zs)) if zs > 6 else 8 // zs + (zs == 6)
        last = layer == LAYERS - 1

        def update(i, carry, layer=layer, zs=zs, xs=xs, now=now, before=before, last=last):
            x0 = i * xs
            v = block_conv(h0, h1, weights.at[layer, 1], x0, xs, layer + 1, zs)
            v = v.reshape(xs, zs, 16, 256)
            for z in range(zs):
                at = layer + 1 + z
                here = (pl.ds(x0, xs), shift + at)
                part = (2.0 * now[here] - before[here] - FINE_STEP * v[:, z]) * keep(at)
                before[here] = part
                if not last:
                    s0[pl.ds(x0 + 1, xs), at + 1] = part.astype(BF)
                    s1[pl.ds(x0 + 1, xs), at + 1] = moved_rows(part).astype(BF)
            return carry

        lax.fori_loop(0, 8 // xs, update, 0, unroll=True)
        now, before = before, now

    haar = haar_signs(iota((256, 256), 0), iota((256, 256), 1))
    scale = 1.0 / math.sqrt(8.0)
    own = (slice(None), pl.ds(shift + 4, OWN))
    latest = now[own].reshape(256, 256)
    earlier = before[own].reshape(256, 256)
    mid[...] = (split_dot(latest, haar) * scale).astype(BF).reshape(8, OWN, 16, 256)
    base[...] = (split_dot(2.0 * latest - earlier, haar) * scale).reshape(8, OWN, 16, 256)


def coarse_kernel_body(*refs):
    own, mine, other, base, pieces = refs[0:4], refs[4], refs[5], refs[6], refs[7:13]
    out, state, hidden, weights, cots, sems = refs[13:19]
    b, quarter, l, core = (lax.axis_index(name) for name in AXES)
    start = 4 * (4 * b + 2 * l + core) - 1
    table = sort_table(core)
    copies = []
    spots = ((0, 27, 0), (0, 27, 1), (0, EARLY, 2), (EARLY, 27, 2), (0, EARLY, 3), (EARLY, 27, 3))
    for i, (w, (low, high, part)) in enumerate(zip(pieces, spots)):
        target = weights.at[pl.ds(low, high - low), pl.ds(64 * part, 64), :]
        copy = pltpu.make_async_copy(w, target, sems.at[i])
        copy.start()
        copies.append(copy)
    for s in range(2):
        for y in range(3):
            for x in (0, 9):
                state[s, y, x] = jnp.zeros((8, 16, 256), BF)
                hidden[s, y, x] = jnp.zeros((6, 16, 256), BF)
    def place(s, x, xs, z, wide):
        before, after = side_rows(wide)
        state[s, 0, pl.ds(x + 1, xs), z] = before.astype(BF)
        state[s, 1, pl.ds(x + 1, xs), z] = wide.astype(BF)
        state[s, 2, pl.ds(x + 1, xs), z] = after.astype(BF)

    for k in range(4):
        z0 = OWN * ((quarter + 4 - k) % 4)
        for z in range(OWN):
            place(0, 0, 8, z0 + z, own[k][:, z].astype(F32))

    for x in range(8):
        parts = sorted_parts(table, mine, other, x, ROWS[0] + ROWS[1], CHUNK)
        for z in range(COTS):
            cots[x, z] = jnp.concatenate([parts[z], parts[COTS + z]], axis=1)
        for z in range(8):
            place(1, x, 1, z, cots[x, SHIFT * core + z][None])
    for copy in copies:
        copy.wait()
    taps = [(x, y, z) for x in (-1, 0, 1) for y in (-1, 0, 1) for z in (-1, 0, 1)]

    def forward(s, x0, xs):
        rows = xs * 96
        total = jnp.zeros((rows, 256), F32)
        for number, (ex, ey, ez) in enumerate(taps):
            left = state[s, 1 + ey, pl.ds(x0 + 1 + ex, xs), pl.ds(1 + ez, 6)].reshape(rows, 256)
            total = total + dot_nt(left, weights[number])
        return total

    def adjoint(s, x0, xs):
        rows = xs * 64
        total = jnp.zeros((rows, 256), F32)
        for number, (ex, ey, ez) in enumerate(taps):
            left = hidden[s, 1 - ey, pl.ds(x0 + 1 - ex, xs), pl.ds(1 - ez, 4)].reshape(rows, 256)
            total = total + dot(left, weights[number])
        return (-COARSE_STEP * total).reshape(xs, 4, 16, 256)

    def store(s, v, x0, xs):
        v = v.reshape(xs, 6, 16, 256)
        for z in range(6):
            at = start + z
            part = v[:, z] * jnp.where((at >= 0) & (at < 128), 1.0, 0.0).astype(F32)
            before, after = side_rows(part)
            here = (pl.ds(x0 + 1, xs), z)
            hidden[(s, 0) + here] = before.astype(BF)
            hidden[(s, 1) + here] = part.astype(BF)
            hidden[(s, 2) + here] = after.astype(BF)

    xs = 4
    for x0 in range(0, 8, xs):
        squash = jnp.tanh(forward(0, x0, xs))
        store(0, squash, x0, xs)
        store(1, (1.0 - squash * squash) * forward(1, x0, xs), x0, xs)
    near = jnp.where(quarter == 1, 1.0, 0.0).astype(F32)
    back = swap_table(8, 16)
    far = jnp.where(quarter == 2, 1.0, 0.0).astype(F32)
    xs = 4
    for x in range(8):
        if x % xs == 0:
            force, pull = adjoint(0, x, xs), adjoint(1, x, xs)
        at = x % xs
        ground = base[x]
        rows = jnp.concatenate([force[at, 0:2] + near * ground, force[at, 2:4] + far * ground, pull[at]], axis=0)
        out[x] = dot(back, rows.reshape(128, 256).astype(BF)).astype(BF).reshape(16, 8, 256)


def receive_table():
    row = np.arange(1024)
    at = row // 128 * 16 + row // 8 % 4 * 4 + row % 4 + row // 4 % 2 * 128
    return (np.arange(256)[None] == at[:, None]).astype(BF)


def local(fine_prev, fine_now, fine_kernels, coarse_kernel, cotangent):
    packed = pl.pallas_call(
        pack_kernel,
        out_shape=jax.ShapeDtypeStruct((64, CHUNK, 128), BF),
        in_specs=[pl.BlockSpec(memory_space=pltpu.HBM)] * 3,
        out_specs=pl.BlockSpec(memory_space=pltpu.VMEM),
        scratch_shapes=[pltpu.VMEM((32, 2, 2, 256), F32)] * 2
        + [pltpu.VMEM((256, 128), BF)]
        + [pltpu.VMEM((64 * size, 256), BF) for size in ROWS]
        + [pltpu.SemaphoreType.DMA((3,))],
        compiler_params=pltpu.CompilerParams(vmem_limit_bytes=60 << 20),
        name="pack",
    )(fine_now, fine_prev, cotangent.reshape(256, 128))
    packed, kernel_part = lax.optimization_barrier((packed, coarse_kernel))
    early = lax.ppermute(kernel_part[:EARLY], "l", [(0, 1), (1, 0)])
    across = lax.ppermute(kernel_part[EARLY:], "l", [(0, 1), (1, 0)])
    there = lax.ppermute(kernel_part, "c", [(0, 1), (1, 0)])
    mine = lax.all_to_all(packed, CHIPS, 0, 0)
    tile = np.tile(np.eye(32, dtype=np.float32), (1, 4)).astype(BF)
    weights = pl.pallas_call(
        weight_kernel,
        grid=(LAYERS,),
        out_shape=jax.ShapeDtypeStruct((LAYERS, 2, 8, 256, 256), BF),
        in_specs=[
            pl.BlockSpec((1, 864, 32), lambda i: (i, 0, 0)),
            pl.BlockSpec((1, 864, 32), lambda i: (i, 0, 0)),
            pl.BlockSpec((32, 128), lambda i: (0, 0)),
        ],
        out_specs=pl.BlockSpec((1, 2, 8, 256, 256), lambda i: (i, 0, 0, 0, 0)),
        scratch_shapes=[pltpu.VMEM((27, 32, 128), BF)],
        compiler_params=pltpu.CompilerParams(vmem_limit_bytes=60 << 20),
        cost_estimate=pl.CostEstimate(flops=10**10, bytes_accessed=10**7, transcendentals=0),
        name="spread_weights",
    )(
        jnp.swapaxes(fine_kernels, 2, 3).reshape(LAYERS, 864, 32),
        fine_kernels.reshape(LAYERS, 864, 32),
        tile,
    )

    mine, weights, there, early = lax.optimization_barrier((mine, weights, there, early))
    other = lax.ppermute(mine, "c", [(0, 1), (1, 0)]).reshape(8, 8, CHUNK, 128)
    mine = mine.reshape(8, 8, CHUNK, 128)
    def round_ring(v):
        return [v] + [lax.ppermute(v, "q", [(i, (i + k) % 4) for i in range(4)]) for k in range(1, 4)]

    buffer = pltpu.VMEM((10, NOW + 2, 16, 256), BF)
    mid, base = pl.pallas_call(
        fine_kernel,
        out_shape=(
            jax.ShapeDtypeStruct((8, OWN, 16, 256), BF),
            jax.ShapeDtypeStruct((8, OWN, 16, 256), F32),
        ),
        in_specs=vmem(2) + [pl.BlockSpec(memory_space=pl.ANY)],
        out_specs=tuple(vmem(2)),
        scratch_shapes=[pltpu.VMEM((8, NOWS, 16, 256), F32)] * 2
        + [buffer] * 4
        + [pltpu.VMEM((LAYERS, 2, 8, 256, 256), BF), pltpu.SemaphoreType.DMA((LAYERS,))],
        compiler_params=pltpu.CompilerParams(vmem_limit_bytes=48 << 20),
        cost_estimate=pl.CostEstimate(flops=10**9, bytes_accessed=10**6, transcendentals=10**6),
        name="fine_layers",
    )(mine, other, weights)
    mid, across = lax.optimization_barrier((mid, across))
    states = round_ring(mid)
    opposite = lax.ppermute(across, "c", [(0, 1), (1, 0)])
    early_opposite = lax.ppermute(early, "c", [(0, 1), (1, 0)])
    partial = pl.pallas_call(
        coarse_kernel_body,
        out_shape=jax.ShapeDtypeStruct((8, 16, 8, 256), BF),
        in_specs=vmem(7) + [pl.BlockSpec(memory_space=pl.ANY)] * 6,
        out_specs=pl.BlockSpec(memory_space=pltpu.VMEM),
        scratch_shapes=[
            pltpu.VMEM((2, 3, 10, 8, 16, 256), BF),
            pltpu.VMEM((2, 3, 10, 6, 16, 256), BF),
            pltpu.VMEM((27, 256, 256), BF),
            pltpu.VMEM((8, COTS, 16, 256), F32),
            pltpu.SemaphoreType.DMA((6,)),
        ],
        compiler_params=pltpu.CompilerParams(vmem_limit_bytes=48 << 20),
        cost_estimate=pl.CostEstimate(flops=2 * 10**10, bytes_accessed=10**7, transcendentals=10**6),
        name="coarse_layer",
    )(*states, mine, other, base, coarse_kernel, there, early, across, early_opposite, opposite)
    parts = lax.all_to_all(partial.reshape(128, 8, 256), AXES, 0, 0)
    parts = parts.reshape(1024, 256)
    table = receive_table()
    over_rows = (((0,), (0,)), ((), ()))
    coarse_next = lax.dot_general(parts, table[:, 0:128], over_rows, preferred_element_type=F32)
    state_adjoint = lax.dot_general(parts, table[:, 128:256], over_rows, preferred_element_type=F32)
    state_adjoint = state_adjoint + 2.0 * cotangent.reshape(256, 128).astype(F32)
    return coarse_next.reshape(256, 1, 1, 128), state_adjoint.reshape(256, 1, 1, 128)


def solution(mesh):
    split = Mesh(mesh.devices.reshape(8, 4, 2, 2), AXES)
    rows = P(None, "b", ("q", "l", "c"), None)
    return jax.shard_map(
        local,
        mesh=split,
        in_specs=(rows, rows, P(), P(None, ("q", "l", "c"), None), rows),
        out_specs=(rows, rows),
        check_vma=False,
    )
```

```python
import math

import jax
import jax.numpy as jnp
import numpy as np
from jax import lax
from jax.experimental import pallas as pl
from jax.experimental.pallas import tpu as pltpu
from jax.sharding import Mesh, PartitionSpec as P


BF = jnp.bfloat16
F32 = jnp.float32
LAYERS = 4
AXES = ("b", "q", "l", "c")
CHIPS = AXES[:3]
FINE_STEP = 0.5
COARSE_STEP = 1.5
NOW, OWN = 10, 2
SHIFT = 4
NOWS, PREVS, COTS = NOW + SHIFT, NOW - 2 + SHIFT, 8 + SHIFT
ROWS = (32, 2 * PREVS, 2 * COTS)
CHUNK = sum(ROWS)
LOWER = 13


def window_start(b, q, l):
    return 16 * b + 8 * l - 6 + 2 * q


def iota(shape, axis):
    return lax.broadcasted_iota(jnp.int32, shape, axis)


def ones_where(mask):
    return jnp.where(mask, 1.0, 0.0).astype(F32)


def swap_table(outer, inner):
    n = outer * inner
    row, column = iota((n, n), 0), iota((n, n), 1)
    return ones_where(column == row % outer * inner + row // outer).astype(BF)


def haar_signs(lane, channel):
    code = lane // 64 % 2 * 4 + lane // 32 % 2 * 2 + lane // 128
    both = code & channel % 8
    odd = (both ^ both // 2 ^ both // 4) & 1
    return jnp.where(lane % 32 == channel // 8, 1.0 - 2.0 * odd.astype(F32), 0.0).astype(BF)


def dot(x, y):
    return jnp.dot(x, y, preferred_element_type=F32)


def dot_nt(x, y):
    return lax.dot_general(x, y, (((1,), (1,)), ((), ())), preferred_element_type=F32)


def vmem(n):
    return [pl.BlockSpec(memory_space=pltpu.VMEM)] * n


def parity_rows(ref):
    return jnp.concatenate([ref[:, a, b, :] for a in range(2) for b in range(2)], axis=0)


def pack_kernel(now_in, prev_in, cot_in, out, now, prev, cot, first, second, third, sems):
    copies = []
    for i, (source, target) in enumerate(((now_in, now), (prev_in, prev), (cot_in, cot))):
        copy = pltpu.make_async_copy(source, target, sems.at[i])
        copy.start()
        copies.append(copy)
    k, lane = iota((32, 256), 0), iota((32, 256), 1)
    for_first = jnp.where(k < 2 * NOWS, lane - 2 * (k % NOWS) - k // NOWS, -1000)
    k, lane = iota((24, 256), 0), iota((24, 256), 1)
    for_second = lane - 2 * (1 + k % PREVS) - k // PREVS
    for_third = jnp.where(lane // 128 == k // COTS, lane % 128 - k % COTS, -1000)
    for target in range(0, 64, 2):
        spots = [(t // 8, t // 2 % 4, t % 2) for t in (target, target + 1)]
        for t, spot in enumerate(spots):
            at = 32 * (target + t)
            first[at : at + 32] = ones_where(for_first == 2 * window_start(*spot)).astype(BF)
        pair = [ones_where(for_second == 2 * window_start(*spot)) for spot in spots]
        second[24 * target : 24 * target + 48] = jnp.concatenate(pair, axis=0).astype(BF)
        pair = [ones_where(for_third == 16 * b + 8 * l - 2) for b, _, l in spots]
        third[24 * target : 24 * target + 48] = jnp.concatenate(pair, axis=0).astype(BF)
    for copy in copies:
        copy.wait()
    now_rows = parity_rows(now).astype(BF)
    prev_rows = parity_rows(prev).astype(BF)
    cot_rows = jnp.concatenate([cot[0:128, :], cot[128:256, :]], axis=1)
    part = 16
    for t in range(0, 64, part):
        groups = []
        for table, size, rows in zip((first, second, third), ROWS, (now_rows, prev_rows, cot_rows)):
            groups.append(dot_nt(table[pl.ds(size * t, size * part), :], rows).reshape(part, size, 128))
        out[pl.ds(t, part)] = jnp.concatenate(groups, axis=1).astype(BF)


def sort_table(core):
    row, column = iota((128, 128), 0), iota((128, 128), 1)
    y = row % 16
    source = (y + core) % 2
    return ones_where(column == (source * 8 + y // 2) * 8 + row // 16).astype(BF)


def sorted_parts(table, mine, other, x, start, stop):
    rows = jnp.concatenate([mine[x].astype(F32), other[x].astype(F32)], axis=0)
    parts = []
    for k in range(start, stop, 8):
        moved = dot(table, rows[:, k : k + 8, :].reshape(128, 128).astype(BF))
        parts += [moved[16 * j : 16 * j + 16] for j in range(8)]
    return parts


def split_dot(x, y):
    top = x.astype(BF)
    low = (x - top.astype(F32)).astype(BF)
    return dot(top, y) + dot(low, y)


def tap_index(dx, dy, dz, a2, b2, d2, a, b, d):
    def offset(moved, bit, to):
        place = (-1 if bit else 2) if moved else bit
        return place - to

    e = (offset(dx, a, a2), offset(dy, b, b2), offset(dz, d, d2))
    if any(abs(v) > 1 for v in e):
        return None
    return 9 * (e[0] + 1) + 3 * (e[1] + 1) + e[2] + 1


def weight_kernel(forward, adjoint, tile, out, wide):
    lane = lax.broadcasted_iota(jnp.int32, (32, 128), 1)
    masks = [jnp.where(lane // 32 == v, 1.0, 0.0).astype(BF) for v in range(4)]
    for way in range(2):
        source = (forward, adjoint)[way]
        wide[...] = dot(source[0], tile[...]).astype(BF).reshape(27, 32, 128)
        for moved in range(8):
            dx, dy, dz = moved >> 2, moved >> 1 & 1, moved & 1
            for u in range(8):
                d, a, b = u >> 2, u >> 1 & 1, u & 1
                for d2 in range(2):
                    total = jnp.zeros((32, 128), BF)
                    for v in range(4):
                        tap = tap_index(dx, dy, dz, v >> 1, v & 1, d2, a, b, d)
                        if tap is not None:
                            total = total + masks[v] * wide[26 - tap if way else tap]
                    out[0, way, moved, 32 * u : 32 * u + 32, 128 * d2 : 128 * d2 + 128] = total


def side_rows(v):
    row = lax.broadcasted_iota(jnp.int32, (16, 256), 0)
    axis = v.ndim - 2
    before = jnp.where(row == 0, 0.0, pltpu.roll(v, 1, axis))
    after = jnp.where(row == 15, 0.0, pltpu.roll(v, 15, axis))
    return before, after


def moved_rows(v):
    lane = lax.broadcasted_iota(jnp.int32, (16, 256), 1)
    before, after = side_rows(v)
    return jnp.where(lane // 32 % 2 == 1, before, after)


def block_conv(plain, turned, weights, x0, xs, z0, zs):
    rows = xs * zs * 16
    lane = lax.broadcasted_iota(jnp.int32, (1, 1, 16, 256), 3)
    high = lane // 64 % 2 == 1
    total = jnp.zeros((rows, 256), F32)

    def at(ref, dx, moved_z):
        xsl = pl.ds(x0 + 1 + dx, xs)
        if not moved_z:
            return ref[xsl, pl.ds(z0 + 1, zs)]
        return jnp.concatenate(
            [ref[xsl, pl.ds(z0 + 2, zs), :, 0:128], ref[xsl, pl.ds(z0, zs), :, 128:256]], axis=-1
        )

    for moved in range(8):
        dx, dy, dz = moved >> 2, moved >> 1 & 1, moved & 1
        ref = turned if dy else plain
        if dx:
            left = jnp.where(high, at(ref, -1, dz), at(ref, 1, dz))
        else:
            left = at(ref, 0, dz)
        total = total + dot(left.reshape(rows, 256), weights[moved])
    return total


def fine_kernel(mine, other, spread, mid, base, cur, old, s0, s1, h0, h1, weights, sems):
    copies = []
    for layer in range(LAYERS):
        copy = pltpu.make_async_copy(spread.at[layer], weights.at[layer], sems.at[layer])
        copy.start()
        copies.append(copy)
    core = lax.axis_index("c")
    shift = SHIFT * core
    start = window_start(*(lax.axis_index(name) for name in CHIPS)) + shift
    table = sort_table(core)
    for ref in (s0, s1, h0, h1):
        for x in (0, 9):
            ref[x] = jnp.zeros((NOW + 2, 16, 256), BF)
        for z in (0, NOW + 1):
            ref[:, z] = jnp.zeros((10, 16, 256), BF)

    def keep(z):
        at = start + z
        return jnp.where((at >= 0) & (at < 128), 1.0, 0.0).astype(F32)

    def unpack(x, carry):
        parts = sorted_parts(table, mine, other, x, 0, ROWS[0] + ROWS[1])
        for z in range(NOWS):
            cur[x, z] = jnp.concatenate([parts[z], parts[NOWS + z]], axis=1)
        at = ROWS[0]
        for z in range(PREVS):
            old[x, z + 1] = jnp.concatenate([parts[at + z], parts[at + PREVS + z]], axis=1)
        for z in range(NOW):
            v = cur[x, shift + z]
            s0[x + 1, z + 1] = v.astype(BF)
            s1[x + 1, z + 1] = moved_rows(v).astype(BF)
        return carry

    lax.fori_loop(0, 8, unpack, 0)

    now, before = cur, old
    for layer in range(LAYERS):
        copies[layer].wait()
        zs = NOW - 2 * layer
        xs = max(1, 128 // (16 * zs)) if zs > 6 else 8 // zs + (zs == 6)

        def squash(i, carry, layer=layer, zs=zs, xs=xs):
            x0 = i * xs
            v = jnp.tanh(block_conv(s0, s1, weights.at[layer, 0], x0, xs, layer, zs))
            v = v.reshape(xs, zs, 16, 256)
            for z in range(zs):
                part = v[:, z] * keep(layer + z)
                h0[pl.ds(x0 + 1, xs), layer + z + 1] = part.astype(BF)
                h1[pl.ds(x0 + 1, xs), layer + z + 1] = moved_rows(part).astype(BF)
            return carry

        lax.fori_loop(0, 8 // xs, squash, 0, unroll=True)
        zs = NOW - 2 * layer - 2
        xs = max(1, 128 // (16 * zs)) if zs > 6 else 8 // zs + (zs == 6)
        last = layer == LAYERS - 1

        def update(i, carry, layer=layer, zs=zs, xs=xs, now=now, before=before, last=last):
            x0 = i * xs
            v = block_conv(h0, h1, weights.at[layer, 1], x0, xs, layer + 1, zs)
            v = v.reshape(xs, zs, 16, 256)
            for z in range(zs):
                at = layer + 1 + z
                here = (pl.ds(x0, xs), shift + at)
                part = (2.0 * now[here] - before[here] - FINE_STEP * v[:, z]) * keep(at)
                before[here] = part
                if not last:
                    s0[pl.ds(x0 + 1, xs), at + 1] = part.astype(BF)
                    s1[pl.ds(x0 + 1, xs), at + 1] = moved_rows(part).astype(BF)
            return carry

        lax.fori_loop(0, 8 // xs, update, 0, unroll=True)
        now, before = before, now

    haar = haar_signs(iota((256, 256), 0), iota((256, 256), 1))
    scale = 1.0 / math.sqrt(8.0)
    own = (slice(None), pl.ds(shift + 4, OWN))
    latest = now[own].reshape(256, 256)
    earlier = before[own].reshape(256, 256)
    mid[...] = (split_dot(latest, haar) * scale).astype(BF).reshape(8, OWN, 16, 256)
    base[...] = (split_dot(2.0 * latest - earlier, haar) * scale).reshape(8, OWN, 16, 256)


def coarse_kernel_body(*refs):
    own, base, chunks, pieces = refs[0:4], refs[4], refs[5:7], refs[7:13]
    out, state, hidden, weights, rows, cots, sems = refs[13:20]
    b, quarter, l, core = (lax.axis_index(name) for name in AXES)
    start = 4 * (4 * b + 2 * l + core) - 1
    table = sort_table(core)
    copies = []
    spots = ((0, 27, 0), (0, 27, 1), (0, LOWER, 2), (LOWER, 27, 2), (0, LOWER, 3), (LOWER, 27, 3))
    for i, (w, (low, high, part)) in enumerate(zip(pieces, spots)):
        target = weights.at[pl.ds(low, high - low), pl.ds(64 * part, 64), :]
        copy = pltpu.make_async_copy(w, target, sems.at[i])
        copy.start()
        copies.append(copy)
    for i, chunk in enumerate(chunks):
        copy = pltpu.make_async_copy(chunk.at[:, :, pl.ds(48, 32), :], rows.at[i], sems.at[6 + i])
        copy.start()
        copies.append(copy)
    for s in range(2):
        for y in range(3):
            for x in (0, 9):
                state[s, y, x] = jnp.zeros((8, 16, 256), BF)
                hidden[s, y, x] = jnp.zeros((6, 16, 256), BF)
    def place(s, x, xs, z, wide):
        before, after = side_rows(wide)
        state[s, 0, pl.ds(x + 1, xs), z] = before.astype(BF)
        state[s, 1, pl.ds(x + 1, xs), z] = wide.astype(BF)
        state[s, 2, pl.ds(x + 1, xs), z] = after.astype(BF)

    for k in range(4):
        z0 = OWN * ((quarter + 4 - k) % 4)
        for z in range(OWN):
            place(0, 0, 8, z0 + z, own[k][:, z].astype(F32))

    for copy in copies[6:]:
        copy.wait()
    for x in range(8):
        parts = sorted_parts(table, rows.at[0], rows.at[1], x, 8, 32)
        for z in range(COTS):
            cots[x, z] = jnp.concatenate([parts[z], parts[COTS + z]], axis=1)
        for z in range(8):
            place(1, x, 1, z, cots[x, SHIFT * core + z][None])
    for copy in copies[:6]:
        copy.wait()
    taps = [(x, y, z) for x in (-1, 0, 1) for y in (-1, 0, 1) for z in (-1, 0, 1)]

    def forward(s, x0, xs):
        rows = xs * 96
        total = jnp.zeros((rows, 256), F32)
        for number, (ex, ey, ez) in enumerate(taps):
            left = state[s, 1 + ey, pl.ds(x0 + 1 + ex, xs), pl.ds(1 + ez, 6)].reshape(rows, 256)
            total = total + dot_nt(left, weights[number])
        return total

    def adjoint(s, x0, xs):
        rows = xs * 64
        total = jnp.zeros((rows, 256), F32)
        for number, (ex, ey, ez) in enumerate(taps):
            left = hidden[s, 1 - ey, pl.ds(x0 + 1 - ex, xs), pl.ds(1 - ez, 4)].reshape(rows, 256)
            total = total + dot(left, weights[number])
        return (-COARSE_STEP * total).reshape(xs, 4, 16, 256)

    def store(s, v, x0, xs):
        v = v.reshape(xs, 6, 16, 256)
        for z in range(6):
            at = start + z
            part = v[:, z] * jnp.where((at >= 0) & (at < 128), 1.0, 0.0).astype(F32)
            before, after = side_rows(part)
            here = (pl.ds(x0 + 1, xs), z)
            hidden[(s, 0) + here] = before.astype(BF)
            hidden[(s, 1) + here] = part.astype(BF)
            hidden[(s, 2) + here] = after.astype(BF)

    xs = 4
    for x0 in range(0, 8, xs):
        squash = jnp.tanh(forward(0, x0, xs))
        store(0, squash, x0, xs)
        store(1, (1.0 - squash * squash) * forward(1, x0, xs), x0, xs)
    near = jnp.where(quarter == 1, 1.0, 0.0).astype(F32)
    back = swap_table(8, 16)
    far = jnp.where(quarter == 2, 1.0, 0.0).astype(F32)
    xs = 4
    for x in range(8):
        if x % xs == 0:
            force, pull = adjoint(0, x, xs), adjoint(1, x, xs)
        at = x % xs
        ground = base[x]
        rows = jnp.concatenate([force[at, 0:2] + near * ground, force[at, 2:4] + far * ground, pull[at]], axis=0)
        out[x] = dot(back, rows.reshape(128, 256).astype(BF)).astype(BF).reshape(16, 8, 256)


def receive_table():
    row = np.arange(1024)
    at = row // 128 * 16 + row // 8 % 4 * 4 + row % 4 + row // 4 % 2 * 128
    return (np.arange(256)[None] == at[:, None]).astype(BF)


def local(fine_prev, fine_now, fine_kernels, coarse_kernel, cotangent):
    packed = pl.pallas_call(
        pack_kernel,
        out_shape=jax.ShapeDtypeStruct((64, CHUNK, 128), BF),
        in_specs=[pl.BlockSpec(memory_space=pltpu.HBM)] * 3,
        out_specs=pl.BlockSpec(memory_space=pltpu.VMEM),
        scratch_shapes=[pltpu.VMEM((32, 2, 2, 256), F32)] * 2
        + [pltpu.VMEM((256, 128), BF)]
        + [pltpu.VMEM((64 * size, 256), BF) for size in ROWS]
        + [pltpu.SemaphoreType.DMA((3,))],
        compiler_params=pltpu.CompilerParams(vmem_limit_bytes=60 << 20),
        name="pack",
    )(fine_now, fine_prev, cotangent.reshape(256, 128))
    packed, kernel_part = lax.optimization_barrier((packed, coarse_kernel))
    lower_part, upper_part = kernel_part[:LOWER], kernel_part[LOWER:]
    there = lax.ppermute(kernel_part, "c", [(0, 1), (1, 0)])
    mine = lax.all_to_all(packed, CHIPS, 0, 0)
    tile = np.tile(np.eye(32, dtype=np.float32), (1, 4)).astype(BF)
    weights = pl.pallas_call(
        weight_kernel,
        grid=(LAYERS,),
        out_shape=jax.ShapeDtypeStruct((LAYERS, 2, 8, 256, 256), BF),
        in_specs=[
            pl.BlockSpec((1, 864, 32), lambda i: (i, 0, 0)),
            pl.BlockSpec((1, 864, 32), lambda i: (i, 0, 0)),
            pl.BlockSpec((32, 128), lambda i: (0, 0)),
        ],
        out_specs=pl.BlockSpec((1, 2, 8, 256, 256), lambda i: (i, 0, 0, 0, 0)),
        scratch_shapes=[pltpu.VMEM((27, 32, 128), BF)],
        compiler_params=pltpu.CompilerParams(vmem_limit_bytes=60 << 20),
        cost_estimate=pl.CostEstimate(flops=10**10, bytes_accessed=10**7, transcendentals=0),
        name="spread_weights",
    )(
        jnp.swapaxes(fine_kernels, 2, 3).reshape(LAYERS, 864, 32),
        fine_kernels.reshape(LAYERS, 864, 32),
        tile,
    )

    mine, weights, there, lower_part, upper_part = lax.optimization_barrier(
        (mine, weights, there, lower_part, upper_part)
    )
    lower = lax.ppermute(lower_part, "l", [(0, 1), (1, 0)])
    upper = lax.ppermute(upper_part, ("b", "l"), [(i, i ^ 9) for i in range(16)])
    other = lax.ppermute(mine, "c", [(0, 1), (1, 0)]).reshape(8, 8, CHUNK, 128)
    mine = mine.reshape(8, 8, CHUNK, 128)
    def round_ring(v):
        return [v] + [lax.ppermute(v, "q", [(i, (i + k) % 4) for i in range(4)]) for k in range(1, 4)]

    buffer = pltpu.VMEM((10, NOW + 2, 16, 256), BF)
    mid, base = pl.pallas_call(
        fine_kernel,
        out_shape=(
            jax.ShapeDtypeStruct((8, OWN, 16, 256), BF),
            jax.ShapeDtypeStruct((8, OWN, 16, 256), F32),
        ),
        in_specs=vmem(2) + [pl.BlockSpec(memory_space=pl.ANY)],
        out_specs=tuple(vmem(2)),
        scratch_shapes=[pltpu.VMEM((8, NOWS, 16, 256), F32)] * 2
        + [buffer] * 4
        + [pltpu.VMEM((LAYERS, 2, 8, 256, 256), BF), pltpu.SemaphoreType.DMA((LAYERS,))],
        compiler_params=pltpu.CompilerParams(vmem_limit_bytes=48 << 20),
        cost_estimate=pl.CostEstimate(flops=10**9, bytes_accessed=10**6, transcendentals=10**6),
        name="fine_layers",
    )(mine, other, weights)
    mid, lower, upper = lax.optimization_barrier((mid, lower, upper))
    states = round_ring(mid)
    far_lower = lax.ppermute(lower, "c", [(0, 1), (1, 0)])
    far_upper = lax.ppermute(upper, "c", [(0, 1), (1, 0)])
    partial = pl.pallas_call(
        coarse_kernel_body,
        out_shape=jax.ShapeDtypeStruct((8, 16, 8, 256), BF),
        in_specs=vmem(5) + [pl.BlockSpec(memory_space=pl.ANY)] * 8,
        out_specs=pl.BlockSpec(memory_space=pltpu.VMEM),
        scratch_shapes=[
            pltpu.VMEM((2, 3, 10, 8, 16, 256), BF),
            pltpu.VMEM((2, 3, 10, 6, 16, 256), BF),
            pltpu.VMEM((27, 256, 256), BF),
            pltpu.VMEM((2, 8, 8, 32, 128), BF),
            pltpu.VMEM((8, COTS, 16, 256), F32),
            pltpu.SemaphoreType.DMA((8,)),
        ],
        compiler_params=pltpu.CompilerParams(vmem_limit_bytes=48 << 20),
        cost_estimate=pl.CostEstimate(flops=2 * 10**10, bytes_accessed=10**7, transcendentals=10**6),
        name="coarse_layer",
    )(*states, base, mine, other, coarse_kernel, there, lower, upper, far_lower, far_upper)
    parts = lax.all_to_all(partial.reshape(128, 8, 256), AXES, 0, 0)
    parts = parts.reshape(1024, 256)
    sums = lax.dot_general(parts, receive_table(), (((0,), (0,)), ((), ())), preferred_element_type=F32)
    coarse_next = sums[:, 0:128]
    state_adjoint = sums[:, 128:256] + 2.0 * cotangent.reshape(256, 128).astype(F32)
    return coarse_next.reshape(256, 1, 1, 128), state_adjoint.reshape(256, 1, 1, 128)


def solution(mesh):
    split = Mesh(mesh.devices.reshape(8, 4, 2, 2), AXES)
    rows = P(None, "b", ("q", "l", "c"), None)
    return jax.shard_map(
        local,
        mesh=split,
        in_specs=(rows, rows, P(), P(None, ("q", "l", "c"), None), rows),
        out_specs=(rows, rows),
        check_vma=False,
    )
```

```python
import math

import jax
import jax.numpy as jnp
import numpy as np
from jax import lax
from jax.experimental import pallas as pl
from jax.experimental.pallas import tpu as pltpu
from jax.sharding import Mesh, PartitionSpec as P


BF = jnp.bfloat16
F32 = jnp.float32
LAYERS = 4
AXES = ("b", "q", "l", "c")
CHIPS = AXES[:3]
FINE_STEP = 0.5
COARSE_STEP = 1.5
NOW, OWN = 10, 2
SHIFT = 4
NOWS, PREVS, COTS = NOW + SHIFT, NOW - 2 + SHIFT, 8 + SHIFT
ROWS = (32, 2 * PREVS, 2 * COTS)
CHUNK = sum(ROWS)
LOWER = 13


def window_start(b, q, l):
    return 16 * b + 8 * l - 6 + 2 * q


def iota(shape, axis):
    return lax.broadcasted_iota(jnp.int32, shape, axis)


def ones_where(mask):
    return jnp.where(mask, 1.0, 0.0).astype(F32)


def swap_table(outer, inner):
    n = outer * inner
    row, column = iota((n, n), 0), iota((n, n), 1)
    return ones_where(column == row % outer * inner + row // outer).astype(BF)


def haar_signs(lane, channel):
    code = lane // 64 % 2 * 4 + lane // 32 % 2 * 2 + lane // 128
    both = code & channel % 8
    odd = (both ^ both // 2 ^ both // 4) & 1
    return jnp.where(lane % 32 == channel // 8, 1.0 - 2.0 * odd.astype(F32), 0.0).astype(BF)


def dot(x, y):
    return jnp.dot(x, y, preferred_element_type=F32)


def dot_nt(x, y):
    return lax.dot_general(x, y, (((1,), (1,)), ((), ())), preferred_element_type=F32)


def vmem(n):
    return [pl.BlockSpec(memory_space=pltpu.VMEM)] * n


def parity_rows(ref):
    return jnp.concatenate([ref[:, a, b, :] for a in range(2) for b in range(2)], axis=0)


def pack_kernel(now_in, prev_in, cot_in, out, now, prev, cot, first, second, third, sems):
    copies = []
    for i, (source, target) in enumerate(((now_in, now), (prev_in, prev), (cot_in, cot))):
        copy = pltpu.make_async_copy(source, target, sems.at[i])
        copy.start()
        copies.append(copy)
    k, lane = iota((32, 256), 0), iota((32, 256), 1)
    for_first = jnp.where(k < 2 * NOWS, lane - 2 * (k % NOWS) - k // NOWS, -1000)
    k, lane = iota((24, 256), 0), iota((24, 256), 1)
    for_second = lane - 2 * (1 + k % PREVS) - k // PREVS
    for_third = jnp.where(lane // 128 == k // COTS, lane % 128 - k % COTS, -1000)
    for target in range(0, 64, 2):
        spots = [(t // 8, t // 2 % 4, t % 2) for t in (target, target + 1)]
        for t, spot in enumerate(spots):
            at = 32 * (target + t)
            first[at : at + 32] = ones_where(for_first == 2 * window_start(*spot)).astype(BF)
        pair = [ones_where(for_second == 2 * window_start(*spot)) for spot in spots]
        second[24 * target : 24 * target + 48] = jnp.concatenate(pair, axis=0).astype(BF)
        pair = [ones_where(for_third == 16 * b + 8 * l - 2) for b, _, l in spots]
        third[24 * target : 24 * target + 48] = jnp.concatenate(pair, axis=0).astype(BF)
    for copy in copies:
        copy.wait()
    now_rows = parity_rows(now).astype(BF)
    prev_rows = parity_rows(prev).astype(BF)
    cot_rows = jnp.concatenate([cot[0:128, :], cot[128:256, :]], axis=1)
    part = 16
    for t in range(0, 64, part):
        groups = []
        for table, size, rows in zip((first, second, third), ROWS, (now_rows, prev_rows, cot_rows)):
            groups.append(dot_nt(table[pl.ds(size * t, size * part), :], rows).reshape(part, size, 128))
        out[pl.ds(t, part)] = jnp.concatenate(groups, axis=1).astype(BF)


def sort_table(core):
    row, column = iota((128, 128), 0), iota((128, 128), 1)
    y = row % 16
    source = (y + core) % 2
    return ones_where(column == (source * 8 + y // 2) * 8 + row // 16).astype(BF)


def sorted_parts(table, mine, other, x, start, stop):
    rows = jnp.concatenate([mine[x].astype(F32), other[x].astype(F32)], axis=0)
    parts = []
    for k in range(start, stop, 8):
        moved = dot(table, rows[:, k : k + 8, :].reshape(128, 128).astype(BF))
        parts += [moved[16 * j : 16 * j + 16] for j in range(8)]
    return parts


def split_dot(x, y):
    top = x.astype(BF)
    low = (x - top.astype(F32)).astype(BF)
    return dot(top, y) + dot(low, y)


def tap_index(dx, dy, dz, a2, b2, d2, a, b, d):
    def offset(moved, bit, to):
        place = (-1 if bit else 2) if moved else bit
        return place - to

    e = (offset(dx, a, a2), offset(dy, b, b2), offset(dz, d, d2))
    if any(abs(v) > 1 for v in e):
        return None
    return 9 * (e[0] + 1) + 3 * (e[1] + 1) + e[2] + 1


def weight_kernel(forward, adjoint, tile, out, wide):
    lane = lax.broadcasted_iota(jnp.int32, (32, 128), 1)
    masks = [jnp.where(lane // 32 == v, 1.0, 0.0).astype(BF) for v in range(4)]
    for way in range(2):
        source = (forward, adjoint)[way]
        wide[...] = dot(source[0], tile[...]).astype(BF).reshape(27, 32, 128)
        for moved in range(8):
            dx, dy, dz = moved >> 2, moved >> 1 & 1, moved & 1
            for u in range(8):
                d, a, b = u >> 2, u >> 1 & 1, u & 1
                for d2 in range(2):
                    total = jnp.zeros((32, 128), BF)
                    for v in range(4):
                        tap = tap_index(dx, dy, dz, v >> 1, v & 1, d2, a, b, d)
                        if tap is not None:
                            total = total + masks[v] * wide[26 - tap if way else tap]
                    out[0, way, moved, 32 * u : 32 * u + 32, 128 * d2 : 128 * d2 + 128] = total


def side_rows(v):
    row = lax.broadcasted_iota(jnp.int32, (16, 256), 0)
    axis = v.ndim - 2
    before = jnp.where(row == 0, 0.0, pltpu.roll(v, 1, axis))
    after = jnp.where(row == 15, 0.0, pltpu.roll(v, 15, axis))
    return before, after


def moved_rows(v):
    lane = lax.broadcasted_iota(jnp.int32, (16, 256), 1)
    before, after = side_rows(v)
    return jnp.where(lane // 32 % 2 == 1, before, after)


def block_conv(plain, turned, weights, x0, xs, z0, zs):
    rows = xs * zs * 16
    lane = lax.broadcasted_iota(jnp.int32, (1, 1, 16, 256), 3)
    high = lane // 64 % 2 == 1
    total = jnp.zeros((rows, 256), F32)

    def at(ref, dx, moved_z):
        xsl = pl.ds(x0 + 1 + dx, xs)
        if not moved_z:
            return ref[xsl, pl.ds(z0 + 1, zs)]
        return jnp.concatenate(
            [ref[xsl, pl.ds(z0 + 2, zs), :, 0:128], ref[xsl, pl.ds(z0, zs), :, 128:256]], axis=-1
        )

    for moved in range(8):
        dx, dy, dz = moved >> 2, moved >> 1 & 1, moved & 1
        ref = turned if dy else plain
        if dx:
            left = jnp.where(high, at(ref, -1, dz), at(ref, 1, dz))
        else:
            left = at(ref, 0, dz)
        total = total + dot(left.reshape(rows, 256), weights[moved])
    return total


def fine_kernel(mine, other, spread, mid, base, cur, old, s0, s1, h0, h1, weights, sems):
    copies = []
    for layer in range(LAYERS):
        copy = pltpu.make_async_copy(spread.at[layer], weights.at[layer], sems.at[layer])
        copy.start()
        copies.append(copy)
    core = lax.axis_index("c")
    shift = SHIFT * core
    start = window_start(*(lax.axis_index(name) for name in CHIPS)) + shift
    table = sort_table(core)
    for ref in (s0, s1, h0, h1):
        for x in (0, 9):
            ref[x] = jnp.zeros((NOW + 2, 16, 256), BF)
        for z in (0, NOW + 1):
            ref[:, z] = jnp.zeros((10, 16, 256), BF)

    def keep(z):
        at = start + z
        return jnp.where((at >= 0) & (at < 128), 1.0, 0.0).astype(F32)

    def unpack(x, carry):
        parts = sorted_parts(table, mine, other, x, 0, ROWS[0] + ROWS[1])
        for z in range(NOWS):
            cur[x, z] = jnp.concatenate([parts[z], parts[NOWS + z]], axis=1)
        at = ROWS[0]
        for z in range(PREVS):
            old[x, z + 1] = jnp.concatenate([parts[at + z], parts[at + PREVS + z]], axis=1)
        for z in range(NOW):
            v = cur[x, shift + z]
            s0[x + 1, z + 1] = v.astype(BF)
            s1[x + 1, z + 1] = moved_rows(v).astype(BF)
        return carry

    lax.fori_loop(0, 8, unpack, 0)

    now, before = cur, old
    for layer in range(LAYERS):
        copies[layer].wait()
        zs = NOW - 2 * layer
        xs = max(1, 128 // (16 * zs)) if zs > 6 else 8 // zs + (zs == 6)

        def squash(i, carry, layer=layer, zs=zs, xs=xs):
            x0 = i * xs
            v = jnp.tanh(block_conv(s0, s1, weights.at[layer, 0], x0, xs, layer, zs))
            v = v.reshape(xs, zs, 16, 256)
            for z in range(zs):
                part = v[:, z] * keep(layer + z)
                h0[pl.ds(x0 + 1, xs), layer + z + 1] = part.astype(BF)
                h1[pl.ds(x0 + 1, xs), layer + z + 1] = moved_rows(part).astype(BF)
            return carry

        lax.fori_loop(0, 8 // xs, squash, 0, unroll=True)
        zs = NOW - 2 * layer - 2
        xs = max(1, 128 // (16 * zs)) if zs > 6 else 8 // zs + (zs == 6)
        last = layer == LAYERS - 1

        def update(i, carry, layer=layer, zs=zs, xs=xs, now=now, before=before, last=last):
            x0 = i * xs
            v = block_conv(h0, h1, weights.at[layer, 1], x0, xs, layer + 1, zs)
            v = v.reshape(xs, zs, 16, 256)
            for z in range(zs):
                at = layer + 1 + z
                here = (pl.ds(x0, xs), shift + at)
                part = (2.0 * now[here] - before[here] - FINE_STEP * v[:, z]) * keep(at)
                before[here] = part
                if not last:
                    s0[pl.ds(x0 + 1, xs), at + 1] = part.astype(BF)
                    s1[pl.ds(x0 + 1, xs), at + 1] = moved_rows(part).astype(BF)
            return carry

        lax.fori_loop(0, 8 // xs, update, 0, unroll=True)
        now, before = before, now

    haar = haar_signs(iota((256, 256), 0), iota((256, 256), 1))
    scale = 1.0 / math.sqrt(8.0)
    own = (slice(None), pl.ds(shift + 4, OWN))
    latest = now[own].reshape(256, 256)
    earlier = before[own].reshape(256, 256)
    mid[...] = (split_dot(latest, haar) * scale).astype(BF).reshape(8, OWN, 16, 256)
    base[...] = (split_dot(2.0 * latest - earlier, haar) * scale).reshape(8, OWN, 16, 256)


TAPS = [(x, y, z) for x in (-1, 0, 1) for y in (-1, 0, 1) for z in (-1, 0, 1)]


def place_state(state, x, xs, z, wide):
    before, after = side_rows(wide)
    state[0, pl.ds(x + 1, xs), z] = before.astype(BF)
    state[1, pl.ds(x + 1, xs), z] = wide.astype(BF)
    state[2, pl.ds(x + 1, xs), z] = after.astype(BF)


def clear_sides(ref):
    for y in range(3):
        for x in (0, 9):
            ref[y, x] = jnp.zeros(ref.shape[2:], BF)


def coarse_forward(state, weights, x0, xs):
    rows = xs * 96
    total = jnp.zeros((rows, 256), F32)
    for number, (ex, ey, ez) in enumerate(TAPS):
        left = state[1 + ey, pl.ds(x0 + 1 + ex, xs), pl.ds(1 + ez, 6)].reshape(rows, 256)
        total = total + dot_nt(left, weights[number])
    return total


def coarse_adjoint(hidden, weights, x0, xs):
    rows = xs * 64
    total = jnp.zeros((rows, 256), F32)
    for number, (ex, ey, ez) in enumerate(TAPS):
        left = hidden[1 - ey, pl.ds(x0 + 1 - ex, xs), pl.ds(1 - ez, 4)].reshape(rows, 256)
        total = total + dot(left, weights[number])
    return (-COARSE_STEP * total).reshape(xs, 4, 16, 256)


def response_kernel(*refs):
    chunks, pieces, (out, weights, state, rows, cots, sems) = refs[0:2], refs[2:8], refs[8:14]
    core = lax.axis_index("c")
    table = sort_table(core)
    copies = []
    spots = ((0, 27, 0), (0, 27, 1), (0, LOWER, 2), (LOWER, 27, 2), (0, LOWER, 3), (LOWER, 27, 3))
    for i, chunk in enumerate(chunks):
        copy = pltpu.make_async_copy(chunk.at[:, :, pl.ds(48, 32), :], rows.at[i], sems.at[6 + i])
        copy.start()
        copies.append(copy)
    for i, (w, (low, high, part)) in enumerate(zip(pieces, spots)):
        target = weights.at[pl.ds(low, high - low), pl.ds(64 * part, 64), :]
        copy = pltpu.make_async_copy(w, target, sems.at[i])
        copy.start()
        copies.append(copy)
    clear_sides(state)
    for copy in copies[:2]:
        copy.wait()
    for x in range(8):
        parts = sorted_parts(table, rows.at[0], rows.at[1], x, 8, 32)
        for z in range(COTS):
            cots[x, z] = jnp.concatenate([parts[z], parts[COTS + z]], axis=1)
        for z in range(8):
            place_state(state, x, 1, z, cots[x, SHIFT * core + z][None])
    for copy in copies[2:]:
        copy.wait()
    xs = 4
    for x0 in range(0, 8, xs):
        out[pl.ds(96 * x0, 96 * xs)] = coarse_forward(state, weights, x0, xs)


def coarse_kernel_body(*refs):
    own, (base, response, weights, out, state, squashed, scaled) = refs[0:4], refs[4:11]
    b, quarter, l, core = (lax.axis_index(name) for name in AXES)
    start = 4 * (4 * b + 2 * l + core) - 1
    for ref in (state, squashed, scaled):
        clear_sides(ref)
    for k in range(4):
        z0 = OWN * ((quarter + 4 - k) % 4)
        for z in range(OWN):
            place_state(state, 0, 8, z0 + z, own[k][:, z].astype(F32))

    def store(ref, v, x0, xs):
        v = v.reshape(xs, 6, 16, 256)
        for z in range(6):
            at = start + z
            inside = jnp.where((at >= 0) & (at < 128), 1.0, 0.0).astype(F32)
            place_state(ref, x0, xs, z, v[:, z] * inside)

    xs = 4
    for x0 in range(0, 8, xs):
        squash = jnp.tanh(coarse_forward(state, weights, x0, xs))
        store(squashed, squash, x0, xs)
        store(scaled, (1.0 - squash * squash) * response[pl.ds(96 * x0, 96 * xs)], x0, xs)
    near = jnp.where(quarter == 1, 1.0, 0.0).astype(F32)
    far = jnp.where(quarter == 2, 1.0, 0.0).astype(F32)
    back = swap_table(8, 16)
    for x in range(8):
        if x % xs == 0:
            force, pull = coarse_adjoint(squashed, weights, x, xs), coarse_adjoint(scaled, weights, x, xs)
        at = x % xs
        ground = base[x]
        rows = jnp.concatenate([force[at, 0:2] + near * ground, force[at, 2:4] + far * ground, pull[at]], axis=0)
        out[x] = dot(back, rows.reshape(128, 256).astype(BF)).astype(BF).reshape(16, 8, 256)


def receive_table():
    row = np.arange(1024)
    at = row // 128 * 16 + row // 8 % 4 * 4 + row % 4 + row // 4 % 2 * 128
    return (np.arange(256)[None] == at[:, None]).astype(BF)


def local(fine_prev, fine_now, fine_kernels, coarse_kernel, cotangent):
    packed = pl.pallas_call(
        pack_kernel,
        out_shape=jax.ShapeDtypeStruct((64, CHUNK, 128), BF),
        in_specs=[pl.BlockSpec(memory_space=pltpu.HBM)] * 3,
        out_specs=pl.BlockSpec(memory_space=pltpu.VMEM),
        scratch_shapes=[pltpu.VMEM((32, 2, 2, 256), F32)] * 2
        + [pltpu.VMEM((256, 128), BF)]
        + [pltpu.VMEM((64 * size, 256), BF) for size in ROWS]
        + [pltpu.SemaphoreType.DMA((3,))],
        compiler_params=pltpu.CompilerParams(vmem_limit_bytes=60 << 20),
        name="pack",
    )(fine_now, fine_prev, cotangent.reshape(256, 128))
    packed, kernel_part = lax.optimization_barrier((packed, coarse_kernel))
    lower_part, upper_part = kernel_part[:LOWER], kernel_part[LOWER:]
    there = lax.ppermute(kernel_part, "c", [(0, 1), (1, 0)])
    mine = lax.all_to_all(packed, CHIPS, 0, 0)
    tile = np.tile(np.eye(32, dtype=np.float32), (1, 4)).astype(BF)
    weights = pl.pallas_call(
        weight_kernel,
        grid=(LAYERS,),
        out_shape=jax.ShapeDtypeStruct((LAYERS, 2, 8, 256, 256), BF),
        in_specs=[
            pl.BlockSpec((1, 864, 32), lambda i: (i, 0, 0)),
            pl.BlockSpec((1, 864, 32), lambda i: (i, 0, 0)),
            pl.BlockSpec((32, 128), lambda i: (0, 0)),
        ],
        out_specs=pl.BlockSpec((1, 2, 8, 256, 256), lambda i: (i, 0, 0, 0, 0)),
        scratch_shapes=[pltpu.VMEM((27, 32, 128), BF)],
        compiler_params=pltpu.CompilerParams(vmem_limit_bytes=60 << 20),
        cost_estimate=pl.CostEstimate(flops=10**10, bytes_accessed=10**7, transcendentals=0),
        name="spread_weights",
    )(
        jnp.swapaxes(fine_kernels, 2, 3).reshape(LAYERS, 864, 32),
        fine_kernels.reshape(LAYERS, 864, 32),
        tile,
    )

    mine, weights, there, lower_part, upper_part = lax.optimization_barrier(
        (mine, weights, there, lower_part, upper_part)
    )
    lower = lax.ppermute(lower_part, "l", [(0, 1), (1, 0)])
    upper = lax.ppermute(upper_part, ("b", "l"), [(i, i ^ 9) for i in range(16)])
    other = lax.ppermute(mine, "c", [(0, 1), (1, 0)]).reshape(8, 8, CHUNK, 128)
    mine = mine.reshape(8, 8, CHUNK, 128)
    def round_ring(v):
        return [v] + [lax.ppermute(v, "q", [(i, (i + k) % 4) for i in range(4)]) for k in range(1, 4)]

    buffer = pltpu.VMEM((10, NOW + 2, 16, 256), BF)
    mid, base = pl.pallas_call(
        fine_kernel,
        out_shape=(
            jax.ShapeDtypeStruct((8, OWN, 16, 256), BF),
            jax.ShapeDtypeStruct((8, OWN, 16, 256), F32),
        ),
        in_specs=vmem(2) + [pl.BlockSpec(memory_space=pl.ANY)],
        out_specs=tuple(vmem(2)),
        scratch_shapes=[pltpu.VMEM((8, NOWS, 16, 256), F32)] * 2
        + [buffer] * 4
        + [pltpu.VMEM((LAYERS, 2, 8, 256, 256), BF), pltpu.SemaphoreType.DMA((LAYERS,))],
        compiler_params=pltpu.CompilerParams(vmem_limit_bytes=48 << 20),
        cost_estimate=pl.CostEstimate(flops=10**9, bytes_accessed=10**6, transcendentals=10**6),
        name="fine_layers",
    )(mine, other, weights)
    mid, lower, upper = lax.optimization_barrier((mid, lower, upper))
    states = round_ring(mid)
    far_lower = lax.ppermute(lower, "c", [(0, 1), (1, 0)])
    far_upper = lax.ppermute(upper, "c", [(0, 1), (1, 0)])
    response, gathered = pl.pallas_call(
        response_kernel,
        out_shape=(jax.ShapeDtypeStruct((768, 256), F32), jax.ShapeDtypeStruct((27, 256, 256), BF)),
        in_specs=[pl.BlockSpec(memory_space=pl.ANY)] * 8,
        out_specs=tuple(vmem(2)),
        scratch_shapes=[
            pltpu.VMEM((3, 10, 8, 16, 256), BF),
            pltpu.VMEM((2, 8, 8, 32, 128), BF),
            pltpu.VMEM((8, COTS, 16, 256), F32),
            pltpu.SemaphoreType.DMA((8,)),
        ],
        compiler_params=pltpu.CompilerParams(vmem_limit_bytes=40 << 20),
        cost_estimate=pl.CostEstimate(flops=5 * 10**9, bytes_accessed=10**7, transcendentals=0),
        name="response",
    )(mine, other, coarse_kernel, there, lower, upper, far_lower, far_upper)
    partial = pl.pallas_call(
        coarse_kernel_body,
        out_shape=jax.ShapeDtypeStruct((8, 16, 8, 256), BF),
        in_specs=vmem(7),
        out_specs=pl.BlockSpec(memory_space=pltpu.VMEM),
        scratch_shapes=[pltpu.VMEM((3, 10, 8, 16, 256), BF)] + [pltpu.VMEM((3, 10, 6, 16, 256), BF)] * 2,
        compiler_params=pltpu.CompilerParams(vmem_limit_bytes=40 << 20),
        cost_estimate=pl.CostEstimate(flops=10**10, bytes_accessed=10**7, transcendentals=10**6),
        name="coarse_layer",
    )(*states, base, response, gathered)
    parts = lax.all_to_all(partial.reshape(128, 8, 256), AXES, 0, 0)
    parts = parts.reshape(1024, 256)
    sums = lax.dot_general(parts, receive_table(), (((0,), (0,)), ((), ())), preferred_element_type=F32)
    coarse_next = sums[:, 0:128]
    state_adjoint = sums[:, 128:256] + 2.0 * cotangent.reshape(256, 128).astype(F32)
    return coarse_next.reshape(256, 1, 1, 128), state_adjoint.reshape(256, 1, 1, 128)


def solution(mesh):
    split = Mesh(mesh.devices.reshape(8, 4, 2, 2), AXES)
    rows = P(None, "b", ("q", "l", "c"), None)
    return jax.shard_map(
        local,
        mesh=split,
        in_specs=(rows, rows, P(), P(None, ("q", "l", "c"), None), rows),
        out_specs=(rows, rows),
        check_vma=False,
    )
```

```python
import math

import jax
import jax.numpy as jnp
import numpy as np
from jax import lax
from jax.experimental import pallas as pl
from jax.experimental.pallas import tpu as pltpu
from jax.sharding import Mesh, PartitionSpec as P


BF = jnp.bfloat16
F32 = jnp.float32
LAYERS = 4
AXES = ("b", "q", "l", "c")
CHIPS = AXES[:3]
FINE_STEP = 0.5
COARSE_STEP = 1.5
NOW, OWN = 10, 2
SHIFT = 4
NOWS, PREVS, COTS = NOW + SHIFT, NOW - 2 + SHIFT, 8 + SHIFT
ROWS = (32, 2 * PREVS, 2 * COTS)
CHUNK = sum(ROWS)


def window_start(b, q, l):
    return 16 * b + 8 * l - 6 + 2 * q


def iota(shape, axis):
    return lax.broadcasted_iota(jnp.int32, shape, axis)


def ones_where(mask):
    return jnp.where(mask, 1.0, 0.0).astype(F32)


def swap_table(outer, inner):
    n = outer * inner
    row, column = iota((n, n), 0), iota((n, n), 1)
    return ones_where(column == row % outer * inner + row // outer).astype(BF)


def haar_signs(lane, channel):
    code = lane // 64 % 2 * 4 + lane // 32 % 2 * 2 + lane // 128
    both = code & channel % 8
    odd = (both ^ both // 2 ^ both // 4) & 1
    return jnp.where(lane % 32 == channel // 8, 1.0 - 2.0 * odd.astype(F32), 0.0).astype(BF)


def dot(x, y):
    return jnp.dot(x, y, preferred_element_type=F32)


def dot_nt(x, y):
    return lax.dot_general(x, y, (((1,), (1,)), ((), ())), preferred_element_type=F32)


def vmem(n):
    return [pl.BlockSpec(memory_space=pltpu.VMEM)] * n


def parity_rows(ref):
    return jnp.concatenate([ref[:, a, b, :] for a in range(2) for b in range(2)], axis=0)


def pack_kernel(now_in, prev_in, cot_in, out, now, prev, cot, first, second, third, packed, sems):
    copies = []
    for i, (source, target) in enumerate(((now_in, now), (prev_in, prev), (cot_in, cot))):
        copy = pltpu.make_async_copy(source, target, sems.at[i])
        copy.start()
        copies.append(copy)
    k, lane = iota((32, 256), 0), iota((32, 256), 1)
    for_first = jnp.where(k < 2 * NOWS, lane - 2 * (k % NOWS) - k // NOWS, -1000)
    k, lane = iota((24, 256), 0), iota((24, 256), 1)
    for_second = lane - 2 * (1 + k % PREVS) - k // PREVS
    for_third = jnp.where(lane // 128 == k // COTS, lane % 128 - k % COTS, -1000)
    for target in range(0, 64, 2):
        spots = [(t // 8, t // 2 % 4, t % 2) for t in (target, target + 1)]
        for t, spot in enumerate(spots):
            at = 32 * (target + t)
            first[at : at + 32] = ones_where(for_first == 2 * window_start(*spot)).astype(BF)
        pair = [ones_where(for_second == 2 * window_start(*spot)) for spot in spots]
        second[24 * target : 24 * target + 48] = jnp.concatenate(pair, axis=0).astype(BF)
        pair = [ones_where(for_third == 16 * b + 8 * l - 2) for b, _, l in spots]
        third[24 * target : 24 * target + 48] = jnp.concatenate(pair, axis=0).astype(BF)
    for copy in copies:
        copy.wait()
    now_rows = parity_rows(now).astype(BF)
    prev_rows = parity_rows(prev).astype(BF)
    cot_rows = jnp.concatenate([cot[0:128, :], cot[128:256, :]], axis=1)
    part = 16
    for t in range(0, 64, part):
        groups = []
        for table, size, rows in zip((first, second, third), ROWS, (now_rows, prev_rows, cot_rows)):
            groups.append(dot_nt(table[pl.ds(size * t, size * part), :], rows).reshape(part, size, 128))
        packed[pl.ds(t, part)] = jnp.concatenate(groups, axis=1).astype(BF)
        copy = pltpu.make_async_copy(packed.at[pl.ds(t, part)], out.at[pl.ds(t, part)], sems.at[3 + t // part])
        copy.start()
        copies.append(copy)
    for copy in copies[3:]:
        copy.wait()


def sort_table(core):
    row, column = iota((128, 128), 0), iota((128, 128), 1)
    y = row % 16
    source = (y + core) % 2
    return ones_where(column == (source * 8 + y // 2) * 8 + row // 16).astype(BF)


def sorted_parts(table, mine, other, x, start, stop):
    rows = jnp.concatenate([mine[x].astype(F32), other[x].astype(F32)], axis=0)
    parts = []
    for k in range(start, stop, 8):
        moved = dot(table, rows[:, k : k + 8, :].reshape(128, 128).astype(BF))
        parts += [moved[16 * j : 16 * j + 16] for j in range(8)]
    return parts


def split_dot(x, y):
    top = x.astype(BF)
    low = (x - top.astype(F32)).astype(BF)
    return dot(top, y) + dot(low, y)


def tap_index(dx, dy, dz, a2, b2, d2, a, b, d):
    def offset(moved, bit, to):
        place = (-1 if bit else 2) if moved else bit
        return place - to

    e = (offset(dx, a, a2), offset(dy, b, b2), offset(dz, d, d2))
    if any(abs(v) > 1 for v in e):
        return None
    return 9 * (e[0] + 1) + 3 * (e[1] + 1) + e[2] + 1


def weight_kernel(forward, adjoint, tile, out, wide):
    lane = lax.broadcasted_iota(jnp.int32, (32, 128), 1)
    masks = [jnp.where(lane // 32 == v, 1.0, 0.0).astype(BF) for v in range(4)]
    for way in range(2):
        source = (forward, adjoint)[way]
        wide[...] = dot(source[0], tile[...]).astype(BF).reshape(27, 32, 128)
        for moved in range(8):
            dx, dy, dz = moved >> 2, moved >> 1 & 1, moved & 1
            for u in range(8):
                d, a, b = u >> 2, u >> 1 & 1, u & 1
                for d2 in range(2):
                    total = jnp.zeros((32, 128), BF)
                    for v in range(4):
                        tap = tap_index(dx, dy, dz, v >> 1, v & 1, d2, a, b, d)
                        if tap is not None:
                            total = total + masks[v] * wide[26 - tap if way else tap]
                    out[0, way, moved, 32 * u : 32 * u + 32, 128 * d2 : 128 * d2 + 128] = total


def side_rows(v):
    row = lax.broadcasted_iota(jnp.int32, (16, 256), 0)
    axis = v.ndim - 2
    before = jnp.where(row == 0, 0.0, pltpu.roll(v, 1, axis))
    after = jnp.where(row == 15, 0.0, pltpu.roll(v, 15, axis))
    return before, after


def moved_rows(v):
    lane = lax.broadcasted_iota(jnp.int32, (16, 256), 1)
    before, after = side_rows(v)
    return jnp.where(lane // 32 % 2 == 1, before, after)


def block_conv(plain, turned, weights, x0, xs, z0, zs):
    rows = xs * zs * 16
    lane = lax.broadcasted_iota(jnp.int32, (1, 1, 16, 256), 3)
    high = lane // 64 % 2 == 1
    total = jnp.zeros((rows, 256), F32)

    def at(ref, dx, moved_z):
        xsl = pl.ds(x0 + 1 + dx, xs)
        if not moved_z:
            return ref[xsl, pl.ds(z0 + 1, zs)]
        return jnp.concatenate(
            [ref[xsl, pl.ds(z0 + 2, zs), :, 0:128], ref[xsl, pl.ds(z0, zs), :, 128:256]], axis=-1
        )

    for moved in range(8):
        dx, dy, dz = moved >> 2, moved >> 1 & 1, moved & 1
        ref = turned if dy else plain
        if dx:
            left = jnp.where(high, at(ref, -1, dz), at(ref, 1, dz))
        else:
            left = at(ref, 0, dz)
        total = total + dot(left.reshape(rows, 256), weights[moved])
    return total


def fine_kernel(mine, other, spread, mid, base, cur, old, s0, s1, h0, h1, weights, sems):
    copies = []
    for layer in range(LAYERS):
        copy = pltpu.make_async_copy(spread.at[layer], weights.at[layer], sems.at[layer])
        copy.start()
        copies.append(copy)
    core = lax.axis_index("c")
    shift = SHIFT * core
    start = window_start(*(lax.axis_index(name) for name in CHIPS)) + shift
    table = sort_table(core)
    for ref in (s0, s1, h0, h1):
        for x in (0, 9):
            ref[x] = jnp.zeros((NOW + 2, 16, 256), BF)
        for z in (0, NOW + 1):
            ref[:, z] = jnp.zeros((10, 16, 256), BF)

    def keep(z):
        at = start + z
        return jnp.where((at >= 0) & (at < 128), 1.0, 0.0).astype(F32)

    def unpack(x, carry):
        parts = sorted_parts(table, mine, other, x, 0, ROWS[0] + ROWS[1])
        for z in range(NOWS):
            cur[x, z] = jnp.concatenate([parts[z], parts[NOWS + z]], axis=1)
        at = ROWS[0]
        for z in range(PREVS):
            old[x, z + 1] = jnp.concatenate([parts[at + z], parts[at + PREVS + z]], axis=1)
        for z in range(NOW):
            v = cur[x, shift + z]
            s0[x + 1, z + 1] = v.astype(BF)
            s1[x + 1, z + 1] = moved_rows(v).astype(BF)
        return carry

    lax.fori_loop(0, 8, unpack, 0)

    now, before = cur, old
    for layer in range(LAYERS):
        copies[layer].wait()
        zs = NOW - 2 * layer
        xs = max(1, 128 // (16 * zs)) if zs > 6 else 8 // zs + (zs == 6)

        def squash(i, carry, layer=layer, zs=zs, xs=xs):
            x0 = i * xs
            v = jnp.tanh(block_conv(s0, s1, weights.at[layer, 0], x0, xs, layer, zs))
            v = v.reshape(xs, zs, 16, 256)
            for z in range(zs):
                part = v[:, z] * keep(layer + z)
                h0[pl.ds(x0 + 1, xs), layer + z + 1] = part.astype(BF)
                h1[pl.ds(x0 + 1, xs), layer + z + 1] = moved_rows(part).astype(BF)
            return carry

        lax.fori_loop(0, 8 // xs, squash, 0, unroll=True)
        zs = NOW - 2 * layer - 2
        xs = max(1, 128 // (16 * zs)) if zs > 6 else 8 // zs + (zs == 6)
        last = layer == LAYERS - 1

        def update(i, carry, layer=layer, zs=zs, xs=xs, now=now, before=before, last=last):
            x0 = i * xs
            v = block_conv(h0, h1, weights.at[layer, 1], x0, xs, layer + 1, zs)
            v = v.reshape(xs, zs, 16, 256)
            for z in range(zs):
                at = layer + 1 + z
                here = (pl.ds(x0, xs), shift + at)
                part = (2.0 * now[here] - before[here] - FINE_STEP * v[:, z]) * keep(at)
                before[here] = part
                if not last:
                    s0[pl.ds(x0 + 1, xs), at + 1] = part.astype(BF)
                    s1[pl.ds(x0 + 1, xs), at + 1] = moved_rows(part).astype(BF)
            return carry

        lax.fori_loop(0, 8 // xs, update, 0, unroll=True)
        now, before = before, now

    haar = haar_signs(iota((256, 256), 0), iota((256, 256), 1))
    scale = 1.0 / math.sqrt(8.0)
    own = (slice(None), pl.ds(shift + 4, OWN))
    latest = now[own].reshape(256, 256)
    earlier = before[own].reshape(256, 256)
    mid[...] = (split_dot(latest, haar) * scale).astype(BF).reshape(8, OWN, 16, 256)
    base[...] = (split_dot(2.0 * latest - earlier, haar) * scale).reshape(8, OWN, 16, 256)


TAPS = [(x, y, z) for x in (-1, 0, 1) for y in (-1, 0, 1) for z in (-1, 0, 1)]


def place_state(state, x, xs, z, wide):
    before, after = side_rows(wide)
    state[0, pl.ds(x + 1, xs), z] = before.astype(BF)
    state[1, pl.ds(x + 1, xs), z] = wide.astype(BF)
    state[2, pl.ds(x + 1, xs), z] = after.astype(BF)


def clear_sides(ref):
    for y in range(3):
        for x in (0, 9):
            ref[y, x] = jnp.zeros(ref.shape[2:], BF)


def coarse_forward(state, weights, x0, xs):
    rows = xs * 96
    total = jnp.zeros((rows, 256), F32)
    for number, (ex, ey, ez) in enumerate(TAPS):
        left = state[1 + ey, pl.ds(x0 + 1 + ex, xs), pl.ds(1 + ez, 6)].reshape(rows, 256)
        total = total + dot_nt(left, weights[number])
    return total


def coarse_adjoint(hidden, weights, x0, xs):
    rows = xs * 64
    total = jnp.zeros((rows, 256), F32)
    for number, (ex, ey, ez) in enumerate(TAPS):
        left = hidden[1 - ey, pl.ds(x0 + 1 - ex, xs), pl.ds(1 - ez, 4)].reshape(rows, 256)
        total = total + dot(left, weights[number])
    return (-COARSE_STEP * total).reshape(xs, 4, 16, 256)


def response_kernel(*refs):
    chunks, pieces, (out, weights, state, rows, cots, sems) = refs[0:2], refs[2:6], refs[6:12]
    core = lax.axis_index("c")
    table = sort_table(core)
    copies = []
    for i, chunk in enumerate(chunks):
        copy = pltpu.make_async_copy(chunk.at[:, :, pl.ds(48, 32), :], rows.at[i], sems.at[4 + i])
        copy.start()
        copies.append(copy)
    for i, w in enumerate(pieces):
        copy = pltpu.make_async_copy(w, weights.at[:, pl.ds(64 * i, 64), :], sems.at[i])
        copy.start()
        copies.append(copy)
    clear_sides(state)
    for copy in copies[:2]:
        copy.wait()
    for x in range(8):
        parts = sorted_parts(table, rows.at[0], rows.at[1], x, 8, 32)
        for z in range(COTS):
            cots[x, z] = jnp.concatenate([parts[z], parts[COTS + z]], axis=1)
        for z in range(8):
            place_state(state, x, 1, z, cots[x, SHIFT * core + z][None])
    for copy in copies[2:]:
        copy.wait()
    xs = 4
    for x0 in range(0, 8, xs):
        out[pl.ds(96 * x0, 96 * xs)] = coarse_forward(state, weights, x0, xs)


def coarse_kernel_body(*refs):
    own, (base, response, weights, out, state, squashed, scaled) = refs[0:4], refs[4:11]
    b, quarter, l, core = (lax.axis_index(name) for name in AXES)
    start = 4 * (4 * b + 2 * l + core) - 1
    for ref in (state, squashed, scaled):
        clear_sides(ref)
    for k in range(4):
        z0 = OWN * ((quarter + 4 - k) % 4)
        for z in range(OWN):
            place_state(state, 0, 8, z0 + z, own[k][:, z].astype(F32))

    def store(ref, v, x0, xs):
        v = v.reshape(xs, 6, 16, 256)
        for z in range(6):
            at = start + z
            inside = jnp.where((at >= 0) & (at < 128), 1.0, 0.0).astype(F32)
            place_state(ref, x0, xs, z, v[:, z] * inside)

    xs = 4
    for x0 in range(0, 8, xs):
        squash = jnp.tanh(coarse_forward(state, weights, x0, xs))
        store(squashed, squash, x0, xs)
        store(scaled, (1.0 - squash * squash) * response[pl.ds(96 * x0, 96 * xs)], x0, xs)
    near = jnp.where(quarter == 1, 1.0, 0.0).astype(F32)
    far = jnp.where(quarter == 2, 1.0, 0.0).astype(F32)
    back = swap_table(8, 16)
    for x in range(8):
        if x % xs == 0:
            force, pull = coarse_adjoint(squashed, weights, x, xs), coarse_adjoint(scaled, weights, x, xs)
        at = x % xs
        ground = base[x]
        rows = jnp.concatenate([force[at, 0:2] + near * ground, force[at, 2:4] + far * ground, pull[at]], axis=0)
        out[x] = dot(back, rows.reshape(128, 256).astype(BF)).astype(BF).reshape(16, 8, 256)


def receive_table():
    row = np.arange(1024)
    at = row // 128 * 16 + row // 8 % 4 * 4 + row % 4 + row // 4 % 2 * 128
    return (np.arange(256)[None] == at[:, None]).astype(BF)


def local(fine_prev, fine_now, fine_kernels, coarse_kernel, cotangent):
    packed = pl.pallas_call(
        pack_kernel,
        out_shape=jax.ShapeDtypeStruct((64, CHUNK, 128), BF),
        in_specs=[pl.BlockSpec(memory_space=pltpu.HBM)] * 3,
        out_specs=pl.BlockSpec(memory_space=pltpu.HBM),
        scratch_shapes=[pltpu.VMEM((32, 2, 2, 256), F32)] * 2
        + [pltpu.VMEM((256, 128), BF)]
        + [pltpu.VMEM((64 * size, 256), BF) for size in ROWS]
        + [pltpu.VMEM((64, CHUNK, 128), BF), pltpu.SemaphoreType.DMA((7,))],
        compiler_params=pltpu.CompilerParams(vmem_limit_bytes=60 << 20),
        name="pack",
    )(fine_now, fine_prev, cotangent.reshape(256, 128))
    packed, kernel_part = lax.optimization_barrier((packed, coarse_kernel))
    there = lax.ppermute(kernel_part, "c", [(0, 1), (1, 0)])
    mine = lax.all_to_all(packed, CHIPS, 0, 0)
    tile = np.tile(np.eye(32, dtype=np.float32), (1, 4)).astype(BF)
    weights = pl.pallas_call(
        weight_kernel,
        grid=(LAYERS,),
        out_shape=jax.ShapeDtypeStruct((LAYERS, 2, 8, 256, 256), BF),
        in_specs=[
            pl.BlockSpec((1, 864, 32), lambda i: (i, 0, 0)),
            pl.BlockSpec((1, 864, 32), lambda i: (i, 0, 0)),
            pl.BlockSpec((32, 128), lambda i: (0, 0)),
        ],
        out_specs=pl.BlockSpec((1, 2, 8, 256, 256), lambda i: (i, 0, 0, 0, 0)),
        scratch_shapes=[pltpu.VMEM((27, 32, 128), BF)],
        compiler_params=pltpu.CompilerParams(vmem_limit_bytes=60 << 20),
        cost_estimate=pl.CostEstimate(flops=10**10, bytes_accessed=10**7, transcendentals=0),
        name="spread_weights",
    )(
        jnp.swapaxes(fine_kernels, 2, 3).reshape(LAYERS, 864, 32),
        fine_kernels.reshape(LAYERS, 864, 32),
        tile,
    )

    mine, weights, there, kernel_part = lax.optimization_barrier((mine, weights, there, kernel_part))
    across = lax.ppermute(kernel_part, ("b", "l", "c"), [(i, i ^ (18 if i % 2 else 2)) for i in range(32)])
    other = lax.ppermute(mine, "c", [(0, 1), (1, 0)]).reshape(8, 8, CHUNK, 128)
    mine = mine.reshape(8, 8, CHUNK, 128)
    def round_ring(v):
        return [v] + [lax.ppermute(v, "q", [(i, (i + k) % 4) for i in range(4)]) for k in range(1, 4)]

    buffer = pltpu.VMEM((10, NOW + 2, 16, 256), BF)
    mid, base = pl.pallas_call(
        fine_kernel,
        out_shape=(
            jax.ShapeDtypeStruct((8, OWN, 16, 256), BF),
            jax.ShapeDtypeStruct((8, OWN, 16, 256), F32),
        ),
        in_specs=vmem(2) + [pl.BlockSpec(memory_space=pl.ANY)],
        out_specs=tuple(vmem(2)),
        scratch_shapes=[pltpu.VMEM((8, NOWS, 16, 256), F32)] * 2
        + [buffer] * 4
        + [pltpu.VMEM((LAYERS, 2, 8, 256, 256), BF), pltpu.SemaphoreType.DMA((LAYERS,))],
        compiler_params=pltpu.CompilerParams(vmem_limit_bytes=48 << 20),
        cost_estimate=pl.CostEstimate(flops=10**9, bytes_accessed=10**6, transcendentals=10**6),
        name="fine_layers",
    )(mine, other, weights)
    mid, across = lax.optimization_barrier((mid, across))
    states = round_ring(mid)
    opposite = lax.ppermute(across, "c", [(0, 1), (1, 0)])
    response, gathered = pl.pallas_call(
        response_kernel,
        out_shape=(jax.ShapeDtypeStruct((768, 256), F32), jax.ShapeDtypeStruct((27, 256, 256), BF)),
        in_specs=[pl.BlockSpec(memory_space=pl.ANY)] * 6,
        out_specs=tuple(vmem(2)),
        scratch_shapes=[
            pltpu.VMEM((3, 10, 8, 16, 256), BF),
            pltpu.VMEM((2, 8, 8, 32, 128), BF),
            pltpu.VMEM((8, COTS, 16, 256), F32),
            pltpu.SemaphoreType.DMA((6,)),
        ],
        compiler_params=pltpu.CompilerParams(vmem_limit_bytes=40 << 20),
        cost_estimate=pl.CostEstimate(flops=5 * 10**9, bytes_accessed=10**7, transcendentals=0),
        name="response",
    )(mine, other, coarse_kernel, there, across, opposite)
    partial = pl.pallas_call(
        coarse_kernel_body,
        out_shape=jax.ShapeDtypeStruct((8, 16, 8, 256), BF),
        in_specs=vmem(7),
        out_specs=pl.BlockSpec(memory_space=pltpu.VMEM),
        scratch_shapes=[pltpu.VMEM((3, 10, 8, 16, 256), BF)] + [pltpu.VMEM((3, 10, 6, 16, 256), BF)] * 2,
        compiler_params=pltpu.CompilerParams(vmem_limit_bytes=40 << 20),
        cost_estimate=pl.CostEstimate(flops=10**10, bytes_accessed=10**7, transcendentals=10**6),
        name="coarse_layer",
    )(*states, base, response, gathered)
    parts = lax.all_to_all(partial.reshape(128, 8, 256), AXES, 0, 0)
    parts = parts.reshape(1024, 256)
    sums = lax.dot_general(parts, receive_table(), (((0,), (0,)), ((), ())), preferred_element_type=F32)
    coarse_next = sums[:, 0:128]
    state_adjoint = sums[:, 128:256] + 2.0 * cotangent.reshape(256, 128).astype(F32)
    return coarse_next.reshape(256, 1, 1, 128), state_adjoint.reshape(256, 1, 1, 128)


def solution(mesh):
    split = Mesh(mesh.devices.reshape(8, 4, 2, 2), AXES)
    rows = P(None, "b", ("q", "l", "c"), None)
    return jax.shard_map(
        local,
        mesh=split,
        in_specs=(rows, rows, P(), P(None, ("q", "l", "c"), None), rows),
        out_specs=(rows, rows),
        check_vma=False,
    )
```

```python
import math

import jax
import jax.numpy as jnp
import numpy as np
from jax import lax
from jax.experimental import pallas as pl
from jax.experimental.pallas import tpu as pltpu
from jax.sharding import Mesh, PartitionSpec as P


BF = jnp.bfloat16
F32 = jnp.float32
LAYERS = 4
AXES = ("b", "q", "l", "c")
CHIPS = AXES[:3]
FIRST = ("l", "b", "q")
SECOND = ("c", "l", "q", "b")
FINE_STEP = 0.5
COARSE_STEP = 1.5
NOW, OWN = 10, 2
SHIFT = 4
NOWS, PREVS, COTS = NOW + SHIFT, NOW - 2 + SHIFT, 8 + SHIFT
ROWS = (32, 2 * PREVS, 2 * COTS)
CHUNK = sum(ROWS)


def window_start(b, q, l):
    return 16 * b + 8 * l - 6 + 2 * q


def iota(shape, axis):
    return lax.broadcasted_iota(jnp.int32, shape, axis)


def ones_where(mask):
    return jnp.where(mask, 1.0, 0.0).astype(F32)


def back_table():
    row, column = iota((128, 128), 0), iota((128, 128), 1)
    y = row // 8 % 4 * 4 + row // 32 % 2 * 2 + row // 64
    return ones_where(column == row % 8 * 16 + y).astype(BF)


def haar_signs(lane, channel):
    code = lane // 64 % 2 * 4 + lane // 32 % 2 * 2 + lane // 128
    both = code & channel % 8
    odd = (both ^ both // 2 ^ both // 4) & 1
    return jnp.where(lane % 32 == channel // 8, 1.0 - 2.0 * odd.astype(F32), 0.0).astype(BF)


def dot(x, y):
    return jnp.dot(x, y, preferred_element_type=F32)


def dot_nt(x, y):
    return lax.dot_general(x, y, (((1,), (1,)), ((), ())), preferred_element_type=F32)


def vmem(n):
    return [pl.BlockSpec(memory_space=pltpu.VMEM)] * n


def parity_rows(ref):
    return jnp.concatenate([ref[:, a, b, :] for a in range(2) for b in range(2)], axis=0)


def pack_kernel(now_in, prev_in, cot_in, out, now, prev, cot, first, second, third, packed, sems):
    copies = []
    for i, (source, target) in enumerate(((now_in, now), (prev_in, prev), (cot_in, cot))):
        copy = pltpu.make_async_copy(source, target, sems.at[i])
        copy.start()
        copies.append(copy)
    k, lane = iota((32, 256), 0), iota((32, 256), 1)
    for_first = jnp.where(k < 2 * NOWS, lane - 2 * (k % NOWS) - k // NOWS, -1000)
    k, lane = iota((24, 256), 0), iota((24, 256), 1)
    for_second = lane - 2 * (1 + k % PREVS) - k // PREVS
    for_third = jnp.where(lane // 128 == k // COTS, lane % 128 - k % COTS, -1000)
    for target in range(0, 64, 2):
        spots = [(t // 4 % 8, t % 4, t // 32) for t in (target, target + 1)]
        for t, spot in enumerate(spots):
            at = 32 * (target + t)
            first[at : at + 32] = ones_where(for_first == 2 * window_start(*spot)).astype(BF)
        pair = [ones_where(for_second == 2 * window_start(*spot)) for spot in spots]
        second[24 * target : 24 * target + 48] = jnp.concatenate(pair, axis=0).astype(BF)
        pair = [ones_where(for_third == 16 * b + 8 * l - 2) for b, _, l in spots]
        third[24 * target : 24 * target + 48] = jnp.concatenate(pair, axis=0).astype(BF)
    for copy in copies:
        copy.wait()
    now_rows = parity_rows(now).astype(BF)
    prev_rows = parity_rows(prev).astype(BF)
    cot_rows = jnp.concatenate([cot[0:128, :], cot[128:256, :]], axis=1)
    part = 16
    for t in range(0, 64, part):
        groups = []
        for table, size, rows in zip((first, second, third), ROWS, (now_rows, prev_rows, cot_rows)):
            groups.append(dot_nt(table[pl.ds(size * t, size * part), :], rows).reshape(part, size, 128))
        packed[pl.ds(t, part)] = jnp.concatenate(groups, axis=1).astype(BF)
        copy = pltpu.make_async_copy(packed.at[pl.ds(t, part)], out.at[pl.ds(t, part)], sems.at[3 + t // part])
        copy.start()
        copies.append(copy)
    for copy in copies[3:]:
        copy.wait()


def sort_table(core):
    row, column = iota((128, 128), 0), iota((128, 128), 1)
    y = row % 16
    source = (y + core) % 2
    return ones_where(column == (source * 8 + y // 2 % 2 * 4 + y // 4) * 8 + row // 16).astype(BF)


def sorted_parts(table, mine, other, x, start, stop):
    rows = [ref[:, x].astype(F32).reshape(8, ref.shape[3], 128) for ref in (mine, other)]
    rows = jnp.concatenate(rows, axis=0)
    parts = []
    for k in range(start, stop, 8):
        moved = dot(table, rows[:, k : k + 8, :].reshape(128, 128).astype(BF))
        parts += [moved[16 * j : 16 * j + 16] for j in range(8)]
    return parts


def split_dot(x, y):
    top = x.astype(BF)
    low = (x - top.astype(F32)).astype(BF)
    return dot(top, y) + dot(low, y)


def tap_index(dx, dy, dz, a2, b2, d2, a, b, d):
    def offset(moved, bit, to):
        place = (-1 if bit else 2) if moved else bit
        return place - to

    e = (offset(dx, a, a2), offset(dy, b, b2), offset(dz, d, d2))
    if any(abs(v) > 1 for v in e):
        return None
    return 9 * (e[0] + 1) + 3 * (e[1] + 1) + e[2] + 1


def weight_kernel(forward, adjoint, tile, out, wide):
    lane = lax.broadcasted_iota(jnp.int32, (32, 128), 1)
    masks = [jnp.where(lane // 32 == v, 1.0, 0.0).astype(BF) for v in range(4)]
    for way in range(2):
        source = (forward, adjoint)[way]
        wide[...] = dot(source[0], tile[...]).astype(BF).reshape(27, 32, 128)
        for moved in range(8):
            dx, dy, dz = moved >> 2, moved >> 1 & 1, moved & 1
            for u in range(8):
                d, a, b = u >> 2, u >> 1 & 1, u & 1
                for d2 in range(2):
                    total = jnp.zeros((32, 128), BF)
                    for v in range(4):
                        tap = tap_index(dx, dy, dz, v >> 1, v & 1, d2, a, b, d)
                        if tap is not None:
                            total = total + masks[v] * wide[26 - tap if way else tap]
                    out[0, way, moved, 32 * u : 32 * u + 32, 128 * d2 : 128 * d2 + 128] = total


def side_rows(v):
    row = lax.broadcasted_iota(jnp.int32, (16, 256), 0)
    axis = v.ndim - 2
    before = jnp.where(row == 0, 0.0, pltpu.roll(v, 1, axis))
    after = jnp.where(row == 15, 0.0, pltpu.roll(v, 15, axis))
    return before, after


def moved_rows(v):
    lane = lax.broadcasted_iota(jnp.int32, (16, 256), 1)
    before, after = side_rows(v)
    return jnp.where(lane // 32 % 2 == 1, before, after)


def block_conv(plain, turned, weights, x0, xs, z0, zs):
    rows = xs * zs * 16
    lane = lax.broadcasted_iota(jnp.int32, (1, 1, 16, 256), 3)
    high = lane // 64 % 2 == 1
    total = jnp.zeros((rows, 256), F32)

    def at(ref, dx, moved_z):
        xsl = pl.ds(x0 + 1 + dx, xs)
        if not moved_z:
            return ref[xsl, pl.ds(z0 + 1, zs)]
        return jnp.concatenate(
            [ref[xsl, pl.ds(z0 + 2, zs), :, 0:128], ref[xsl, pl.ds(z0, zs), :, 128:256]], axis=-1
        )

    for moved in range(8):
        dx, dy, dz = moved >> 2, moved >> 1 & 1, moved & 1
        ref = turned if dy else plain
        if dx:
            left = jnp.where(high, at(ref, -1, dz), at(ref, 1, dz))
        else:
            left = at(ref, 0, dz)
        total = total + dot(left.reshape(rows, 256), weights[moved])
    return total


def fine_kernel(mine, other, spread, mid, base, cur, old, s0, s1, h0, h1, weights, sems):
    copies = []
    for layer in range(LAYERS):
        copy = pltpu.make_async_copy(spread.at[layer], weights.at[layer], sems.at[layer])
        copy.start()
        copies.append(copy)
    core = lax.axis_index("c")
    shift = SHIFT * core
    start = window_start(*(lax.axis_index(name) for name in CHIPS)) + shift
    table = sort_table(core)
    for ref in (s0, s1, h0, h1):
        for x in (0, 9):
            ref[x] = jnp.zeros((NOW + 2, 16, 256), BF)
        for z in (0, NOW + 1):
            ref[:, z] = jnp.zeros((10, 16, 256), BF)

    def keep(z):
        at = start + z
        return jnp.where((at >= 0) & (at < 128), 1.0, 0.0).astype(F32)

    def unpack(x, carry):
        parts = sorted_parts(table, mine, other, x, 0, ROWS[0] + ROWS[1])
        for z in range(NOWS):
            cur[x, z] = jnp.concatenate([parts[z], parts[NOWS + z]], axis=1)
        at = ROWS[0]
        for z in range(PREVS):
            old[x, z + 1] = jnp.concatenate([parts[at + z], parts[at + PREVS + z]], axis=1)
        for z in range(NOW):
            v = cur[x, shift + z]
            s0[x + 1, z + 1] = v.astype(BF)
            s1[x + 1, z + 1] = moved_rows(v).astype(BF)
        return carry

    lax.fori_loop(0, 8, unpack, 0)

    now, before = cur, old
    for layer in range(LAYERS):
        copies[layer].wait()
        zs = NOW - 2 * layer
        xs = max(1, 128 // (16 * zs)) if zs > 6 else 8 // zs + (zs == 6)

        def squash(i, carry, layer=layer, zs=zs, xs=xs):
            x0 = i * xs
            v = jnp.tanh(block_conv(s0, s1, weights.at[layer, 0], x0, xs, layer, zs))
            v = v.reshape(xs, zs, 16, 256)
            for z in range(zs):
                part = v[:, z] * keep(layer + z)
                h0[pl.ds(x0 + 1, xs), layer + z + 1] = part.astype(BF)
                h1[pl.ds(x0 + 1, xs), layer + z + 1] = moved_rows(part).astype(BF)
            return carry

        lax.fori_loop(0, 8 // xs, squash, 0, unroll=True)
        zs = NOW - 2 * layer - 2
        xs = max(1, 128 // (16 * zs)) if zs > 6 else 8 // zs + (zs == 6)
        last = layer == LAYERS - 1

        def update(i, carry, layer=layer, zs=zs, xs=xs, now=now, before=before, last=last):
            x0 = i * xs
            v = block_conv(h0, h1, weights.at[layer, 1], x0, xs, layer + 1, zs)
            v = v.reshape(xs, zs, 16, 256)
            for z in range(zs):
                at = layer + 1 + z
                here = (pl.ds(x0, xs), shift + at)
                part = (2.0 * now[here] - before[here] - FINE_STEP * v[:, z]) * keep(at)
                before[here] = part
                if not last:
                    s0[pl.ds(x0 + 1, xs), at + 1] = part.astype(BF)
                    s1[pl.ds(x0 + 1, xs), at + 1] = moved_rows(part).astype(BF)
            return carry

        lax.fori_loop(0, 8 // xs, update, 0, unroll=True)
        now, before = before, now

    haar = haar_signs(iota((256, 256), 0), iota((256, 256), 1))
    scale = 1.0 / math.sqrt(8.0)
    own = (slice(None), pl.ds(shift + 4, OWN))
    latest = now[own].reshape(256, 256)
    earlier = before[own].reshape(256, 256)
    mid[...] = (split_dot(latest, haar) * scale).astype(BF).reshape(8, OWN, 16, 256)
    base[...] = (split_dot(2.0 * latest - earlier, haar) * scale).reshape(8, OWN, 16, 256)


TAPS = [(x, y, z) for x in (-1, 0, 1) for y in (-1, 0, 1) for z in (-1, 0, 1)]


def place_state(state, x, xs, z, wide):
    before, after = side_rows(wide)
    state[0, pl.ds(x + 1, xs), z] = before.astype(BF)
    state[1, pl.ds(x + 1, xs), z] = wide.astype(BF)
    state[2, pl.ds(x + 1, xs), z] = after.astype(BF)


def clear_sides(ref):
    for y in range(3):
        for x in (0, 9):
            ref[y, x] = jnp.zeros(ref.shape[2:], BF)


def coarse_forward(state, weights, x0, xs):
    rows = xs * 96
    total = jnp.zeros((rows, 256), F32)
    for number, (ex, ey, ez) in enumerate(TAPS):
        left = state[1 + ey, pl.ds(x0 + 1 + ex, xs), pl.ds(1 + ez, 6)].reshape(rows, 256)
        total = total + dot_nt(left, weights[number])
    return total


def coarse_adjoint(hidden, weights, x0, xs):
    rows = xs * 64
    total = jnp.zeros((rows, 256), F32)
    for number, (ex, ey, ez) in enumerate(TAPS):
        left = hidden[1 - ey, pl.ds(x0 + 1 - ex, xs), pl.ds(1 - ez, 4)].reshape(rows, 256)
        total = total + dot(left, weights[number])
    return (-COARSE_STEP * total).reshape(xs, 4, 16, 256)


def response_kernel(*refs):
    chunks, pieces, (out, weights, state, rows, cots, sems) = refs[0:2], refs[2:6], refs[6:12]
    core = lax.axis_index("c")
    table = sort_table(core)
    copies = []
    for i, chunk in enumerate(chunks):
        copy = pltpu.make_async_copy(chunk.at[:, :, :, pl.ds(48, 32), :], rows.at[i], sems.at[4 + i])
        copy.start()
        copies.append(copy)
    for i, w in enumerate(pieces):
        copy = pltpu.make_async_copy(w, weights.at[:, pl.ds(64 * i, 64), :], sems.at[i])
        copy.start()
        copies.append(copy)
    clear_sides(state)
    for copy in copies[:2]:
        copy.wait()
    for x in range(8):
        parts = sorted_parts(table, rows.at[0], rows.at[1], x, 8, 32)
        for z in range(COTS):
            cots[x, z] = jnp.concatenate([parts[z], parts[COTS + z]], axis=1)
        for z in range(8):
            place_state(state, x, 1, z, cots[x, SHIFT * core + z][None])
    for copy in copies[2:]:
        copy.wait()
    xs = 4
    for x0 in range(0, 8, xs):
        out[pl.ds(96 * x0, 96 * xs)] = coarse_forward(state, weights, x0, xs)


def coarse_kernel_body(*refs):
    own, (base, response, weights, out, state, squashed, scaled) = refs[0:4], refs[4:11]
    b, quarter, l, core = (lax.axis_index(name) for name in AXES)
    start = 4 * (4 * b + 2 * l + core) - 1
    for ref in (state, squashed, scaled):
        clear_sides(ref)
    for k in range(4):
        z0 = OWN * ((quarter + 4 - k) % 4)
        for z in range(OWN):
            place_state(state, 0, 8, z0 + z, own[k][:, z].astype(F32))

    def store(ref, v, x0, xs):
        v = v.reshape(xs, 6, 16, 256)
        for z in range(6):
            at = start + z
            inside = jnp.where((at >= 0) & (at < 128), 1.0, 0.0).astype(F32)
            place_state(ref, x0, xs, z, v[:, z] * inside)

    xs = 4
    for x0 in range(0, 8, xs):
        squash = jnp.tanh(coarse_forward(state, weights, x0, xs))
        store(squashed, squash, x0, xs)
        store(scaled, (1.0 - squash * squash) * response[pl.ds(96 * x0, 96 * xs)], x0, xs)
    near = jnp.where(quarter == 1, 1.0, 0.0).astype(F32)
    far = jnp.where(quarter == 2, 1.0, 0.0).astype(F32)
    back = back_table()
    for x in range(8):
        if x % xs == 0:
            force, pull = coarse_adjoint(squashed, weights, x, xs), coarse_adjoint(scaled, weights, x, xs)
        at = x % xs
        ground = base[x]
        rows = jnp.concatenate([force[at, 0:2] + near * ground, force[at, 2:4] + far * ground, pull[at]], axis=0)
        out[:, x] = dot(back, rows.reshape(128, 256).astype(BF)).astype(BF).reshape(16, 8, 256)


def receive_table():
    row = np.arange(1024)
    at = row // 8 % 8 * 16 + row // 256 % 2 * 8 + row // 512 * 4 + row % 4 + row // 4 % 2 * 128
    return (np.arange(256)[None] == at[:, None]).astype(BF)


def local(fine_prev, fine_now, fine_kernels, coarse_kernel, cotangent):
    packed = pl.pallas_call(
        pack_kernel,
        out_shape=jax.ShapeDtypeStruct((64, CHUNK, 128), BF),
        in_specs=[pl.BlockSpec(memory_space=pltpu.HBM)] * 3,
        out_specs=pl.BlockSpec(memory_space=pltpu.HBM),
        scratch_shapes=[pltpu.VMEM((32, 2, 2, 256), F32)] * 2
        + [pltpu.VMEM((256, 128), BF)]
        + [pltpu.VMEM((64 * size, 256), BF) for size in ROWS]
        + [pltpu.VMEM((64, CHUNK, 128), BF), pltpu.SemaphoreType.DMA((7,))],
        compiler_params=pltpu.CompilerParams(vmem_limit_bytes=60 << 20),
        name="pack",
    )(fine_now, fine_prev, cotangent.reshape(256, 128))
    packed, kernel_part = lax.optimization_barrier((packed, coarse_kernel))
    there = lax.ppermute(kernel_part, "c", [(0, 1), (1, 0)])
    mine = lax.all_to_all(packed, FIRST, 0, 0)
    tile = np.tile(np.eye(32, dtype=np.float32), (1, 4)).astype(BF)
    weights = pl.pallas_call(
        weight_kernel,
        grid=(LAYERS,),
        out_shape=jax.ShapeDtypeStruct((LAYERS, 2, 8, 256, 256), BF),
        in_specs=[
            pl.BlockSpec((1, 864, 32), lambda i: (i, 0, 0)),
            pl.BlockSpec((1, 864, 32), lambda i: (i, 0, 0)),
            pl.BlockSpec((32, 128), lambda i: (0, 0)),
        ],
        out_specs=pl.BlockSpec((1, 2, 8, 256, 256), lambda i: (i, 0, 0, 0, 0)),
        scratch_shapes=[pltpu.VMEM((27, 32, 128), BF)],
        compiler_params=pltpu.CompilerParams(vmem_limit_bytes=60 << 20),
        cost_estimate=pl.CostEstimate(flops=10**10, bytes_accessed=10**7, transcendentals=0),
        name="spread_weights",
    )(
        jnp.swapaxes(fine_kernels, 2, 3).reshape(LAYERS, 864, 32),
        fine_kernels.reshape(LAYERS, 864, 32),
        tile,
    )

    mine, weights, there, kernel_part = lax.optimization_barrier((mine, weights, there, kernel_part))
    across = lax.ppermute(kernel_part, ("b", "l", "c"), [(i, i ^ (18 if i % 2 else 2)) for i in range(32)])
    other = lax.ppermute(mine, "c", [(0, 1), (1, 0)]).reshape(2, 8, 4, CHUNK, 128)
    mine = mine.reshape(2, 8, 4, CHUNK, 128)
    def round_ring(v):
        return [v] + [lax.ppermute(v, "q", [(i, (i + k) % 4) for i in range(4)]) for k in range(1, 4)]

    buffer = pltpu.VMEM((10, NOW + 2, 16, 256), BF)
    mid, base = pl.pallas_call(
        fine_kernel,
        out_shape=(
            jax.ShapeDtypeStruct((8, OWN, 16, 256), BF),
            jax.ShapeDtypeStruct((8, OWN, 16, 256), F32),
        ),
        in_specs=vmem(2) + [pl.BlockSpec(memory_space=pl.ANY)],
        out_specs=tuple(vmem(2)),
        scratch_shapes=[pltpu.VMEM((8, NOWS, 16, 256), F32)] * 2
        + [buffer] * 4
        + [pltpu.VMEM((LAYERS, 2, 8, 256, 256), BF), pltpu.SemaphoreType.DMA((LAYERS,))],
        compiler_params=pltpu.CompilerParams(vmem_limit_bytes=48 << 20),
        cost_estimate=pl.CostEstimate(flops=10**9, bytes_accessed=10**6, transcendentals=10**6),
        name="fine_layers",
    )(mine, other, weights)
    mid, across = lax.optimization_barrier((mid, across))
    states = round_ring(mid)
    opposite = lax.ppermute(across, "c", [(0, 1), (1, 0)])
    response, gathered = pl.pallas_call(
        response_kernel,
        out_shape=(jax.ShapeDtypeStruct((768, 256), F32), jax.ShapeDtypeStruct((27, 256, 256), BF)),
        in_specs=[pl.BlockSpec(memory_space=pl.ANY)] * 6,
        out_specs=tuple(vmem(2)),
        scratch_shapes=[
            pltpu.VMEM((3, 10, 8, 16, 256), BF),
            pltpu.VMEM((2, 2, 8, 4, 32, 128), BF),
            pltpu.VMEM((8, COTS, 16, 256), F32),
            pltpu.SemaphoreType.DMA((6,)),
        ],
        compiler_params=pltpu.CompilerParams(vmem_limit_bytes=40 << 20),
        cost_estimate=pl.CostEstimate(flops=5 * 10**9, bytes_accessed=10**7, transcendentals=0),
        name="response",
    )(mine, other, coarse_kernel, there, across, opposite)
    partial = pl.pallas_call(
        coarse_kernel_body,
        out_shape=jax.ShapeDtypeStruct((16, 8, 8, 256), BF),
        in_specs=vmem(7),
        out_specs=pl.BlockSpec(memory_space=pltpu.VMEM),
        scratch_shapes=[pltpu.VMEM((3, 10, 8, 16, 256), BF)] + [pltpu.VMEM((3, 10, 6, 16, 256), BF)] * 2,
        compiler_params=pltpu.CompilerParams(vmem_limit_bytes=40 << 20),
        cost_estimate=pl.CostEstimate(flops=10**10, bytes_accessed=10**7, transcendentals=10**6),
        name="coarse_layer",
    )(*states, base, response, gathered)
    parts = lax.all_to_all(partial.reshape(128, 8, 256), SECOND, 0, 0)
    parts = parts.reshape(1024, 256)
    sums = lax.dot_general(parts, receive_table(), (((0,), (0,)), ((), ())), preferred_element_type=F32)
    coarse_next = sums[:, 0:128]
    state_adjoint = sums[:, 128:256] + 2.0 * cotangent.reshape(256, 128).astype(F32)
    return coarse_next.reshape(256, 1, 1, 128), state_adjoint.reshape(256, 1, 1, 128)


def solution(mesh):
    split = Mesh(mesh.devices.reshape(8, 4, 2, 2), AXES)
    rows = P(None, "b", ("q", "l", "c"), None)
    return jax.shard_map(
        local,
        mesh=split,
        in_specs=(rows, rows, P(), P(None, ("q", "l", "c"), None), rows),
        out_specs=(rows, rows),
        check_vma=False,
    )
```

```python
import math

import jax
import jax.numpy as jnp
import numpy as np
from jax import lax
from jax.experimental import pallas as pl
from jax.experimental.pallas import tpu as pltpu
from jax.sharding import Mesh, PartitionSpec as P


BF = jnp.bfloat16
F32 = jnp.float32
LAYERS = 4
AXES = ("b", "q", "l", "c")
CHIPS = AXES[:3]
FINE_STEP = 0.5
COARSE_STEP = 1.5
NOW, OWN = 10, 2
SHIFT = 4
NOWS, PREVS, COTS = NOW + SHIFT, NOW - 2 + SHIFT, 8 + SHIFT
ROWS = (32, 2 * PREVS, 2 * COTS)
CHUNK = sum(ROWS)


def window_start(b, q, l):
    return 16 * b + 8 * l - 6 + 2 * q


def iota(shape, axis):
    return lax.broadcasted_iota(jnp.int32, shape, axis)


def ones_where(mask):
    return jnp.where(mask, 1.0, 0.0).astype(F32)


def swap_table(outer, inner):
    n = outer * inner
    row, column = iota((n, n), 0), iota((n, n), 1)
    return ones_where(column == row % outer * inner + row // outer).astype(BF)


def haar_signs(lane, channel):
    code = lane // 64 % 2 * 4 + lane // 32 % 2 * 2 + lane // 128
    both = code & channel % 8
    odd = (both ^ both // 2 ^ both // 4) & 1
    return jnp.where(lane % 32 == channel // 8, 1.0 - 2.0 * odd.astype(F32), 0.0).astype(BF)


def dot(x, y):
    return jnp.dot(x, y, preferred_element_type=F32)


def dot_nt(x, y):
    return lax.dot_general(x, y, (((1,), (1,)), ((), ())), preferred_element_type=F32)


def vmem(n):
    return [pl.BlockSpec(memory_space=pltpu.VMEM)] * n


def parity_rows(ref):
    return jnp.concatenate([ref[:, a, b, :] for a in range(2) for b in range(2)], axis=0)


def pack_kernel(now_in, prev_in, cot_in, out, now, prev, cot, first, second, third, packed, sems):
    copies = []
    for i, (source, target) in enumerate(((now_in, now), (prev_in, prev), (cot_in, cot))):
        copy = pltpu.make_async_copy(source, target, sems.at[i])
        copy.start()
        copies.append(copy)
    k, lane = iota((32, 256), 0), iota((32, 256), 1)
    for_first = jnp.where(k < 2 * NOWS, lane - 2 * (k % NOWS) - k // NOWS, -1000)
    k, lane = iota((24, 256), 0), iota((24, 256), 1)
    for_second = lane - 2 * (1 + k % PREVS) - k // PREVS
    for_third = jnp.where(lane // 128 == k // COTS, lane % 128 - k % COTS, -1000)
    for target in range(0, 64, 2):
        spots = [(t // 8, t // 2 % 4, t % 2) for t in (target, target + 1)]
        for t, spot in enumerate(spots):
            at = 32 * (target + t)
            first[at : at + 32] = ones_where(for_first == 2 * window_start(*spot)).astype(BF)
        pair = [ones_where(for_second == 2 * window_start(*spot)) for spot in spots]
        second[24 * target : 24 * target + 48] = jnp.concatenate(pair, axis=0).astype(BF)
        pair = [ones_where(for_third == 16 * b + 8 * l - 2) for b, _, l in spots]
        third[24 * target : 24 * target + 48] = jnp.concatenate(pair, axis=0).astype(BF)
    for copy in copies:
        copy.wait()
    now_rows = parity_rows(now).astype(BF)
    prev_rows = parity_rows(prev).astype(BF)
    cot_rows = jnp.concatenate([cot[0:128, :], cot[128:256, :]], axis=1)
    part = 16
    for t in range(0, 64, part):
        groups = []
        for table, size, rows in zip((first, second, third), ROWS, (now_rows, prev_rows, cot_rows)):
            groups.append(dot_nt(table[pl.ds(size * t, size * part), :], rows).reshape(part, size, 128))
        packed[pl.ds(t, part)] = jnp.concatenate(groups, axis=1).astype(BF)
        copy = pltpu.make_async_copy(packed.at[pl.ds(t, part)], out.at[pl.ds(t, part)], sems.at[3 + t // part])
        copy.start()
        copies.append(copy)
    for copy in copies[3:]:
        copy.wait()


def sort_table(core):
    row, column = iota((128, 128), 0), iota((128, 128), 1)
    y = row % 16
    source = (y + core) % 2
    return ones_where(column == (source * 8 + y // 2) * 8 + row // 16).astype(BF)


def sorted_parts(table, mine, other, x, start, stop):
    rows = jnp.concatenate([mine[x].astype(F32), other[x].astype(F32)], axis=0)
    parts = []
    for k in range(start, stop, 8):
        moved = dot(table, rows[:, k : k + 8, :].reshape(128, 128).astype(BF))
        parts += [moved[16 * j : 16 * j + 16] for j in range(8)]
    return parts


def split_dot(x, y):
    top = x.astype(BF)
    low = (x - top.astype(F32)).astype(BF)
    return dot(top, y) + dot(low, y)


def tap_index(dx, dy, dz, a2, b2, d2, a, b, d):
    def offset(moved, bit, to):
        place = (-1 if bit else 2) if moved else bit
        return place - to

    e = (offset(dx, a, a2), offset(dy, b, b2), offset(dz, d, d2))
    if any(abs(v) > 1 for v in e):
        return None
    return 9 * (e[0] + 1) + 3 * (e[1] + 1) + e[2] + 1


def weight_kernel(forward, adjoint, tile, out, wide):
    lane = lax.broadcasted_iota(jnp.int32, (32, 128), 1)
    masks = [jnp.where(lane // 32 == v, 1.0, 0.0).astype(BF) for v in range(4)]
    for way in range(2):
        source = (forward, adjoint)[way]
        wide[...] = dot(source[0], tile[...]).astype(BF).reshape(27, 32, 128)
        for moved in range(8):
            dx, dy, dz = moved >> 2, moved >> 1 & 1, moved & 1
            for u in range(8):
                d, a, b = u >> 2, u >> 1 & 1, u & 1
                for d2 in range(2):
                    total = jnp.zeros((32, 128), BF)
                    for v in range(4):
                        tap = tap_index(dx, dy, dz, v >> 1, v & 1, d2, a, b, d)
                        if tap is not None:
                            total = total + masks[v] * wide[26 - tap if way else tap]
                    out[0, way, moved, 32 * u : 32 * u + 32, 128 * d2 : 128 * d2 + 128] = total


def side_rows(v):
    row = lax.broadcasted_iota(jnp.int32, (16, 256), 0)
    axis = v.ndim - 2
    before = jnp.where(row == 0, 0.0, pltpu.roll(v, 1, axis))
    after = jnp.where(row == 15, 0.0, pltpu.roll(v, 15, axis))
    return before, after


def moved_rows(v):
    lane = lax.broadcasted_iota(jnp.int32, (16, 256), 1)
    before, after = side_rows(v)
    return jnp.where(lane // 32 % 2 == 1, before, after)


def block_conv(plain, turned, weights, x0, xs, z0, zs):
    rows = xs * zs * 16
    lane = lax.broadcasted_iota(jnp.int32, (1, 1, 16, 256), 3)
    high = lane // 64 % 2 == 1
    total = jnp.zeros((rows, 256), F32)

    def at(ref, dx, moved_z):
        xsl = pl.ds(x0 + 1 + dx, xs)
        if not moved_z:
            return ref[xsl, pl.ds(z0 + 1, zs)]
        return jnp.concatenate(
            [ref[xsl, pl.ds(z0 + 2, zs), :, 0:128], ref[xsl, pl.ds(z0, zs), :, 128:256]], axis=-1
        )

    for moved in range(8):
        dx, dy, dz = moved >> 2, moved >> 1 & 1, moved & 1
        ref = turned if dy else plain
        if dx:
            left = jnp.where(high, at(ref, -1, dz), at(ref, 1, dz))
        else:
            left = at(ref, 0, dz)
        total = total + dot(left.reshape(rows, 256), weights[moved])
    return total


def fine_kernel(mine, other, spread, mid, base, cur, old, s0, s1, h0, h1, weights, sems):
    copies = []
    for layer in range(LAYERS):
        copy = pltpu.make_async_copy(spread.at[layer], weights.at[layer], sems.at[layer])
        copy.start()
        copies.append(copy)
    core = lax.axis_index("c")
    shift = SHIFT * core
    start = window_start(*(lax.axis_index(name) for name in CHIPS)) + shift
    table = sort_table(core)
    for ref in (s0, s1, h0, h1):
        for x in (0, 9):
            ref[x] = jnp.zeros((NOW + 2, 16, 256), BF)
        for z in (0, NOW + 1):
            ref[:, z] = jnp.zeros((10, 16, 256), BF)

    def keep(z):
        at = start + z
        return jnp.where((at >= 0) & (at < 128), 1.0, 0.0).astype(F32)

    def unpack(x, carry):
        parts = sorted_parts(table, mine, other, x, 0, ROWS[0] + ROWS[1])
        for z in range(NOWS):
            cur[x, z] = jnp.concatenate([parts[z], parts[NOWS + z]], axis=1)
        at = ROWS[0]
        for z in range(PREVS):
            old[x, z + 1] = jnp.concatenate([parts[at + z], parts[at + PREVS + z]], axis=1)
        for z in range(NOW):
            v = cur[x, shift + z]
            s0[x + 1, z + 1] = v.astype(BF)
            s1[x + 1, z + 1] = moved_rows(v).astype(BF)
        return carry

    lax.fori_loop(0, 8, unpack, 0, unroll=2)

    now, before = cur, old
    for layer in range(LAYERS):
        copies[layer].wait()
        zs = NOW - 2 * layer
        xs = max(1, 128 // (16 * zs)) if zs > 6 else 8 // zs + (zs == 6)

        def squash(i, carry, layer=layer, zs=zs, xs=xs):
            x0 = i * xs
            v = jnp.tanh(block_conv(s0, s1, weights.at[layer, 0], x0, xs, layer, zs))
            v = v.reshape(xs, zs, 16, 256)
            for z in range(zs):
                part = v[:, z] * keep(layer + z)
                h0[pl.ds(x0 + 1, xs), layer + z + 1] = part.astype(BF)
                h1[pl.ds(x0 + 1, xs), layer + z + 1] = moved_rows(part).astype(BF)
            return carry

        lax.fori_loop(0, 8 // xs, squash, 0, unroll=True)
        zs = NOW - 2 * layer - 2
        xs = max(1, 128 // (16 * zs)) if zs > 6 else 8 // zs + (zs == 6)
        last = layer == LAYERS - 1

        def update(i, carry, layer=layer, zs=zs, xs=xs, now=now, before=before, last=last):
            x0 = i * xs
            v = block_conv(h0, h1, weights.at[layer, 1], x0, xs, layer + 1, zs)
            v = v.reshape(xs, zs, 16, 256)
            for z in range(zs):
                at = layer + 1 + z
                here = (pl.ds(x0, xs), shift + at)
                part = (2.0 * now[here] - before[here] - FINE_STEP * v[:, z]) * keep(at)
                before[here] = part
                if not last:
                    s0[pl.ds(x0 + 1, xs), at + 1] = part.astype(BF)
                    s1[pl.ds(x0 + 1, xs), at + 1] = moved_rows(part).astype(BF)
            return carry

        lax.fori_loop(0, 8 // xs, update, 0, unroll=True)
        now, before = before, now

    haar = haar_signs(iota((256, 256), 0), iota((256, 256), 1))
    scale = 1.0 / math.sqrt(8.0)
    own = (slice(None), pl.ds(shift + 4, OWN))
    latest = now[own].reshape(256, 256)
    earlier = before[own].reshape(256, 256)
    mid[...] = (split_dot(latest, haar) * scale).astype(BF).reshape(8, OWN, 16, 256)
    base[...] = (split_dot(2.0 * latest - earlier, haar) * scale).reshape(8, OWN, 16, 256)


TAPS = [(x, y, z) for x in (-1, 0, 1) for y in (-1, 0, 1) for z in (-1, 0, 1)]


def place_state(state, x, xs, z, wide):
    before, after = side_rows(wide)
    state[0, pl.ds(x + 1, xs), z] = before.astype(BF)
    state[1, pl.ds(x + 1, xs), z] = wide.astype(BF)
    state[2, pl.ds(x + 1, xs), z] = after.astype(BF)


def clear_sides(ref):
    for y in range(3):
        for x in (0, 9):
            ref[y, x] = jnp.zeros(ref.shape[2:], BF)


def coarse_forward(state, weights, x0, xs):
    rows = xs * 96
    total = jnp.zeros((rows, 256), F32)
    for number, (ex, ey, ez) in enumerate(TAPS):
        left = state[1 + ey, pl.ds(x0 + 1 + ex, xs), pl.ds(1 + ez, 6)].reshape(rows, 256)
        total = total + dot_nt(left, weights[number])
    return total


def coarse_adjoint(hidden, weights, x0, xs):
    rows = xs * 64
    total = jnp.zeros((rows, 256), F32)
    for number, (ex, ey, ez) in enumerate(TAPS):
        left = hidden[1 - ey, pl.ds(x0 + 1 - ex, xs), pl.ds(1 - ez, 4)].reshape(rows, 256)
        total = total + dot(left, weights[number])
    return (-COARSE_STEP * total).reshape(xs, 4, 16, 256)


def response_kernel(*refs):
    chunks, pieces, (out, weights, state, rows, cots, sems) = refs[0:2], refs[2:6], refs[6:12]
    core = lax.axis_index("c")
    table = sort_table(core)
    copies = []
    for i, chunk in enumerate(chunks):
        copy = pltpu.make_async_copy(chunk.at[:, :, pl.ds(48, 32), :], rows.at[i], sems.at[4 + i])
        copy.start()
        copies.append(copy)
    for i, w in enumerate(pieces):
        copy = pltpu.make_async_copy(w, weights.at[:, pl.ds(64 * i, 64), :], sems.at[i])
        copy.start()
        copies.append(copy)
    clear_sides(state)
    for copy in copies[:2]:
        copy.wait()
    for x in range(8):
        parts = sorted_parts(table, rows.at[0], rows.at[1], x, 8, 32)
        for z in range(COTS):
            cots[x, z] = jnp.concatenate([parts[z], parts[COTS + z]], axis=1)
        for z in range(8):
            place_state(state, x, 1, z, cots[x, SHIFT * core + z][None])
    for copy in copies[2:]:
        copy.wait()
    xs = 4
    for x0 in range(0, 8, xs):
        out[pl.ds(96 * x0, 96 * xs)] = coarse_forward(state, weights, x0, xs)


def coarse_kernel_body(*refs):
    own, (base, response, weights, out, state, squashed, scaled) = refs[0:4], refs[4:11]
    b, quarter, l, core = (lax.axis_index(name) for name in AXES)
    start = 4 * (4 * b + 2 * l + core) - 1
    for ref in (state, squashed, scaled):
        clear_sides(ref)
    for k in range(4):
        z0 = OWN * ((quarter + 4 - k) % 4)
        for z in range(OWN):
            place_state(state, 0, 8, z0 + z, own[k][:, z].astype(F32))

    def store(ref, v, x0, xs):
        v = v.reshape(xs, 6, 16, 256)
        for z in range(6):
            at = start + z
            inside = jnp.where((at >= 0) & (at < 128), 1.0, 0.0).astype(F32)
            place_state(ref, x0, xs, z, v[:, z] * inside)

    xs = 4
    for x0 in range(0, 8, xs):
        squash = jnp.tanh(coarse_forward(state, weights, x0, xs))
        store(squashed, squash, x0, xs)
        store(scaled, (1.0 - squash * squash) * response[pl.ds(96 * x0, 96 * xs)], x0, xs)
    near = jnp.where(quarter == 1, 1.0, 0.0).astype(F32)
    far = jnp.where(quarter == 2, 1.0, 0.0).astype(F32)
    back = swap_table(8, 16)
    for x in range(8):
        if x % xs == 0:
            force, pull = coarse_adjoint(squashed, weights, x, xs), coarse_adjoint(scaled, weights, x, xs)
        at = x % xs
        ground = base[x]
        rows = jnp.concatenate([force[at, 0:2] + near * ground, force[at, 2:4] + far * ground, pull[at]], axis=0)
        out[x] = dot(back, rows.reshape(128, 256).astype(BF)).astype(BF).reshape(16, 8, 256)


def receive_table():
    row = np.arange(1024)
    at = row // 128 * 16 + row // 8 % 4 * 4 + row % 4 + row // 4 % 2 * 128
    return (np.arange(256)[None] == at[:, None]).astype(BF)


def local(fine_prev, fine_now, fine_kernels, coarse_kernel, cotangent):
    packed = pl.pallas_call(
        pack_kernel,
        out_shape=jax.ShapeDtypeStruct((64, CHUNK, 128), BF),
        in_specs=[pl.BlockSpec(memory_space=pltpu.HBM)] * 3,
        out_specs=pl.BlockSpec(memory_space=pltpu.HBM),
        scratch_shapes=[pltpu.VMEM((32, 2, 2, 256), F32)] * 2
        + [pltpu.VMEM((256, 128), BF)]
        + [pltpu.VMEM((64 * size, 256), BF) for size in ROWS]
        + [pltpu.VMEM((64, CHUNK, 128), BF), pltpu.SemaphoreType.DMA((7,))],
        compiler_params=pltpu.CompilerParams(vmem_limit_bytes=60 << 20),
        name="pack",
    )(fine_now, fine_prev, cotangent.reshape(256, 128))
    packed, kernel_part = lax.optimization_barrier((packed, coarse_kernel))
    there = lax.ppermute(kernel_part, "c", [(0, 1), (1, 0)])
    mine = lax.all_to_all(packed, CHIPS, 0, 0)
    tile = np.tile(np.eye(32, dtype=np.float32), (1, 4)).astype(BF)
    weights = pl.pallas_call(
        weight_kernel,
        grid=(LAYERS,),
        out_shape=jax.ShapeDtypeStruct((LAYERS, 2, 8, 256, 256), BF),
        in_specs=[
            pl.BlockSpec((1, 864, 32), lambda i: (i, 0, 0)),
            pl.BlockSpec((1, 864, 32), lambda i: (i, 0, 0)),
            pl.BlockSpec((32, 128), lambda i: (0, 0)),
        ],
        out_specs=pl.BlockSpec((1, 2, 8, 256, 256), lambda i: (i, 0, 0, 0, 0)),
        scratch_shapes=[pltpu.VMEM((27, 32, 128), BF)],
        compiler_params=pltpu.CompilerParams(vmem_limit_bytes=60 << 20),
        cost_estimate=pl.CostEstimate(flops=10**10, bytes_accessed=10**7, transcendentals=0),
        name="spread_weights",
    )(
        jnp.swapaxes(fine_kernels, 2, 3).reshape(LAYERS, 864, 32),
        fine_kernels.reshape(LAYERS, 864, 32),
        tile,
    )

    mine, weights, there, kernel_part = lax.optimization_barrier((mine, weights, there, kernel_part))
    across = lax.ppermute(kernel_part, ("b", "l", "c"), [(i, i ^ (18 if i % 2 else 2)) for i in range(32)])
    other = lax.ppermute(mine, "c", [(0, 1), (1, 0)]).reshape(8, 8, CHUNK, 128)
    mine = mine.reshape(8, 8, CHUNK, 128)
    def round_ring(v):
        moved = {k: lax.ppermute(v, "q", [(i, (i + k) % 4) for i in range(4)]) for k in (2, 1, 3)}
        return [v, moved[1], moved[2], moved[3]]

    buffer = pltpu.VMEM((10, NOW + 2, 16, 256), BF)
    mid, base = pl.pallas_call(
        fine_kernel,
        out_shape=(
            jax.ShapeDtypeStruct((8, OWN, 16, 256), BF),
            jax.ShapeDtypeStruct((8, OWN, 16, 256), F32),
        ),
        in_specs=vmem(2) + [pl.BlockSpec(memory_space=pl.ANY)],
        out_specs=tuple(vmem(2)),
        scratch_shapes=[pltpu.VMEM((8, NOWS, 16, 256), F32)] * 2
        + [buffer] * 4
        + [pltpu.VMEM((LAYERS, 2, 8, 256, 256), BF), pltpu.SemaphoreType.DMA((LAYERS,))],
        compiler_params=pltpu.CompilerParams(vmem_limit_bytes=48 << 20),
        cost_estimate=pl.CostEstimate(flops=10**9, bytes_accessed=10**6, transcendentals=10**6),
        name="fine_layers",
    )(mine, other, weights)
    mid, across = lax.optimization_barrier((mid, across))
    states = round_ring(mid)
    opposite = lax.ppermute(across, "c", [(0, 1), (1, 0)])
    response, gathered = pl.pallas_call(
        response_kernel,
        out_shape=(jax.ShapeDtypeStruct((768, 256), F32), jax.ShapeDtypeStruct((27, 256, 256), BF)),
        in_specs=[pl.BlockSpec(memory_space=pl.ANY)] * 6,
        out_specs=tuple(vmem(2)),
        scratch_shapes=[
            pltpu.VMEM((3, 10, 8, 16, 256), BF),
            pltpu.VMEM((2, 8, 8, 32, 128), BF),
            pltpu.VMEM((8, COTS, 16, 256), F32),
            pltpu.SemaphoreType.DMA((6,)),
        ],
        compiler_params=pltpu.CompilerParams(vmem_limit_bytes=40 << 20),
        cost_estimate=pl.CostEstimate(flops=5 * 10**9, bytes_accessed=10**7, transcendentals=0),
        name="response",
    )(mine, other, coarse_kernel, there, across, opposite)
    partial = pl.pallas_call(
        coarse_kernel_body,
        out_shape=jax.ShapeDtypeStruct((8, 16, 8, 256), BF),
        in_specs=vmem(7),
        out_specs=pl.BlockSpec(memory_space=pltpu.VMEM),
        scratch_shapes=[pltpu.VMEM((3, 10, 8, 16, 256), BF)] + [pltpu.VMEM((3, 10, 6, 16, 256), BF)] * 2,
        compiler_params=pltpu.CompilerParams(vmem_limit_bytes=40 << 20),
        cost_estimate=pl.CostEstimate(flops=10**10, bytes_accessed=10**7, transcendentals=10**6),
        name="coarse_layer",
    )(*states, base, response, gathered)
    parts = lax.all_to_all(partial.reshape(128, 8, 256), AXES, 0, 0)
    parts = parts.reshape(1024, 256)
    sums = lax.dot_general(parts, receive_table(), (((0,), (0,)), ((), ())), preferred_element_type=F32)
    coarse_next = sums[:, 0:128]
    state_adjoint = sums[:, 128:256] + 2.0 * cotangent.reshape(256, 128).astype(F32)
    return coarse_next.reshape(256, 1, 1, 128), state_adjoint.reshape(256, 1, 1, 128)


def solution(mesh):
    split = Mesh(mesh.devices.reshape(8, 4, 2, 2), AXES)
    rows = P(None, "b", ("q", "l", "c"), None)
    return jax.shard_map(
        local,
        mesh=split,
        in_specs=(rows, rows, P(), P(None, ("q", "l", "c"), None), rows),
        out_specs=(rows, rows),
        check_vma=False,
    )
```
